32 devices in a mesh: section: 2 (over x), dp: 16 (over z, y, core).
Axes of the slice: x: 2, y: 2, z: 4, core: 2. Of those that a mesh axis runs over, the one named last changes fastest.
Arguments:
- boundary: bfloat16 [2, 16384, 768], P('section', 'dp'), may hold values from -6 to 6
- inward: bfloat16 [2, 768, 2304], P('section'), may hold values from -0.21875 to 0.21875
- inbias: float32 [2, 2304], P('section'), may hold values from -1.5 to 1.5
- outward: bfloat16 [2, 768, 768], P('section'), may hold values from -3 to 3
- outbias: float32 [2, 768], P('section'), may hold values from -1.5 to 1.5
- normgain: float32 [2, 768], P('section'), may hold values from 0.25 to 1.75
- normshift: float32 [2, 768], P('section'), may hold values from -1.5 to 1.5
- expand: bfloat16 [2, 768, 3072], P('section'), may hold values from -0.21875 to 0.21875
- expbias: float32 [2, 3072], P('section'), may hold values from -1.5 to 1.5
- shrink: bfloat16 [2, 3072, 768], P('section'), may hold values from -0.109375 to 0.109375
- shrbias: float32 [2, 768], P('section'), may hold values from -1.5 to 1.5
- lastgain: float32 [2, 768], P('section'), may hold values from 0.25 to 1.75
- lastshift: float32 [2, 768], P('section'), may hold values from -1.5 to 1.5
Outputs:
- results: bfloat16 [2, 16384, 768], P('section', 'dp')
- inward_grads: float32 [2, 768, 2304], P('section')
- inbias_grads: float32 [2, 2304], P('section')
- outward_grads: float32 [2, 768, 768], P('section')
- outbias_grads: float32 [2, 768], P('section')
- normgain_grads: float32 [2, 768], P('section')
- normshift_grads: float32 [2, 768], P('section')
- expand_grads: float32 [2, 768, 3072], P('section')
- expbias_grads: float32 [2, 3072], P('section')
- shrink_grads: float32 [2, 3072, 768], P('section')
- shrbias_grads: float32 [2, 768], P('section')
- lastgain_grads: float32 [2, 768], P('section')
- lastshift_grads: float32 [2, 768], P('section')
The draws below stay inside these ranges and needn't reach their ends.
All inputs are finite; a program needn't handle non-finite values.
Results may differ from the reference program's by a relative error of at most 0.014.
Values may be sent and summed in bfloat16 or wider, within the bound.
A program may use at most 384 MiB of HBM per device.

```python
import math
import jax
import jax.numpy as jnp
from jax import lax

D = 768
HEAD = 64
FF = 3072
SEQ = 512
TOK_DEV = 1024
TOKENS = 16384


def levels(key, extent, shards, low, high):
    gain, own = 1.0, jax.random.fold_in(key, 6)
    for axis_at, blocks in shards:
        draws = jnp.exp(jax.random.uniform(jax.random.fold_in(own, axis_at), (blocks,), jnp.float32, low / len(shards), high / len(shards)))
        gain = gain * jnp.repeat(draws, extent[axis_at] // blocks).reshape([-1 if axis == axis_at else 1 for axis in range(len(extent))])
    return gain


def noise(stream_key, extent, width, bound, pieces=(), held_as=jnp.bfloat16):
    values = jax.random.normal(stream_key, extent, jnp.float32) * width
    if len(pieces) > 0:
        values = levels(stream_key, extent, pieces, -0.22, 0.18) * values
    return jnp.clip(values, min=-bound, max=bound).astype(held_as)


def setup_inputs(seed: int = 0) -> dict:
    keys = jax.random.split(jax.random.key(seed), 14)
    boundary = noise(keys[0], (2, TOKENS, D), 1.0, 6.0, ((0, 2), (1, 16)))
    inward = noise(keys[1], (2, D, 3 * D), D ** -0.5, 0.21875, ((0, 2),))
    inbias = noise(keys[2], (2, 3 * D), 0.3, 1.5, ((0, 2),), jnp.float32)
    outward = noise(keys[3], (2, D, D), (max(1, D // 192)) ** -0.5, 3.0, ((0, 2),))
    outbias = noise(keys[4], (2, D), 0.3, 1.5, ((0, 2),), jnp.float32)
    normgain = jnp.clip(1.0 + 0.15 * jax.random.normal(keys[5], (2, D), jnp.float32), 0.25, 1.75)
    normshift = noise(keys[6], (2, D), 0.3, 1.5, ((0, 2),), jnp.float32)
    expand = noise(keys[7], (2, D, FF), D ** -0.5, 0.21875, ((0, 2),))
    expbias = noise(keys[8], (2, FF), 0.3, 1.5, ((0, 2),), jnp.float32)
    shrink = noise(keys[9], (2, FF, D), FF ** -0.5, 0.109375, ((0, 2),))
    shrbias = noise(keys[10], (2, D), 0.3, 1.5, ((0, 2),), jnp.float32)
    lastgain = jnp.clip(1.0 + 0.15 * jax.random.normal(keys[11], (2, D), jnp.float32), 0.25, 1.75)
    lastshift = noise(keys[12], (2, D), 0.3, 1.5, ((0, 2),), jnp.float32)
    return {"boundary": boundary, "inward": inward, "inbias": inbias, "outward": outward, "outbias": outbias, "normgain": normgain, "normshift": normshift, "expand": expand, "expbias": expbias, "shrink": shrink, "shrbias": shrbias, "lastgain": lastgain, "lastshift": lastshift}


EPSILON = 1e-05
PRECISE = lax.Precision.HIGHEST

@jax.custom_vjp
def low(v):
    return lax.optimization_barrier(v.astype(jnp.bfloat16)).astype(jnp.float32)

@jax.custom_vjp
def low_back(v):
    return v

def low_keep(v):
    return (low(v), None)

def low_pass(kept, grad):
    return (grad,)

def back_keep(v):
    return (v, None)

def back_low(kept, grad):
    return (low(grad),)
low.defvjp(low_keep, low_pass)
low_back.defvjp(back_keep, back_low)

def matmul(operand, matrix):
    return jnp.dot(operand, matrix, precision=PRECISE, preferred_element_type=jnp.float32)

def layer_norm(values, norm_gain, norm_shift):
    center = values - lax.optimization_barrier(jnp.mean(values, axis=-1, keepdims=True))
    spread = lax.optimization_barrier(jnp.mean(center * center, axis=-1, keepdims=True))
    return center * lax.rsqrt(spread + EPSILON) * norm_gain + norm_shift

def attention(queries, keys_in, values_in, block_width):
    seq_count, seq_length, head_count, head_size = queries.shape
    block_count = seq_length // block_width
    angle_step = math.pi / (2.0 * seq_length)
    angles = jnp.arange(seq_length).astype(jnp.float32).reshape(block_count, block_width) * angle_step
    causal = jnp.arange(block_width)[:, None] >= jnp.arange(block_width)[None, :]

    def split_blocks(source):
        return jnp.moveaxis(source.reshape(seq_count, block_count, block_width, head_count, head_size), 1, 0)

    def block_step(carried, inputs):
        cosine_state, sine_state, cosine_norm, sine_norm = carried
        query_block, key_block, value_block, block_angles = inputs
        cosine_factor = jnp.cos(block_angles)[None, :, None, None]
        sine_factor = jnp.sin(block_angles)[None, :, None, None]
        weighting = jnp.where(causal, jnp.cos(block_angles[:, None] - block_angles[None, :]), 0.0)
        scores = jnp.einsum('bihe,bjhe->bhij', query_block, key_block, precision=PRECISE) * weighting
        query_cosine = query_block * cosine_factor
        query_sine = query_block * sine_factor
        numerator = jnp.einsum('bhij,bjhe->bihe', scores, value_block, precision=PRECISE)
        numerator = numerator + jnp.einsum('bihe,bhef->bihf', query_cosine, cosine_state, precision=PRECISE)
        numerator = numerator + jnp.einsum('bihe,bhef->bihf', query_sine, sine_state, precision=PRECISE)
        denominator = jnp.transpose(lax.optimization_barrier(jnp.sum(scores, axis=-1)), (0, 2, 1))
        denominator = denominator + jnp.einsum('bihe,bhe->bih', query_cosine, cosine_norm, precision=PRECISE)
        denominator = denominator + jnp.einsum('bihe,bhe->bih', query_sine, sine_norm, precision=PRECISE)
        key_cosine = key_block * cosine_factor
        key_sine = key_block * sine_factor
        cosine_state = cosine_state + jnp.einsum('bjhe,bjhf->bhef', key_cosine, value_block, precision=PRECISE)
        sine_state = sine_state + jnp.einsum('bjhe,bjhf->bhef', key_sine, value_block, precision=PRECISE)
        cosine_norm = cosine_norm + lax.optimization_barrier(jnp.sum(key_cosine, axis=1))
        sine_norm = sine_norm + lax.optimization_barrier(jnp.sum(key_sine, axis=1))
        return ((cosine_state, sine_state, cosine_norm, sine_norm), numerator / denominator[..., None])
    initial = (jnp.zeros((seq_count, head_count, head_size, head_size), jnp.float32), jnp.zeros((seq_count, head_count, head_size, head_size), jnp.float32), jnp.zeros((seq_count, head_count, head_size), jnp.float32), jnp.zeros((seq_count, head_count, head_size), jnp.float32))
    unused_state, blocks_out = lax.scan(jax.checkpoint(block_step), initial, (split_blocks(queries), split_blocks(keys_in), split_blocks(values_in), angles))
    return jnp.moveaxis(blocks_out, 0, 1).reshape(seq_count, seq_length, head_count, head_size)

def layer_forward(layer_input, weights):
    inward, inbias, outward, outbias, normgain, normshift, expand, expbias, shrink, shrbias, lastgain, lastshift = weights
    row_count, model_width = layer_input.shape
    packed = low_back(matmul(layer_input, inward) + inbias)
    queries = low(jax.nn.softplus(packed[:, :model_width]))
    keys_in = low(jax.nn.softplus(packed[:, model_width:2 * model_width]))
    values_in = low(packed[:, 2 * model_width:])
    shape_four = (row_count // SEQ, SEQ, model_width // HEAD, HEAD)
    attended = attention(queries.reshape(shape_four), keys_in.reshape(shape_four), values_in.reshape(shape_four), min(64, SEQ // 4)).reshape(row_count, model_width)
    attended = low(low_back(attended))
    branch = low_back(matmul(attended, outward) + outbias)
    hidden = layer_norm(layer_input + branch, normgain, normshift)
    lifted = low_back(matmul(low(hidden), expand) + expbias)
    active = low(jax.nn.gelu(lifted, approximate=False))
    reduced = low_back(matmul(active, shrink) + shrbias)
    return layer_norm(hidden + reduced, lastgain, lastshift)

def reference(boundary, inward, inbias, outward, outbias, normgain, normshift, expand, expbias, shrink, shrbias, lastgain, lastshift):
    stacked = (inward, inbias, outward, outbias, normgain, normshift, expand, expbias, shrink, shrbias, lastgain, lastshift)
    firsts = tuple((element[0].astype(jnp.float32) for element in stacked))
    seconds = tuple((element[1].astype(jnp.float32) for element in stacked))
    groups = TOKENS // TOK_DEV
    entries = boundary[0].astype(jnp.float32).reshape(groups, TOK_DEV, D)
    cotangents = boundary[1].astype(jnp.float32).reshape(groups, TOK_DEV, D)

    def both_layers(layer_input, first_set, second_set):
        middle = low(low_back(layer_forward(layer_input, first_set)))
        return layer_forward(middle, second_set)

    def group_step(totals, group_pair):
        layer_input, seed_grad = group_pair
        output, pullback = jax.vjp(both_layers, layer_input, firsts, seconds)
        input_grad, first_grads, second_grads = pullback(seed_grad)
        totals = jax.tree.map(jnp.add, totals, (first_grads, second_grads))
        return (totals, (input_grad.astype(jnp.bfloat16), output.astype(jnp.bfloat16)))
    initial = jax.tree.map(jnp.zeros_like, (firsts, seconds))
    totals, (input_grads, outputs) = lax.scan(group_step, initial, (entries, cotangents))
    results = jnp.stack([input_grads.reshape(TOKENS, D), outputs.reshape(TOKENS, D)])
    gradients = [jnp.stack([first_grad, second_grad]) for first_grad, second_grad in zip(totals[0], totals[1])]
    return (results, gradients[0], gradients[1], gradients[2], gradients[3], gradients[4], gradients[5], gradients[6], gradients[7], gradients[8], gradients[9], gradients[10], gradients[11])
```

```python
from functools import partial
import math

import jax
import jax.numpy as jnp
import numpy as np
from jax import lax
from jax.experimental import pallas as pl
from jax.experimental.pallas import tpu as pltpu
from jax.sharding import PartitionSpec as P

HEAD = 64
SEQ = 512
CHUNK = 256
PAIR = 2 * HEAD
EPSILON = 1e-05
MESH = pl.DeviceIdType.MESH
F32 = jnp.float32
BF16 = jnp.bfloat16
VMEM_BYTES = 63 * 2**20


def dot(a, b):
    return jnp.dot(a, b, preferred_element_type=F32)


def dot_nt(a, b):
    return lax.dot_general(a, b, (((1,), (1,)), ((), ())), preferred_element_type=F32)


def dot_tn(a, b):
    return lax.dot_general(a, b, (((0,), (0,)), ((), ())), preferred_element_type=F32)


def softplus(p):
    return jnp.maximum(p, 0.0) + jnp.log1p(jnp.exp(-jnp.abs(p)))


def sigmoid_of_softplus(q):
    series = q * (1.0 - q * (0.5 - q * (1.0 / 6.0 - q * (1.0 / 24.0))))
    return jnp.where(q < 0.03, series, 1.0 - jnp.exp(-q))


def cosine_tables():
    step = math.pi / (2.0 * SEQ)
    i = np.arange(CHUNK)[:, None]
    j = np.arange(CHUNK)[None, :]
    near = np.where(i >= j, np.cos((i - j) * step), 0.0).astype(np.float32)
    far = np.cos((i - j + CHUNK) * step).astype(np.float32)
    return near, far


def lane_masks():
    lanes = np.arange(PAIR)
    return np.stack([lanes < HEAD, lanes >= HEAD])[:, None, :].astype(np.float32)


def layer_kernel(
    boundary, inward, outward, expand, shrink,
    inbias, outbias, normgain, normshift, expbias, shrbias, lastgain, lastshift,
    near, far, masks,
    results, f_x, f_a, f_h, f_g, f_p, f_o, f_u, f_f, vectors,
    win, wout, wexp, wshr,
    xs, qkv, att, low, zin, hbs, gs, gps, n1s, n2s, s1s, s2s, dys, ybuf, xbuf,
    acc, keep, das, carry,
    load_sems, out_sems, res_sems, fwd_send, fwd_recv, bwd_send, bwd_recv,
):
    rows_all, width = xs.shape
    hidden = wexp.shape[1]
    chunks = rows_all // CHUNK
    pairs = width // PAIR
    slabs = hidden // width
    section = lax.axis_index("section")
    first = section == 0
    peer = {"section": 1 - section}

    loads = [
        pltpu.make_async_copy(src, dst, load_sems.at[i])
        for i, (src, dst) in enumerate(
            [(inward, win), (outward, wout), (expand, wexp), (shrink, wshr)]
        )
    ]
    load_x = pltpu.make_async_copy(boundary, xs, load_sems.at[4])
    load_y = pltpu.make_async_copy(boundary, dys, load_sems.at[4])

    @pl.when(first)
    def _():
        load_x.start()

    for load in loads:
        load.start()

    @pl.when(jnp.logical_not(first))
    def _():
        load_y.start()

    barrier = pltpu.get_barrier_semaphore()
    pl.semaphore_signal(barrier, inc=1, device_id=peer, device_id_type=MESH)
    vectors[...] = jnp.zeros_like(vectors)
    pl.semaphore_wait(barrier, 1)

    def rows_of(c):
        return pl.ds(pl.multiple_of(c * CHUNK, CHUNK), CHUNK)

    def send_forward(c):
        return pltpu.make_async_remote_copy(
            src_ref=ybuf.at[rows_of(c)], dst_ref=xs.at[rows_of(c)],
            send_sem=fwd_send.at[c], recv_sem=fwd_recv.at[c],
            device_id=peer, device_id_type=MESH,
        )

    def send_backward(c):
        return pltpu.make_async_remote_copy(
            src_ref=xbuf.at[rows_of(c)], dst_ref=dys.at[rows_of(c)],
            send_sem=bwd_send.at[c], recv_sem=bwd_recv.at[c],
            device_id=peer, device_id_type=MESH,
        )

    def result_copy(buf, c):
        return pltpu.make_async_copy(buf.at[rows_of(c)], results.at[rows_of(c)], res_sems.at[c])

    early = [(xs, f_x), (att, f_a), (hbs, f_h), (gs, f_g)]
    late = [(qkv, f_p), (n1s, f_o), (gps, f_u), (n2s, f_f)]

    def factor_copies(c, which, base):
        return [
            pltpu.make_async_copy(src.at[rows_of(c)], dst.at[rows_of(c)], out_sems.at[c, base + i])
            for i, (src, dst) in enumerate(which)
        ]

    def column_sum(at, value):
        vectors[at] += jnp.sum(value, axis=0, keepdims=True)

    def norm_forward(e):
        mean = jnp.mean(e, axis=-1, keepdims=True)
        center = e - mean
        s = lax.rsqrt(jnp.mean(center * center, axis=-1, keepdims=True) + EPSILON)
        return center * s, s

    def norm_backward(dn, n, s):
        m1 = jnp.mean(dn, axis=-1, keepdims=True)
        m2 = jnp.mean(dn * n, axis=-1, keepdims=True)
        return s * (dn - m1 - n * m2)

    def pair_columns(hp):
        return [pl.ds(pl.multiple_of(i * width + hp * PAIR, PAIR), PAIR) for i in range(3)]

    def attend(c, wide):
        rows = rows_of(c)
        tiles = [(rows, near)] + ([(rows_of(c - 1), far)] if wide else [])
        m = [masks[a].astype(BF16) for a in range(2)]

        def one_pair(hp, _):
            cq, ck, cv = pair_columns(hp)
            q = qkv[rows, cq]
            nz = None
            for key_rows, weights in tiles:
                k, v = qkv[key_rows, ck], qkv[key_rows, cv]
                for a in range(2):
                    s = (dot_nt(q * m[a], k) * weights[...]).astype(BF16)
                    right = jnp.concatenate(
                        [v * m[a], jnp.broadcast_to(m[a], v.shape)], axis=1
                    )
                    part = dot(s, right)
                    nz = part if nz is None else nz + part
            inverse = 1.0 / nz[:, PAIR:]
            a_full = nz[:, :PAIR] * inverse
            a_high = a_full.astype(BF16)
            att[rows, cq] = a_high
            low[rows, cq] = (a_full - a_high.astype(F32)).astype(BF16)
            zin[rows, cq] = inverse.astype(BF16)
            return 0

        lax.fori_loop(0, pairs, one_pair, 0)

    def attend_backward(c, wide):
        rows = rows_of(c)
        m = [masks[a].astype(BF16) for a in range(2)]

        def one_pair(hp, _):
            cq, ck, cv = pair_columns(hp)
            q, k, v = qkv[rows, cq], qkv[rows, ck], qkv[rows, cv]
            dn = (das[:, cq].astype(F32) * zin[rows, cq].astype(F32)).astype(BF16)
            prod = dn.astype(F32) * (att[rows, cq].astype(F32) + low[rows, cq].astype(F32))
            dz = [-jnp.sum(prod * masks[a], axis=-1, keepdims=True) for a in range(2)]
            qm = [q * m[a] for a in range(2)]
            dnm = [dn * m[a] for a in range(2)]

            def tile(kt, vt, weights):
                dq = dk = dv = None
                for a in range(2):
                    w = weights[...]
                    s = (dot_nt(qm[a], kt) * w).astype(BF16)
                    ds = ((dot_nt(dnm[a], vt) + dz[a]) * w).astype(BF16)
                    parts = (dot(ds, kt * m[a]), dot_tn(ds, qm[a]), dot_tn(s, dnm[a]))
                    dq, dk, dv = parts if a == 0 else (
                        dq + parts[0], dk + parts[1], dv + parts[2]
                    )
                return dq, dk, dv

            dq, dk, dv = tile(k, v, near)
            wide_cols = [pl.ds(pl.multiple_of(i * width + hp * PAIR, PAIR), PAIR) for i in range(2)]
            if wide:
                kp, vp = qkv[rows_of(c - 1), ck], qkv[rows_of(c - 1), cv]
                dqp, dkp, dvp = tile(kp, vp, far)
                dq = dq + dqp
                carry[:, wide_cols[0]] = dkp
                carry[:, wide_cols[1]] = dvp
            else:
                dk = dk + carry[:, wide_cols[0]]
                dv = dv + carry[:, wide_cols[1]]
            qkv[rows, cq] = (dq * sigmoid_of_softplus(q.astype(F32))).astype(BF16)
            qkv[rows, ck] = (dk * sigmoid_of_softplus(k.astype(F32))).astype(BF16)
            qkv[rows, cv] = dv.astype(BF16)
            return 0

        lax.fori_loop(0, pairs, one_pair, 0)

    def forward(c, begins):
        rows = rows_of(c)

        @pl.when(begins)
        def _():
            loads[0].wait()

            @pl.when(first)
            def _():
                load_x.wait()

        @pl.when(jnp.logical_not(first))
        def _():
            send_forward(c).wait_recv()

        for i in range(3):
            cols = slice(i * width, (i + 1) * width)
            p = dot(xs[rows, :], win[:, cols]) + inbias[:, cols]
            qkv[rows, cols] = (softplus(p) if i < 2 else p).astype(BF16)

        @pl.when(c % 2 == 0)
        def _():
            attend(c, False)

        @pl.when(c % 2 == 1)
        def _():
            attend(c, True)

        @pl.when(begins)
        def _():
            for load in loads[1:]:
                load.wait()

        e = xs[rows, :].astype(F32) + (dot(att[rows, :], wout[...]) + outbias[...])
        n1, s1 = norm_forward(e)
        n1s[rows, :] = n1.astype(BF16)
        s1s[rows, :] = s1
        h = n1 * normgain[...] + normshift[...]
        hbs[rows, :] = h.astype(BF16)
        acc[...] = h + shrbias[...]
        for i in range(slabs):
            cols = slice(i * width, (i + 1) * width)
            u = dot(hbs[rows, :], wexp[:, cols]) + expbias[:, cols]
            phi = 0.5 * (1.0 + lax.erf(u * math.sqrt(0.5)))
            g = (u * phi).astype(BF16)
            gs[rows, cols] = g
            gps[rows, cols] = (
                phi + u * (jnp.exp(u * u * -0.5) * (1.0 / math.sqrt(2.0 * math.pi)))
            ).astype(BF16)
            acc[...] += dot(g, wshr[cols, :])
        n2, s2 = norm_forward(acc[...])
        n2s[rows, :] = n2.astype(BF16)
        s2s[rows, :] = s2
        ybuf[rows, :] = (n2 * lastgain[...] + lastshift[...]).astype(BF16)

        @pl.when(first)
        def _():
            send_forward(c).start()

        @pl.when(jnp.logical_not(first))
        def _():
            result_copy(ybuf, c).start()

        for copy in factor_copies(c, early, 0):
            copy.start()

    def backward(c):
        rows = rows_of(c)

        @pl.when(first)
        def _():
            send_backward(c).wait_recv()

        @pl.when(jnp.logical_and(jnp.logical_not(first), c == 1))
        def _():
            load_y.wait()

        dy = dys[rows, :].astype(F32)
        n2 = n2s[rows, :].astype(F32)
        column_sum(7 + slabs, dy * n2)
        column_sum(8 + slabs, dy)
        dr = norm_backward(dy * lastgain[...], n2, s2s[rows, :])
        df = dr.astype(BF16)
        n2s[rows, :] = df
        column_sum(6 + slabs, df.astype(F32))
        acc[...] = dr
        for i in range(slabs):
            cols = slice(i * width, (i + 1) * width)
            dg = dot_nt(n2s[rows, :], wshr[cols, :])
            du = (dg * gps[rows, cols].astype(F32)).astype(BF16)
            gps[rows, cols] = du
            column_sum(6 + i, du.astype(F32))
            acc[...] += dot_nt(du, wexp[:, cols])
        dh = acc[...]
        n1 = n1s[rows, :].astype(F32)
        column_sum(4, dh * n1)
        column_sum(5, dh)
        de = norm_backward(dh * normgain[...], n1, s1s[rows, :])
        keep[...] = de
        do = de.astype(BF16)
        n1s[rows, :] = do
        column_sum(3, do.astype(F32))
        das[...] = dot_nt(do, wout[...]).astype(BF16)

        @pl.when(c % 2 == 0)
        def _():
            attend_backward(c, False)

        @pl.when(c % 2 == 1)
        def _():
            attend_backward(c, True)

        for i in range(3):
            column_sum(i, qkv[rows, i * width : (i + 1) * width].astype(F32))
        dx = keep[...] + dot_nt(qkv[rows, :], win[...])
        xbuf[rows, :] = dx.astype(BF16)

        @pl.when(first)
        def _():
            result_copy(xbuf, c).start()

        @pl.when(jnp.logical_not(first))
        def _():
            send_backward(c).start()

        for copy in factor_copies(c, late, 4):
            copy.start()

    def step(t, _):
        group, place = t // 4, t % 4
        ahead = jnp.where(first, t < chunks, place < 2)
        c_forward = jnp.where(first, t, 2 * group + place)
        back = t - chunks
        c_backward = jnp.where(first, 2 * (back // 2) + 1 - back % 2, 2 * group + 3 - place)

        @pl.when(ahead)
        def _():
            forward(c_forward, t == 0)

        @pl.when(jnp.logical_not(ahead))
        def _():
            backward(c_backward)

        return 0

    lax.fori_loop(0, 2 * chunks, step, 0)

    def finish(c, _):
        @pl.when(first)
        def _():
            send_forward(c).wait_send()
            result_copy(xbuf, c).wait()

        @pl.when(jnp.logical_not(first))
        def _():
            send_backward(c).wait_send()
            result_copy(ybuf, c).wait()

        for copy in factor_copies(c, early, 0) + factor_copies(c, late, 4):
            copy.wait()
        return 0

    lax.fori_loop(0, chunks, finish, 0)


def run_layer(boundary, weights, biases):
    rows, width = boundary.shape
    hidden = weights[2].shape[1]
    chunks = rows // CHUNK
    near, far = cosine_tables()
    masks = lane_masks()
    slabs = hidden // width
    any_space = pl.BlockSpec(memory_space=pl.ANY)
    vmem = pl.BlockSpec(memory_space=pltpu.VMEM)
    out_widths = [width] * 4 + [hidden, 3 * width, width, hidden, width]
    out_shape = [jax.ShapeDtypeStruct((rows, w), BF16) for w in out_widths]
    out_shape.append(jax.ShapeDtypeStruct((9 + slabs, 1, width), F32))
    low = lambda *shape: pltpu.VMEM(shape, BF16)
    wide = lambda *shape: pltpu.VMEM(shape, F32)
    dma = pltpu.SemaphoreType.DMA
    return pl.pallas_call(
        layer_kernel,
        out_shape=out_shape,
        in_specs=[any_space] * 5 + [vmem] * 11,
        out_specs=[any_space] * 9 + [vmem],
        scratch_shapes=[
            low(width, 3 * width), low(width, width), low(width, hidden), low(hidden, width),
            low(rows, width), low(rows, 3 * width), low(rows, width), low(rows, width),
            low(rows, width), low(rows, width), low(rows, hidden), low(rows, hidden),
            low(rows, width), low(rows, width), wide(rows, 1), wide(rows, 1),
            low(rows, width), low(rows, width), low(rows, width),
            wide(CHUNK, width), wide(CHUNK, width), low(CHUNK, width), wide(CHUNK, 2 * width),
            dma((5,)), dma((chunks, 8)), dma((chunks,)), dma((chunks,)), dma((chunks,)),
            dma((chunks,)), dma((chunks,)),
        ],
        compiler_params=pltpu.CompilerParams(
            collective_id=0, has_side_effects=True, vmem_limit_bytes=VMEM_BYTES
        ),
        name="layer",
    )(boundary, *weights, *biases, jnp.asarray(near), jnp.asarray(far), jnp.asarray(masks))


def shards(
    boundary, inward, inbias, outward, outbias, normgain, normshift, expand, expbias,
    shrink, shrbias, lastgain, lastshift,
):
    width = outward.shape[-1]
    hidden = expand.shape[-1]
    slabs = hidden // width
    outs = run_layer(
        boundary[0],
        (inward[0], outward[0], expand[0], shrink[0]),
        (inbias, outbias, normgain, normshift, expbias, shrbias, lastgain, lastshift),
    )
    results, f_x, f_a, f_h, f_g, f_p, f_o, f_u, f_f, vectors = outs

    def summed(left, right):
        grad = dot_tn(left, right).astype(BF16)
        mine = lax.psum_scatter(grad, "dp", scatter_dimension=0, tiled=True)
        return lax.all_gather(mine, "dp", axis=0, tiled=True).astype(F32)[None]

    vec = lax.psum(vectors.reshape(-1), "dp")

    def piece(start, count):
        return vec[start * width : (start + count) * width][None]

    return (
        results[None],
        summed(f_x, f_p), piece(0, 3),
        summed(f_a, f_o), piece(3, 1), piece(4, 1), piece(5, 1),
        summed(f_h, f_u), piece(6, slabs),
        summed(f_g, f_f), piece(6 + slabs, 1), piece(7 + slabs, 1), piece(8 + slabs, 1),
    )


def solution(mesh):
    matrix, vector = P("section", None, None), P("section", None)
    params = (
        matrix, vector, matrix, vector, vector, vector, matrix, vector, matrix, vector,
        vector, vector,
    )
    specs = (P("section", "dp", None),) + params
    return jax.shard_map(shards, mesh=mesh, in_specs=specs, out_specs=specs, check_vma=False)
```

```python
from functools import partial
import math

import jax
import jax.numpy as jnp
import numpy as np
from jax import lax
from jax.experimental import pallas as pl
from jax.experimental.pallas import tpu as pltpu
from jax.sharding import PartitionSpec as P

HEAD = 64
SEQ = 512
CHUNK = 256
PAIR = 2 * HEAD
EPSILON = 1e-05
MESH = pl.DeviceIdType.MESH
F32 = jnp.float32
BF16 = jnp.bfloat16
VMEM_BYTES = 63 * 2**20


def dot(a, b):
    return jnp.dot(a, b, preferred_element_type=F32)


def dot_nt(a, b):
    return lax.dot_general(a, b, (((1,), (1,)), ((), ())), preferred_element_type=F32)


def dot_tn(a, b):
    return lax.dot_general(a, b, (((0,), (0,)), ((), ())), preferred_element_type=F32)


def softplus(p):
    return jnp.maximum(p, 0.0) + jnp.log1p(jnp.exp(-jnp.abs(p)))


def sigmoid_of_softplus(q):
    series = q * (1.0 - q * (0.5 - q * (1.0 / 6.0 - q * (1.0 / 24.0))))
    return jnp.where(q < 0.03, series, 1.0 - jnp.exp(-q))


def cosine_tables():
    step = math.pi / (2.0 * SEQ)
    i = np.arange(CHUNK)[:, None]
    j = np.arange(CHUNK)[None, :]
    near = np.where(i >= j, np.cos((i - j) * step), 0.0).astype(np.float32)
    far = np.cos((i - j + CHUNK) * step).astype(np.float32)
    return near, far


def lane_masks():
    lanes = np.arange(PAIR)
    return np.stack([lanes < HEAD, lanes >= HEAD])[:, None, :].astype(np.float32)


def layer_kernel(
    boundary, inward, outward, expand, shrink,
    inbias, outbias, normgain, normshift, expbias, shrbias, lastgain, lastshift,
    near, far, masks,
    results, f_x, f_a, f_h, f_g, f_p, f_o, f_u, f_f, vector_rows,
    win, wout, wexp, wshr,
    xs, qkv, att, low, zin, hbs, gs, gps, n1s, n2s, s1s, s2s, dys, ybuf, xbuf,
    acc, keep, das, carry, vectors,
    load_sems, out_sems, res_sems, fwd_send, fwd_recv, bwd_send, bwd_recv,
):
    rows_all, width = xs.shape
    hidden = wexp.shape[1]
    chunks = rows_all // CHUNK
    pairs = width // PAIR
    slabs = hidden // width
    section = lax.axis_index("section")
    first = section == 0
    peer = {"section": 1 - section}

    loads = [
        pltpu.make_async_copy(src, dst, load_sems.at[i])
        for i, (src, dst) in enumerate(
            [(inward, win), (outward, wout), (expand, wexp), (shrink, wshr)]
        )
    ]
    load_x = pltpu.make_async_copy(boundary, xs, load_sems.at[4])
    load_y = pltpu.make_async_copy(boundary, dys, load_sems.at[4])

    @pl.when(first)
    def _():
        load_x.start()

    for load in loads:
        load.start()

    @pl.when(jnp.logical_not(first))
    def _():
        load_y.start()

    barrier = pltpu.get_barrier_semaphore()
    pl.semaphore_signal(barrier, inc=1, device_id=peer, device_id_type=MESH)
    vectors[...] = jnp.zeros_like(vectors)
    pl.semaphore_wait(barrier, 1)

    def rows_of(c):
        return pl.ds(pl.multiple_of(c * CHUNK, CHUNK), CHUNK)

    def send_forward(c):
        return pltpu.make_async_remote_copy(
            src_ref=ybuf.at[rows_of(c)], dst_ref=xs.at[rows_of(c)],
            send_sem=fwd_send.at[c], recv_sem=fwd_recv.at[c],
            device_id=peer, device_id_type=MESH,
        )

    def send_backward(c):
        return pltpu.make_async_remote_copy(
            src_ref=xbuf.at[rows_of(c)], dst_ref=dys.at[rows_of(c)],
            send_sem=bwd_send.at[c], recv_sem=bwd_recv.at[c],
            device_id=peer, device_id_type=MESH,
        )

    def result_copy(buf, c):
        return pltpu.make_async_copy(buf.at[rows_of(c)], results.at[rows_of(c)], res_sems.at[c])

    early = [(xs, f_x), (att, f_a), (hbs, f_h), (gs, f_g)]
    late = [(qkv, f_p), (n1s, f_o), (gps, f_u), (n2s, f_f)]

    def factor_copies(c, which, base):
        return [
            pltpu.make_async_copy(src.at[rows_of(c)], dst.at[rows_of(c)], out_sems.at[c, base + i])
            for i, (src, dst) in enumerate(which)
        ]

    def column_sum(at, value):
        vectors[at] += jnp.sum(value, axis=0, keepdims=True)

    def norm_forward(e):
        mean = jnp.mean(e, axis=-1, keepdims=True)
        center = e - mean
        s = lax.rsqrt(jnp.mean(center * center, axis=-1, keepdims=True) + EPSILON)
        return center * s, s

    def norm_backward(dn, n, s):
        m1 = jnp.mean(dn, axis=-1, keepdims=True)
        m2 = jnp.mean(dn * n, axis=-1, keepdims=True)
        return s * (dn - m1 - n * m2)

    def pair_columns(hp):
        return [pl.ds(pl.multiple_of(i * width + hp * PAIR, PAIR), PAIR) for i in range(3)]

    def attend(c, wide):
        rows = rows_of(c)
        tiles = [(rows, near)] + ([(rows_of(c - 1), far)] if wide else [])
        m = [masks[a].astype(BF16) for a in range(2)]

        def one_pair(hp, _):
            cq, ck, cv = pair_columns(hp)
            q = qkv[rows, cq]
            nz = None
            for key_rows, weights in tiles:
                k, v = qkv[key_rows, ck], qkv[key_rows, cv]
                for a in range(2):
                    s = (dot_nt(q * m[a], k) * weights[...]).astype(BF16)
                    right = jnp.concatenate(
                        [v * m[a], jnp.broadcast_to(m[a], v.shape)], axis=1
                    )
                    part = dot(s, right)
                    nz = part if nz is None else nz + part
            inverse = 1.0 / nz[:, PAIR:]
            a_full = nz[:, :PAIR] * inverse
            a_high = a_full.astype(BF16)
            att[rows, cq] = a_high
            low[rows, cq] = (a_full - a_high.astype(F32)).astype(BF16)
            zin[rows, cq] = inverse.astype(BF16)
            return 0

        lax.fori_loop(0, pairs, one_pair, 0)

    def attend_backward(c, wide):
        rows = rows_of(c)
        m = [masks[a].astype(BF16) for a in range(2)]

        def one_pair(hp, _):
            cq, ck, cv = pair_columns(hp)
            q, k, v = qkv[rows, cq], qkv[rows, ck], qkv[rows, cv]
            dn = (das[:, cq].astype(F32) * zin[rows, cq].astype(F32)).astype(BF16)
            prod = dn.astype(F32) * (att[rows, cq].astype(F32) + low[rows, cq].astype(F32))
            dz = [-jnp.sum(prod * masks[a], axis=-1, keepdims=True) for a in range(2)]
            qm = [q * m[a] for a in range(2)]
            dnm = [dn * m[a] for a in range(2)]

            def tile(kt, vt, weights):
                dq = dk = dv = None
                for a in range(2):
                    w = weights[...]
                    s = (dot_nt(qm[a], kt) * w).astype(BF16)
                    ds = ((dot_nt(dnm[a], vt) + dz[a]) * w).astype(BF16)
                    parts = (dot(ds, kt * m[a]), dot_tn(ds, qm[a]), dot_tn(s, dnm[a]))
                    dq, dk, dv = parts if a == 0 else (
                        dq + parts[0], dk + parts[1], dv + parts[2]
                    )
                return dq, dk, dv

            dq, dk, dv = tile(k, v, near)
            wide_cols = [pl.ds(pl.multiple_of(i * width + hp * PAIR, PAIR), PAIR) for i in range(2)]
            if wide:
                kp, vp = qkv[rows_of(c - 1), ck], qkv[rows_of(c - 1), cv]
                dqp, dkp, dvp = tile(kp, vp, far)
                dq = dq + dqp
                carry[:, wide_cols[0]] = dkp
                carry[:, wide_cols[1]] = dvp
            else:
                dk = dk + carry[:, wide_cols[0]]
                dv = dv + carry[:, wide_cols[1]]
            qkv[rows, cq] = (dq * sigmoid_of_softplus(q.astype(F32))).astype(BF16)
            qkv[rows, ck] = (dk * sigmoid_of_softplus(k.astype(F32))).astype(BF16)
            qkv[rows, cv] = dv.astype(BF16)
            return 0

        lax.fori_loop(0, pairs, one_pair, 0)

    def forward(c, begins):
        rows = rows_of(c)

        @pl.when(begins)
        def _():
            loads[0].wait()

            @pl.when(first)
            def _():
                load_x.wait()

        @pl.when(jnp.logical_not(first))
        def _():
            send_forward(c).wait_recv()

        for i in range(3):
            cols = slice(i * width, (i + 1) * width)
            p = dot(xs[rows, :], win[:, cols]) + inbias[:, cols]
            qkv[rows, cols] = (softplus(p) if i < 2 else p).astype(BF16)

        @pl.when(c % 2 == 0)
        def _():
            attend(c, False)

        @pl.when(c % 2 == 1)
        def _():
            attend(c, True)

        @pl.when(begins)
        def _():
            for load in loads[1:]:
                load.wait()

        e = xs[rows, :].astype(F32) + (dot(att[rows, :], wout[...]) + outbias[...])
        n1, s1 = norm_forward(e)
        n1s[rows, :] = n1.astype(BF16)
        s1s[rows, :] = s1
        h = n1 * normgain[...] + normshift[...]
        hbs[rows, :] = h.astype(BF16)
        acc[...] = h + shrbias[...]
        for i in range(slabs):
            cols = slice(i * width, (i + 1) * width)
            u = dot(hbs[rows, :], wexp[:, cols]) + expbias[:, cols]
            phi = 0.5 * (1.0 + lax.erf(u * math.sqrt(0.5)))
            g = (u * phi).astype(BF16)
            gs[rows, cols] = g
            gps[rows, cols] = (
                phi + u * (jnp.exp(u * u * -0.5) * (1.0 / math.sqrt(2.0 * math.pi)))
            ).astype(BF16)
            acc[...] += dot(g, wshr[cols, :])
        n2, s2 = norm_forward(acc[...])
        n2s[rows, :] = n2.astype(BF16)
        s2s[rows, :] = s2
        ybuf[rows, :] = (n2 * lastgain[...] + lastshift[...]).astype(BF16)

        @pl.when(first)
        def _():
            send_forward(c).start()

        @pl.when(jnp.logical_not(first))
        def _():
            result_copy(ybuf, c).start()

        for copy in factor_copies(c, early, 0):
            copy.start()

    def backward(c):
        rows = rows_of(c)

        @pl.when(first)
        def _():
            send_backward(c).wait_recv()

        @pl.when(jnp.logical_and(jnp.logical_not(first), c == 1))
        def _():
            load_y.wait()

        dy = dys[rows, :].astype(F32)
        n2 = n2s[rows, :].astype(F32)
        column_sum(7 + slabs, dy * n2)
        column_sum(8 + slabs, dy)
        dr = norm_backward(dy * lastgain[...], n2, s2s[rows, :])
        df = dr.astype(BF16)
        n2s[rows, :] = df
        column_sum(6 + slabs, df.astype(F32))
        acc[...] = dr
        for i in range(slabs):
            cols = slice(i * width, (i + 1) * width)
            dg = dot_nt(n2s[rows, :], wshr[cols, :])
            du = (dg * gps[rows, cols].astype(F32)).astype(BF16)
            gps[rows, cols] = du
            column_sum(6 + i, du.astype(F32))
            acc[...] += dot_nt(du, wexp[:, cols])
        dh = acc[...]
        n1 = n1s[rows, :].astype(F32)
        column_sum(4, dh * n1)
        column_sum(5, dh)
        de = norm_backward(dh * normgain[...], n1, s1s[rows, :])
        keep[...] = de
        do = de.astype(BF16)
        n1s[rows, :] = do
        column_sum(3, do.astype(F32))
        das[...] = dot_nt(do, wout[...]).astype(BF16)

        @pl.when(c % 2 == 0)
        def _():
            attend_backward(c, False)

        @pl.when(c % 2 == 1)
        def _():
            attend_backward(c, True)

        for i in range(3):
            column_sum(i, qkv[rows, i * width : (i + 1) * width].astype(F32))
        dx = keep[...] + dot_nt(qkv[rows, :], win[...])
        xbuf[rows, :] = dx.astype(BF16)

        @pl.when(first)
        def _():
            result_copy(xbuf, c).start()

        @pl.when(jnp.logical_not(first))
        def _():
            send_backward(c).start()

        for copy in factor_copies(c, late, 4):
            copy.start()

    def step(t, _):
        group, place = t // 4, t % 4
        ahead = jnp.where(first, t < chunks, place < 2)
        c_forward = jnp.where(first, t, 2 * group + place)
        back = t - chunks
        c_backward = jnp.where(first, 2 * (back // 2) + 1 - back % 2, 2 * group + 3 - place)

        @pl.when(ahead)
        def _():
            forward(c_forward, t == 0)

        @pl.when(jnp.logical_not(ahead))
        def _():
            backward(c_backward)

        return 0

    lax.fori_loop(0, 2 * chunks, step, 0)
    for i in range(vectors.shape[0]):
        vector_rows[i : i + 1, :] = vectors[i]

    def finish(c, _):
        @pl.when(first)
        def _():
            send_forward(c).wait_send()
            result_copy(xbuf, c).wait()

        @pl.when(jnp.logical_not(first))
        def _():
            send_backward(c).wait_send()
            result_copy(ybuf, c).wait()

        for copy in factor_copies(c, early, 0) + factor_copies(c, late, 4):
            copy.wait()
        return 0

    lax.fori_loop(0, chunks, finish, 0)


def run_layer(boundary, weights, biases):
    rows, width = boundary.shape
    hidden = weights[2].shape[1]
    chunks = rows // CHUNK
    near, far = cosine_tables()
    masks = lane_masks()
    slabs = hidden // width
    any_space = pl.BlockSpec(memory_space=pl.ANY)
    vmem = pl.BlockSpec(memory_space=pltpu.VMEM)
    out_widths = [width] * 4 + [hidden, 3 * width, width, hidden, width]
    out_shape = [jax.ShapeDtypeStruct((rows, w), BF16) for w in out_widths]
    vector_count = -(-(9 + slabs) // 8) * 8
    out_shape.append(jax.ShapeDtypeStruct((vector_count, width), F32))
    low = lambda *shape: pltpu.VMEM(shape, BF16)
    wide = lambda *shape: pltpu.VMEM(shape, F32)
    dma = pltpu.SemaphoreType.DMA
    return pl.pallas_call(
        layer_kernel,
        out_shape=out_shape,
        in_specs=[any_space] * 5 + [vmem] * 11,
        out_specs=[any_space] * 9 + [vmem],
        scratch_shapes=[
            low(width, 3 * width), low(width, width), low(width, hidden), low(hidden, width),
            low(rows, width), low(rows, 3 * width), low(rows, width), low(rows, width),
            low(rows, width), low(rows, width), low(rows, hidden), low(rows, hidden),
            low(rows, width), low(rows, width), wide(rows, 1), wide(rows, 1),
            low(rows, width), low(rows, width), low(rows, width),
            wide(CHUNK, width), wide(CHUNK, width), low(CHUNK, width), wide(CHUNK, 2 * width),
            wide(vector_count, 1, width),
            dma((5,)), dma((chunks, 8)), dma((chunks,)), dma((chunks,)), dma((chunks,)),
            dma((chunks,)), dma((chunks,)),
        ],
        compiler_params=pltpu.CompilerParams(
            collective_id=0, has_side_effects=True, vmem_limit_bytes=VMEM_BYTES
        ),
        name="layer",
    )(boundary, *weights, *biases, jnp.asarray(near), jnp.asarray(far), jnp.asarray(masks))


SETS = 2
LANES_Z = 4
HOP_LAG = 2


def gradient_kernel(
    f_x, f_a, f_h, f_g, f_p, f_o, f_u, f_f, vec_in,
    total, vec_out,
    x, a, h, g, p, o, u, f,
    part, core_in, chain_pair, chain_one, y_in, end_in, vec, vec_got,
    load_sems, core_s, core_r, y_s, y_r, pair_s, pair_r, one_s, one_r, end_s, end_r,
    got, z_s, yy_s, kept, out_s, out_r, vec_s, vec_r,
):
    width = x.shape[1]
    slabs = g.shape[1] // width
    me = lax.axis_index("dp")
    core, y, z = me % 2, (me // 2) % 2, me // 4
    last = LANES_Z - 1
    core_peer, y_peer = {"dp": me + 1 - 2 * core}, {"dp": me + 2 - 4 * y}
    hop = [last - z, z]
    ahead = [{"dp": me - 4}, {"dp": me + 4}]
    behind = [ahead[1], ahead[0]]

    blocks = (
        [(g, i, f, 0) for i in range(slabs)]
        + [(h, 0, u, i) for i in range(slabs)]
        + [(a, 0, o, 0)]
        + [(x, 0, p, i) for i in range(3)]
    )
    duos = len(blocks) // 2
    sets = duos * SETS
    set_rows = width // SETS
    half = set_rows // 2
    piece = half // 4

    sources = [(f_g, g), (f_f, f), (f_h, h), (f_u, u), (f_a, a), (f_o, o), (f_x, x), (f_p, p)]
    loads = [
        pltpu.make_async_copy(src, dst, load_sems.at[i]) for i, (src, dst) in enumerate(sources)
    ]
    load_at = {0: (0, 1), slabs // 2: (2, 3), slabs: (4, 5, 6, 7)}
    for load in loads:
        load.start()

    barrier = pltpu.get_barrier_semaphore()
    for peer in (core_peer, y_peer):
        pl.semaphore_signal(barrier, inc=1, device_id=peer, device_id_type=MESH)
    for d in range(2):
        @pl.when(hop[d] < last)
        def _():
            pl.semaphore_signal(barrier, inc=1, device_id=ahead[d], device_id_type=MESH)
    pl.semaphore_wait(barrier, jnp.where(jnp.logical_and(z > 0, z < last), 4, 3))

    def remote(src, dst, send, recv, peer):
        return pltpu.make_async_remote_copy(
            src_ref=src, dst_ref=dst, send_sem=send, recv_sem=recv,
            device_id=peer, device_id_type=MESH,
        )

    def span(k, d, first, count):
        start = (k % SETS) * set_rows + d * half + first * piece
        return pl.ds(pl.multiple_of(start, 16), count * piece)

    def mine(k, d, first, count=1):
        return part.at[k // SETS, core, span(k, d, first, count)]

    def final(k, d, first, count=1):
        return total.at[2 * (k // SETS) + core, span(k, d, first, count)]

    def add(dst, src):
        dst[...] = (dst[...].astype(F32) + src[...].astype(F32)).astype(BF16)

    def core_copy(m):
        return remote(part.at[m, 1 - core], core_in.at[m], core_s.at[m], core_r.at[m], core_peer)

    def y_copy(k, d):
        return remote(mine(k, d, 1 - y), y_in.at[k, d], y_s.at[k, d], y_r.at[k, d], y_peer)

    def pair_copy(k, d):
        return remote(
            mine(k, d, 2, 2), chain_pair.at[k, d], pair_s.at[k, d], pair_r.at[k, d], ahead[d]
        )

    def one_copy(k, d):
        return remote(mine(k, d, y), chain_one.at[k, d], one_s.at[k, d], one_r.at[k, d], ahead[d])

    def end_copy(k, d):
        return remote(mine(k, d, 3 - y), end_in.at[k], end_s.at[k], end_r.at[k], y_peer)

    def spread_z(k, d, b, i, src):
        return remote(src, final(k, d, b), z_s.at[k, d, i], got.at[k, d, b], behind[d])

    def spread_y(k, d, b, i, src):
        return remote(src, final(k, d, b), yy_s.at[k, d, i], got.at[k, d, b], y_peer)

    def keep_copy(k, d, b, i):
        return pltpu.make_async_copy(mine(k, d, b), final(k, d, b), kept.at[k, d, i])

    def out_copy(k, d):
        return remote(
            final(k, d, 0, 4), final(k, d, 0, 4), out_s.at[k, d], out_r.at[k, d], core_peer
        )

    def arrived(k, d, b):
        spread_z(k, d, b, 0, final(k, d, b)).wait_recv()

    outer = jnp.logical_or(z == 0, z == last)
    z_pair = {"dp": me + 4 - 8 * (z % 2)}
    z_mid = {"dp": jnp.where(z == 1, me + 4, me - 4)}
    z_out = {"dp": jnp.where(z == 1, me - 4, me + 4)}

    def vec_copy(i, peer):
        return remote(vec.at[i], vec_got.at[min(i, 3)], vec_s.at[i], vec_r.at[min(i, 3)], peer)

    def compute(m):
        for i in load_at.get(m, ()):
            loads[i].wait()
        for side in range(2):
            left, i, right, j = blocks[2 * m + side]
            for r in range(3):
                rows = slice(r * (width // 3), (r + 1) * (width // 3))
                cols = slice(i * width + rows.start, i * width + rows.stop)
                part[m, side, rows, :] = dot_tn(
                    left[:, cols], right[:, j * width : (j + 1) * width]
                ).astype(BF16)
        core_copy(m).start()

    vec[0] = vec_in[...]
    vec_copy(0, core_peer).start()
    compute(0)

    def tick(t, _):
        for m in range(1, duos):
            @pl.when(t == SETS * (m - 1))
            def _():
                compute(m)

        for i, peer in ((1, y_peer), (2, z_pair)):
            @pl.when(t == i)
            def _():
                vec_copy(i - 1, peer).wait_recv()
                vec[i] = vec[i - 1] + vec_got[i - 1]
                vec_copy(i, peer).start()

        @pl.when(t == 3)
        def _():
            vec_copy(2, z_pair).wait_recv()
            vec[3] = vec[2] + vec_got[2]

            @pl.when(jnp.logical_not(outer))
            def _():
                vec_copy(3, z_mid).start()

        @pl.when(jnp.logical_and(t == 4, jnp.logical_not(outer)))
        def _():
            vec_copy(3, z_mid).wait_recv()
            vec[4] = vec[3] + vec_got[3]
            vec_copy(4, z_out).start()
            vec_out[...] = vec[4]

        @pl.when(jnp.logical_and(t == 5, outer))
        def _():
            vec_copy(3, z_mid).wait_recv()
            vec_out[...] = vec_got[3]

        @pl.when(t < sets)
        def _():
            @pl.when(t % SETS == 0)
            def _():
                m = t // SETS
                core_copy(m).wait_recv()
                for r in range(3):
                    rows = pl.ds(r * (width // 3), width // 3)
                    add(part.at[m, core, rows], core_in.at[m, rows])

            for d in range(2):
                y_copy(t, d).start()

                @pl.when(hop[d] == 0)
                def _():
                    pair_copy(t, d).start()

        def during(k, more=True):
            return jnp.logical_and(jnp.logical_and(k >= 0, k < sets), more)

        k = t - 1

        @pl.when(during(k))
        def _():
            for d in range(2):
                y_copy(k, d).wait_recv()
                add(mine(k, d, y), y_in.at[k, d])

                @pl.when(hop[d] == 0)
                def _():
                    one_copy(k, d).start()

        for d in range(2):
            k = t - 1 - HOP_LAG * hop[d]

            @pl.when(during(k, hop[d] > 0))
            def _():
                pair_copy(k, d).wait_recv()
                add(mine(k, d, 2, 2), chain_pair.at[k, d])

                @pl.when(hop[d] < last)
                def _():
                    pair_copy(k, d).start()

                @pl.when(hop[d] == last)
                def _():
                    end_copy(k, d).start()

                one_copy(k, d).wait_recv()
                add(mine(k, d, y), chain_one.at[k, d])

                @pl.when(hop[d] < last)
                def _():
                    one_copy(k, d).start()

        base = 2 + HOP_LAG * last
        for d in range(2):
            k = t - base

            @pl.when(during(k, hop[d] == last))
            def _():
                spread_z(k, d, y, 0, mine(k, d, y)).start()
                spread_y(k, d, y, 0, mine(k, d, y)).start()
                keep_copy(k, d, y, 0).start()
                end_copy(k, d).wait_recv()
                add(mine(k, d, 2 + y), end_in.at[k])
                spread_y(k, d, 2 + y, 1, mine(k, d, 2 + y)).start()
                spread_z(k, d, 2 + y, 1 + y, mine(k, d, 2 + y)).start()
                keep_copy(k, d, 2 + y, 1).start()

            k2 = t - base - 1

            @pl.when(during(k2, hop[d] == last))
            def _():
                arrived(k2, d, 3 - y)
                spread_z(k2, d, 3 - y, 2 - y, final(k2, d, 3 - y)).start()

            k3 = t - base - HOP_LAG * (last - hop[d])

            @pl.when(during(k3, hop[d] < last))
            def _():
                for i, b in ((0, y), (1, 2), (2, 3)):
                    arrived(k3, d, b)

                    @pl.when(hop[d] > 0)
                    def _():
                        spread_z(k3, d, b, i, final(k3, d, b)).start()

                    if i == 0:
                        spread_y(k3, d, b, 0, final(k3, d, b)).start()

            k4 = k3 - 1

            @pl.when(during(k4))
            def _():
                arrived(k4, d, 1 - y)

                @pl.when(hop[d] == last)
                def _():
                    keep_copy(k4, d, y, 0).wait()
                    keep_copy(k4, d, 2 + y, 1).wait()

                out_copy(k4, d).start()

        return 0

    ticks = sets + 2 + HOP_LAG * last + HOP_LAG * last + 1
    lax.fori_loop(0, ticks, tick, 0)

    def settle(k, _):
        for d in range(2):
            y_copy(k, d).wait_send()
            out_copy(k, d).wait()
            spread_y(k, d, y, 0, final(k, d, y)).wait_send()

            @pl.when(hop[d] < last)
            def _():
                pair_copy(k, d).wait_send()
                one_copy(k, d).wait_send()

            @pl.when(hop[d] == last)
            def _():
                end_copy(k, d).wait_send()
                spread_y(k, d, 2 + y, 1, final(k, d, 2 + y)).wait_send()

            @pl.when(hop[d] > 0)
            def _():
                for i, b in ((0, y), (1, 2), (2, 3)):
                    spread_z(k, d, b, i, final(k, d, b)).wait_send()

        return 0

    lax.fori_loop(0, sets, settle, 0)

    def settle_core(m, _):
        core_copy(m).wait_send()
        return 0

    lax.fori_loop(0, duos, settle_core, 0)
    for i in range(3):
        vec_copy(i, core_peer).wait_send()

    @pl.when(jnp.logical_not(outer))
    def _():
        vec_copy(3, z_mid).wait_send()
        vec_copy(4, z_out).wait_send()


def reduce_gradients(factors, vectors):
    rows, width = factors[0].shape
    hidden = factors[3].shape[1]
    blocks = 4 + 2 * (hidden // width)
    duos = blocks // 2
    sets = duos * SETS
    piece = width // SETS // 8
    any_space = pl.BlockSpec(memory_space=pl.ANY)
    vmem = pl.BlockSpec(memory_space=pltpu.VMEM)
    low = lambda *shape: pltpu.VMEM(shape, BF16)
    dma = lambda *shape: pltpu.SemaphoreType.DMA(shape)
    return pl.pallas_call(
        gradient_kernel,
        out_shape=[
            jax.ShapeDtypeStruct((blocks, width, width), BF16),
            jax.ShapeDtypeStruct(vectors.shape, F32),
        ],
        in_specs=[any_space] * 8 + [vmem],
        out_specs=[any_space, vmem],
        scratch_shapes=[low(*factor.shape) for factor in factors]
        + [
            low(duos, 2, width, width), low(duos, width, width),
            low(sets, 2, 2 * piece, width), low(sets, 2, piece, width),
            low(sets, 2, piece, width), low(sets, piece, width),
            pltpu.VMEM((5,) + vectors.shape, F32), pltpu.VMEM((4,) + vectors.shape, F32),
            dma(8), dma(duos), dma(duos), dma(sets, 2), dma(sets, 2), dma(sets, 2), dma(sets, 2),
            dma(sets, 2), dma(sets, 2), dma(sets), dma(sets),
            dma(sets, 2, 4), dma(sets, 2, 3), dma(sets, 2, 2), dma(sets, 2, 2), dma(sets, 2),
            dma(sets, 2), dma(5), dma(4),
        ],
        compiler_params=pltpu.CompilerParams(
            collective_id=1, has_side_effects=True, vmem_limit_bytes=VMEM_BYTES
        ),
        name="gradients",
    )(*factors, vectors)


def shards(
    boundary, inward, inbias, outward, outbias, normgain, normshift, expand, expbias,
    shrink, shrbias, lastgain, lastshift,
):
    width = outward.shape[-1]
    hidden = expand.shape[-1]
    slabs = hidden // width
    outs = run_layer(
        boundary[0],
        (inward[0], outward[0], expand[0], shrink[0]),
        (inbias, outbias, normgain, normshift, expbias, shrbias, lastgain, lastshift),
    )
    results, factors, vectors = outs[0], outs[1:9], outs[9]
    if lax.axis_size("dp") == 4 * LANES_Z:
        total, vec = reduce_gradients(factors, vectors)

        def beside(blocks):
            return jnp.concatenate([block.astype(F32) for block in blocks], axis=1)

        shrink_grad = total[:slabs].reshape(hidden, width).astype(F32)
        expand_grad = beside([total[slabs + i] for i in range(slabs)])
        outward_grad = total[2 * slabs].astype(F32)
        inward_grad = beside([total[2 * slabs + 1 + i] for i in range(3)])
    else:
        f_x, f_a, f_h, f_g, f_p, f_o, f_u, f_f = factors

        def summed(left, right):
            grad = dot_tn(left, right).astype(BF16)
            mine = lax.psum_scatter(grad, "dp", scatter_dimension=0, tiled=True)
            return lax.all_gather(mine, "dp", axis=0, tiled=True).astype(F32)

        inward_grad, outward_grad = summed(f_x, f_p), summed(f_a, f_o)
        expand_grad, shrink_grad = summed(f_h, f_u), summed(f_g, f_f)
        vec = lax.psum(vectors, "dp")

    def piece(start, count):
        return vec[start : start + count].reshape(1, count * width)

    return (
        results[None],
        inward_grad[None], piece(0, 3),
        outward_grad[None], piece(3, 1), piece(4, 1), piece(5, 1),
        expand_grad[None], piece(6, slabs),
        shrink_grad[None], piece(6 + slabs, 1), piece(7 + slabs, 1), piece(8 + slabs, 1),
    )


def solution(mesh):
    matrix, vector = P("section", None, None), P("section", None)
    params = (
        matrix, vector, matrix, vector, vector, vector, matrix, vector, matrix, vector,
        vector, vector,
    )
    specs = (P("section", "dp", None),) + params
    return jax.shard_map(shards, mesh=mesh, in_specs=specs, out_specs=specs, check_vma=False)
```

```python
from functools import partial
import math

import jax
import jax.numpy as jnp
import numpy as np
from jax import lax
from jax.experimental import pallas as pl
from jax.experimental.pallas import tpu as pltpu
from jax.sharding import PartitionSpec as P

HEAD = 64
SEQ = 512
CHUNK = 256
PAIR = 2 * HEAD
EPSILON = 1e-05
MESH = pl.DeviceIdType.MESH
F32 = jnp.float32
BF16 = jnp.bfloat16
VMEM_BYTES = 63 * 2**20


def dot(a, b):
    return jnp.dot(a, b, preferred_element_type=F32)


def dot_nt(a, b):
    return lax.dot_general(a, b, (((1,), (1,)), ((), ())), preferred_element_type=F32)


def dot_tn(a, b):
    return lax.dot_general(a, b, (((0,), (0,)), ((), ())), preferred_element_type=F32)


def softplus(p):
    return jnp.maximum(p, 0.0) + jnp.log1p(jnp.exp(-jnp.abs(p)))


def sigmoid_of_softplus(q):
    series = q * (1.0 - q * (0.5 - q * (1.0 / 6.0 - q * (1.0 / 24.0))))
    return jnp.where(q < 0.03, series, 1.0 - jnp.exp(-q))


def cosine_tables():
    step = math.pi / (2.0 * SEQ)
    i = np.arange(CHUNK)[:, None]
    j = np.arange(CHUNK)[None, :]
    near = np.where(i >= j, np.cos((i - j) * step), 0.0).astype(np.float32)
    far = np.cos((i - j + CHUNK) * step).astype(np.float32)
    return near, far


def lane_masks():
    lanes = np.arange(PAIR)
    return np.stack([lanes < HEAD, lanes >= HEAD])[:, None, :].astype(np.float32)


def layer_kernel(
    boundary, inward, outward, expand, shrink,
    inbias, outbias, normgain, normshift, expbias, shrbias, lastgain, lastshift,
    near, far, masks,
    results, f_x, f_a, f_h, f_g, f_p, f_o, f_u, f_f, vector_rows,
    win, wout, wexp, wshr,
    xs, qkv, att, low, zin, hbs, gs, gps, n1s, n2s, s1s, s2s, dys, ybuf, xbuf,
    acc, keep, das, carry, vectors,
    load_sems, out_sems, res_sems, fwd_send, fwd_recv, bwd_send, bwd_recv,
):
    rows_all, width = xs.shape
    hidden = wexp.shape[1]
    chunks = rows_all // CHUNK
    pairs = width // PAIR
    slabs = hidden // width
    section = lax.axis_index("section")
    first = section == 0
    peer = {"section": 1 - section}

    loads = [
        pltpu.make_async_copy(src, dst, load_sems.at[i])
        for i, (src, dst) in enumerate(
            [(inward, win), (outward, wout), (expand, wexp), (shrink, wshr)]
        )
    ]
    load_x = pltpu.make_async_copy(boundary, xs, load_sems.at[4])
    load_y = pltpu.make_async_copy(boundary, dys, load_sems.at[4])

    loads[0].start()

    @pl.when(first)
    def _():
        load_x.start()

    @pl.when(jnp.logical_not(first))
    def _():
        load_y.start()

    barrier = pltpu.get_barrier_semaphore()
    pl.semaphore_signal(barrier, inc=1, device_id=peer, device_id_type=MESH)
    vectors[...] = jnp.zeros_like(vectors)
    pl.semaphore_wait(barrier, 1)

    def rows_of(c):
        return pl.ds(pl.multiple_of(c * CHUNK, CHUNK), CHUNK)

    def send_forward(c):
        return pltpu.make_async_remote_copy(
            src_ref=ybuf.at[rows_of(c)], dst_ref=xs.at[rows_of(c)],
            send_sem=fwd_send.at[c], recv_sem=fwd_recv.at[c],
            device_id=peer, device_id_type=MESH,
        )

    def send_backward(c):
        return pltpu.make_async_remote_copy(
            src_ref=xbuf.at[rows_of(c)], dst_ref=dys.at[rows_of(c)],
            send_sem=bwd_send.at[c], recv_sem=bwd_recv.at[c],
            device_id=peer, device_id_type=MESH,
        )

    def result_copy(buf, c):
        return pltpu.make_async_copy(buf.at[rows_of(c)], results.at[rows_of(c)], res_sems.at[c])

    early = [(xs, f_x), (att, f_a), (hbs, f_h), (gs, f_g)]
    late = [(qkv, f_p), (n1s, f_o), (gps, f_u), (n2s, f_f)]

    def factor_copies(c, which, base):
        return [
            pltpu.make_async_copy(src.at[rows_of(c)], dst.at[rows_of(c)], out_sems.at[c, base + i])
            for i, (src, dst) in enumerate(which)
        ]

    def column_sum(at, value):
        vectors[at] += jnp.sum(value, axis=0, keepdims=True)

    def norm_forward(e):
        mean = jnp.mean(e, axis=-1, keepdims=True)
        center = e - mean
        s = lax.rsqrt(jnp.mean(center * center, axis=-1, keepdims=True) + EPSILON)
        return center * s, s

    def norm_backward(dn, n, s):
        m1 = jnp.mean(dn, axis=-1, keepdims=True)
        m2 = jnp.mean(dn * n, axis=-1, keepdims=True)
        return s * (dn - m1 - n * m2)

    def pair_columns(hp):
        return [pl.ds(pl.multiple_of(i * width + hp * PAIR, PAIR), PAIR) for i in range(3)]

    def attend(c, wide):
        rows = rows_of(c)
        tiles = [(rows, near)] + ([(rows_of(c - 1), far)] if wide else [])
        m = [masks[a].astype(BF16) for a in range(2)]

        def one_pair(hp, _):
            cq, ck, cv = pair_columns(hp)
            q = qkv[rows, cq]
            nz = None
            for key_rows, weights in tiles:
                k, v = qkv[key_rows, ck], qkv[key_rows, cv]
                for a in range(2):
                    s = (dot_nt(q * m[a], k) * weights[...]).astype(BF16)
                    right = jnp.concatenate(
                        [v * m[a], jnp.broadcast_to(m[a], v.shape)], axis=1
                    )
                    part = dot(s, right)
                    nz = part if nz is None else nz + part
            inverse = 1.0 / nz[:, PAIR:]
            a_full = nz[:, :PAIR] * inverse
            a_high = a_full.astype(BF16)
            att[rows, cq] = a_high
            low[rows, cq] = (a_full - a_high.astype(F32)).astype(BF16)
            zin[rows, cq] = inverse.astype(BF16)
            return 0

        lax.fori_loop(0, pairs, one_pair, 0, unroll=True)

    def attend_backward(c, wide):
        rows = rows_of(c)
        m = [masks[a].astype(BF16) for a in range(2)]

        def one_pair(hp, _):
            cq, ck, cv = pair_columns(hp)
            q, k, v = qkv[rows, cq], qkv[rows, ck], qkv[rows, cv]
            dn = (das[:, cq].astype(F32) * zin[rows, cq].astype(F32)).astype(BF16)
            prod = dn.astype(F32) * (att[rows, cq].astype(F32) + low[rows, cq].astype(F32))
            dz = [-jnp.sum(prod * masks[a], axis=-1, keepdims=True) for a in range(2)]
            qm = [q * m[a] for a in range(2)]
            dnm = [dn * m[a] for a in range(2)]

            def tile(kt, vt, weights):
                dq = dk = dv = None
                for a in range(2):
                    w = weights[...]
                    s = (dot_nt(qm[a], kt) * w).astype(BF16)
                    ds = ((dot_nt(dnm[a], vt) + dz[a]) * w).astype(BF16)
                    parts = (dot(ds, kt * m[a]), dot_tn(ds, qm[a]), dot_tn(s, dnm[a]))
                    dq, dk, dv = parts if a == 0 else (
                        dq + parts[0], dk + parts[1], dv + parts[2]
                    )
                return dq, dk, dv

            dq, dk, dv = tile(k, v, near)
            wide_cols = [pl.ds(pl.multiple_of(i * width + hp * PAIR, PAIR), PAIR) for i in range(2)]
            if wide:
                kp, vp = qkv[rows_of(c - 1), ck], qkv[rows_of(c - 1), cv]
                dqp, dkp, dvp = tile(kp, vp, far)
                dq = dq + dqp
                carry[:, wide_cols[0]] = dkp
                carry[:, wide_cols[1]] = dvp
            else:
                dk = dk + carry[:, wide_cols[0]]
                dv = dv + carry[:, wide_cols[1]]
            qkv[rows, cq] = (dq * sigmoid_of_softplus(q.astype(F32))).astype(BF16)
            qkv[rows, ck] = (dk * sigmoid_of_softplus(k.astype(F32))).astype(BF16)
            qkv[rows, cv] = dv.astype(BF16)
            return 0

        lax.fori_loop(0, pairs, one_pair, 0, unroll=True)

    def forward(c, begins):
        rows = rows_of(c)

        @pl.when(begins)
        def _():
            loads[0].wait()

            @pl.when(first)
            def _():
                load_x.wait()

            for load in loads[1:]:
                load.start()

        @pl.when(jnp.logical_not(first))
        def _():
            send_forward(c).wait_recv()

        for i in range(3):
            cols = slice(i * width, (i + 1) * width)
            p = dot(xs[rows, :], win[:, cols]) + inbias[:, cols]
            qkv[rows, cols] = (softplus(p) if i < 2 else p).astype(BF16)

        @pl.when(c % 2 == 0)
        def _():
            attend(c, False)

        @pl.when(c % 2 == 1)
        def _():
            attend(c, True)

        @pl.when(begins)
        def _():
            for load in loads[1:]:
                load.wait()

        e = xs[rows, :].astype(F32) + (dot(att[rows, :], wout[...]) + outbias[...])
        n1, s1 = norm_forward(e)
        n1s[rows, :] = n1.astype(BF16)
        s1s[rows, :] = s1
        h = n1 * normgain[...] + normshift[...]
        hbs[rows, :] = h.astype(BF16)
        acc[...] = h + shrbias[...]
        for i in range(slabs):
            cols = slice(i * width, (i + 1) * width)
            u = dot(hbs[rows, :], wexp[:, cols]) + expbias[:, cols]
            phi = 0.5 * (1.0 + lax.erf(u * math.sqrt(0.5)))
            g = (u * phi).astype(BF16)
            gs[rows, cols] = g
            gps[rows, cols] = (
                phi + u * (jnp.exp(u * u * -0.5) * (1.0 / math.sqrt(2.0 * math.pi)))
            ).astype(BF16)
            acc[...] += dot(g, wshr[cols, :])
        n2, s2 = norm_forward(acc[...])
        n2s[rows, :] = n2.astype(BF16)
        s2s[rows, :] = s2
        ybuf[rows, :] = (n2 * lastgain[...] + lastshift[...]).astype(BF16)

        @pl.when(first)
        def _():
            send_forward(c).start()

        @pl.when(jnp.logical_not(first))
        def _():
            result_copy(ybuf, c).start()

        for copy in factor_copies(c, early, 0):
            copy.start()

    def backward(c):
        rows = rows_of(c)

        @pl.when(first)
        def _():
            send_backward(c).wait_recv()

        @pl.when(jnp.logical_and(jnp.logical_not(first), c == 1))
        def _():
            load_y.wait()

        dy = dys[rows, :].astype(F32)
        n2 = n2s[rows, :].astype(F32)
        column_sum(7 + slabs, dy * n2)
        column_sum(8 + slabs, dy)
        dr = norm_backward(dy * lastgain[...], n2, s2s[rows, :])
        df = dr.astype(BF16)
        n2s[rows, :] = df
        column_sum(6 + slabs, df.astype(F32))
        acc[...] = dr
        for i in range(slabs):
            cols = slice(i * width, (i + 1) * width)
            dg = dot_nt(n2s[rows, :], wshr[cols, :])
            du = (dg * gps[rows, cols].astype(F32)).astype(BF16)
            gps[rows, cols] = du
            column_sum(6 + i, du.astype(F32))
            acc[...] += dot_nt(du, wexp[:, cols])
        dh = acc[...]
        n1 = n1s[rows, :].astype(F32)
        column_sum(4, dh * n1)
        column_sum(5, dh)
        de = norm_backward(dh * normgain[...], n1, s1s[rows, :])
        keep[...] = de
        do = de.astype(BF16)
        n1s[rows, :] = do
        column_sum(3, do.astype(F32))
        das[...] = dot_nt(do, wout[...]).astype(BF16)

        @pl.when(c % 2 == 0)
        def _():
            attend_backward(c, False)

        @pl.when(c % 2 == 1)
        def _():
            attend_backward(c, True)

        for i in range(3):
            column_sum(i, qkv[rows, i * width : (i + 1) * width].astype(F32))
        dx = keep[...] + dot_nt(qkv[rows, :], win[...])
        xbuf[rows, :] = dx.astype(BF16)

        @pl.when(first)
        def _():
            result_copy(xbuf, c).start()

        @pl.when(jnp.logical_not(first))
        def _():
            send_backward(c).start()

        for copy in factor_copies(c, late, 4):
            copy.start()

    def step(t, _):
        group, place = t // 4, t % 4
        ahead = jnp.where(first, t < chunks, place < 2)
        c_forward = jnp.where(first, t, 2 * group + place)
        back = t - chunks
        c_backward = jnp.where(first, 2 * (back // 2) + 1 - back % 2, 2 * group + 3 - place)

        @pl.when(ahead)
        def _():
            forward(c_forward, t == 0)

        @pl.when(jnp.logical_not(ahead))
        def _():
            backward(c_backward)

        return 0

    lax.fori_loop(0, 2 * chunks, step, 0)
    for i in range(vectors.shape[0]):
        vector_rows[i : i + 1, :] = vectors[i]

    def finish(c, _):
        @pl.when(first)
        def _():
            send_forward(c).wait_send()
            result_copy(xbuf, c).wait()

        @pl.when(jnp.logical_not(first))
        def _():
            send_backward(c).wait_send()
            result_copy(ybuf, c).wait()

        for copy in factor_copies(c, early, 0) + factor_copies(c, late, 4):
            copy.wait()
        return 0

    lax.fori_loop(0, chunks, finish, 0)


def run_layer(boundary, weights, biases):
    rows, width = boundary.shape
    hidden = weights[2].shape[1]
    chunks = rows // CHUNK
    near, far = cosine_tables()
    masks = lane_masks()
    slabs = hidden // width
    any_space = pl.BlockSpec(memory_space=pl.ANY)
    vmem = pl.BlockSpec(memory_space=pltpu.VMEM)
    out_widths = [width] * 4 + [hidden, 3 * width, width, hidden, width]
    out_shape = [jax.ShapeDtypeStruct((rows, w), BF16) for w in out_widths]
    vector_count = -(-(9 + slabs) // 8) * 8
    out_shape.append(jax.ShapeDtypeStruct((vector_count, width), F32))
    low = lambda *shape: pltpu.VMEM(shape, BF16)
    wide = lambda *shape: pltpu.VMEM(shape, F32)
    dma = pltpu.SemaphoreType.DMA
    return pl.pallas_call(
        layer_kernel,
        out_shape=out_shape,
        in_specs=[any_space] * 5 + [vmem] * 11,
        out_specs=[any_space] * 9 + [vmem],
        scratch_shapes=[
            low(width, 3 * width), low(width, width), low(width, hidden), low(hidden, width),
            low(rows, width), low(rows, 3 * width), low(rows, width), low(rows, width),
            low(rows, width), low(rows, width), low(rows, hidden), low(rows, hidden),
            low(rows, width), low(rows, width), wide(rows, 1), wide(rows, 1),
            low(rows, width), low(rows, width), low(rows, width),
            wide(CHUNK, width), wide(CHUNK, width), low(CHUNK, width), wide(CHUNK, 2 * width),
            wide(vector_count, 1, width),
            dma((5,)), dma((chunks, 8)), dma((chunks,)), dma((chunks,)), dma((chunks,)),
            dma((chunks,)), dma((chunks,)),
        ],
        compiler_params=pltpu.CompilerParams(
            collective_id=0, has_side_effects=True, vmem_limit_bytes=VMEM_BYTES
        ),
        name="layer",
    )(boundary, *weights, *biases, jnp.asarray(near), jnp.asarray(far), jnp.asarray(masks))


SETS = 2
LANES_Z = 4

ARRIVE_Y = 2
PAIR_AT = (0, 2, 3, 13)
ONE_AT = (0, 3, 4, 17)
LAST_ONE, LAST_PAIR, LAST_CROSS = 21, 20, 21
BACK_AT = (0, 20, 21, 24)
OUT_AT = (22, 22, 22, 25)


def gradient_kernel(
    f_x, f_a, f_h, f_g, f_p, f_o, f_u, f_f, vec_in,
    total, vec_out,
    x, a, h, g, p, o, u, f,
    part, core_in, chain_pair, chain_one, y_in, end_in, vec, vec_got,
    load_sems, core_s, core_r, y_s, y_r, pair_s, pair_r, one_s, one_r, end_s, end_r,
    got, z_s, yy_s, kept, out_s, out_r, vec_s, vec_r,
):
    width = x.shape[1]
    slabs = g.shape[1] // width
    me = lax.axis_index("dp")
    core, y, z = me % 2, (me // 2) % 2, me // 4
    last = LANES_Z - 1
    core_peer, y_peer = {"dp": me + 1 - 2 * core}, {"dp": me + 2 - 4 * y}
    hop = [last - z, z]
    ahead = [{"dp": me - 4}, {"dp": me + 4}]
    behind = [ahead[1], ahead[0]]

    blocks = (
        [(a, 0, o, 0)]
        + [(x, 0, p, i) for i in range(3)]
        + [(h, 0, u, i) for i in range(slabs)]
        + [(g, i, f, 0) for i in range(slabs)]
    )
    duos = len(blocks) // 2
    sets = duos * SETS
    set_rows = width // SETS
    half = set_rows // 2
    piece = half // 4

    sources = [(f_a, a), (f_o, o), (f_x, x), (f_p, p), (f_h, h), (f_u, u), (f_f, f), (f_g, g)]
    loads = [
        pltpu.make_async_copy(src, dst, load_sems.at[i]) for i, (src, dst) in enumerate(sources)
    ]
    load_at = {0: (0, 1, 2, 3), 2 * SETS: (4, 5), (2 + slabs // 2) * SETS: (6, 7)}
    for load in loads[:4]:
        load.start()

    barrier = pltpu.get_barrier_semaphore()
    for peer in (core_peer, y_peer):
        pl.semaphore_signal(barrier, inc=1, device_id=peer, device_id_type=MESH)
    for d in range(2):
        @pl.when(hop[d] < last)
        def _():
            pl.semaphore_signal(barrier, inc=1, device_id=ahead[d], device_id_type=MESH)
    pl.semaphore_wait(barrier, jnp.where(jnp.logical_and(z > 0, z < last), 4, 3))

    def remote(src, dst, send, recv, peer):
        return pltpu.make_async_remote_copy(
            src_ref=src, dst_ref=dst, send_sem=send, recv_sem=recv,
            device_id=peer, device_id_type=MESH,
        )

    def span(k, d, first, count):
        start = (k % SETS) * set_rows + d * half + first * piece
        return pl.ds(pl.multiple_of(start, 16), count * piece)

    def mine(k, d, first, count=1):
        return part.at[k // SETS, core, span(k, d, first, count)]

    def final(k, d, first, count=1):
        return total.at[2 * (k // SETS) + core, span(k, d, first, count)]

    def add(dst, src):
        dst[...] = (dst[...].astype(F32) + src[...].astype(F32)).astype(BF16)

    def core_copy(k):
        rows = pl.ds(pl.multiple_of((k % SETS) * set_rows, set_rows), set_rows)
        return remote(
            part.at[k // SETS, 1 - core, rows], core_in.at[k], core_s.at[k], core_r.at[k], core_peer
        )

    def y_copy(k, d):
        return remote(mine(k, d, 1 - y), y_in.at[k, d], y_s.at[k, d], y_r.at[k, d], y_peer)

    def pair_copy(k, d):
        return remote(
            mine(k, d, 2, 2), chain_pair.at[k, d], pair_s.at[k, d], pair_r.at[k, d], ahead[d]
        )

    def one_copy(k, d):
        return remote(mine(k, d, y), chain_one.at[k, d], one_s.at[k, d], one_r.at[k, d], ahead[d])

    def end_copy(k, d):
        return remote(mine(k, d, 3 - y), end_in.at[k], end_s.at[k], end_r.at[k], y_peer)

    def spread_z(k, d, b, i, src):
        return remote(src, final(k, d, b), z_s.at[k, d, i], got.at[k, d, b], behind[d])

    def spread_y(k, d, b, i, src):
        return remote(src, final(k, d, b), yy_s.at[k, d, i], got.at[k, d, b], y_peer)

    def keep_copy(k, d, b, i):
        return pltpu.make_async_copy(mine(k, d, b), final(k, d, b), kept.at[k, d, i])

    def out_copy(k, d):
        return remote(
            final(k, d, 0, 4), final(k, d, 0, 4), out_s.at[k, d], out_r.at[k, d], core_peer
        )

    def arrived(k, d, b):
        spread_z(k, d, b, 0, final(k, d, b)).wait_recv()

    outer = jnp.logical_or(z == 0, z == last)
    z_pair = {"dp": me + 4 - 8 * (z % 2)}
    z_mid = {"dp": jnp.where(z == 1, me + 4, me - 4)}
    z_out = {"dp": jnp.where(z == 1, me - 4, me + 4)}

    def vec_copy(i, peer):
        return remote(vec.at[i], vec_got.at[min(i, 3)], vec_s.at[i], vec_r.at[min(i, 3)], peer)

    def compute(k):
        for i in load_at.get(k, ()):
            loads[i].wait()
        m, at = k // SETS, (k % SETS) * set_rows
        for side in range(2):
            left, i, right, j = blocks[2 * m + side]
            cols = slice(i * width + at, i * width + at + set_rows)
            part[m, side, at : at + set_rows, :] = dot_tn(
                left[:, cols], right[:, j * width : (j + 1) * width]
            ).astype(BF16)
        core_copy(k).start()

    vec[0] = vec_in[...]
    vec_copy(0, core_peer).start()
    compute(0)
    for load in loads[4:]:
        load.start()

    def feed(t):
        for k in range(1, sets):
            @pl.when(t == k - 1)
            def _():
                compute(k)

        for i, peer in ((1, y_peer), (2, z_pair)):
            @pl.when(t == i)
            def _():
                vec_copy(i - 1, peer).wait_recv()
                vec[i] = vec[i - 1] + vec_got[i - 1]
                vec_copy(i, peer).start()

        @pl.when(t == 3)
        def _():
            vec_copy(2, z_pair).wait_recv()
            vec[3] = vec[2] + vec_got[2]

            @pl.when(jnp.logical_not(outer))
            def _():
                vec_copy(3, z_mid).start()

        @pl.when(jnp.logical_and(t == 4, jnp.logical_not(outer)))
        def _():
            vec_copy(3, z_mid).wait_recv()
            vec[4] = vec[3] + vec_got[3]
            vec_copy(4, z_out).start()
            vec_out[...] = vec[4]

        @pl.when(jnp.logical_and(t == 5, outer))
        def _():
            vec_copy(3, z_mid).wait_recv()
            vec_out[...] = vec_got[3]

        @pl.when(t < sets)
        def _():
            core_copy(t).wait_recv()
            for d in range(2):
                add(mine(t, d, 0, 4), core_in.at[t, pl.ds(d * half, half)])
                y_copy(t, d).start()

                @pl.when(hop[d] == 0)
                def _():
                    pair_copy(t, d).start()

    def during(k, more=True):
        return jnp.logical_and(jnp.logical_and(k >= 0, k < sets), more)

    def by_place(place, offsets):
        out = jnp.int32(offsets[0])
        for i, offset in enumerate(offsets[1:], 1):
            out = jnp.where(place == i, offset, out)
        return out

    def arrive_y(t):
        k = t - ARRIVE_Y

        @pl.when(during(k))
        def _():
            for d in range(2):
                y_copy(k, d).wait_recv()
                add(mine(k, d, y), y_in.at[k, d])

                @pl.when(hop[d] == 0)
                def _():
                    one_copy(k, d).start()

    def hop_pair(t):
        for d in range(2):
            k = t - by_place(hop[d], PAIR_AT)

            @pl.when(during(k, hop[d] > 0))
            def _():
                pair_copy(k, d).wait_recv()
                add(mine(k, d, 2, 2), chain_pair.at[k, d])

                @pl.when(hop[d] < last)
                def _():
                    pair_copy(k, d).start()

                @pl.when(hop[d] == last)
                def _():
                    end_copy(k, d).start()

    def hop_one(t):
        for d in range(2):
            k = t - by_place(hop[d], ONE_AT)

            @pl.when(during(k, hop[d] > 0))
            def _():
                one_copy(k, d).wait_recv()
                add(mine(k, d, y), chain_one.at[k, d])

                @pl.when(hop[d] < last)
                def _():
                    one_copy(k, d).start()

    def last_one(t):
        k = t - LAST_ONE
        for d in range(2):
            @pl.when(during(k, hop[d] == last))
            def _():
                spread_z(k, d, y, 0, mine(k, d, y)).start()
                spread_y(k, d, y, 0, mine(k, d, y)).start()
                keep_copy(k, d, y, 0).start()

    def last_pair(t):
        k = t - LAST_PAIR
        for d in range(2):
            @pl.when(during(k, hop[d] == last))
            def _():
                end_copy(k, d).wait_recv()
                add(mine(k, d, 2 + y), end_in.at[k])
                spread_y(k, d, 2 + y, 1, mine(k, d, 2 + y)).start()
                spread_z(k, d, 2 + y, 1 + y, mine(k, d, 2 + y)).start()
                keep_copy(k, d, 2 + y, 1).start()

    def last_cross(t):
        k = t - LAST_CROSS
        for d in range(2):
            @pl.when(during(k, hop[d] == last))
            def _():
                arrived(k, d, 3 - y)
                spread_z(k, d, 3 - y, 2 - y, final(k, d, 3 - y)).start()

    def way_back(t):
        for d in range(2):
            k = t - by_place(last - hop[d], BACK_AT)

            @pl.when(during(k, hop[d] < last))
            def _():
                for i, b in ((0, y), (1, 2), (2, 3)):
                    arrived(k, d, b)

                    @pl.when(hop[d] > 0)
                    def _():
                        spread_z(k, d, b, i, final(k, d, b)).start()

                    if i == 0:
                        spread_y(k, d, b, 0, final(k, d, b)).start()

    def to_core(t):
        for d in range(2):
            k = t - by_place(last - hop[d], OUT_AT)

            @pl.when(during(k))
            def _():
                arrived(k, d, 1 - y)

                @pl.when(hop[d] == last)
                def _():
                    keep_copy(k, d, y, 0).wait()
                    keep_copy(k, d, 2 + y, 1).wait()

                out_copy(k, d).start()

    def tick(t, _):
        for stage in (
            last_one, hop_one, arrive_y, hop_pair, to_core, last_cross, feed, last_pair, way_back
        ):
            stage(t)
        return 0

    lax.fori_loop(0, sets + max(OUT_AT), tick, 0)

    def settle(k, _):
        core_copy(k).wait_send()
        for d in range(2):
            y_copy(k, d).wait_send()
            out_copy(k, d).wait()
            spread_y(k, d, y, 0, final(k, d, y)).wait_send()

            @pl.when(hop[d] < last)
            def _():
                pair_copy(k, d).wait_send()
                one_copy(k, d).wait_send()

            @pl.when(hop[d] == last)
            def _():
                end_copy(k, d).wait_send()
                spread_y(k, d, 2 + y, 1, final(k, d, 2 + y)).wait_send()

            @pl.when(hop[d] > 0)
            def _():
                for i, b in ((0, y), (1, 2), (2, 3)):
                    spread_z(k, d, b, i, final(k, d, b)).wait_send()

        return 0

    lax.fori_loop(0, sets, settle, 0)

    for i in range(3):
        vec_copy(i, core_peer).wait_send()

    @pl.when(jnp.logical_not(outer))
    def _():
        vec_copy(3, z_mid).wait_send()
        vec_copy(4, z_out).wait_send()


def reduce_gradients(factors, vectors):
    rows, width = factors[0].shape
    hidden = factors[3].shape[1]
    blocks = 4 + 2 * (hidden // width)
    duos = blocks // 2
    sets = duos * SETS
    piece = width // SETS // 8
    any_space = pl.BlockSpec(memory_space=pl.ANY)
    vmem = pl.BlockSpec(memory_space=pltpu.VMEM)
    low = lambda *shape: pltpu.VMEM(shape, BF16)
    dma = lambda *shape: pltpu.SemaphoreType.DMA(shape)
    return pl.pallas_call(
        gradient_kernel,
        out_shape=[
            jax.ShapeDtypeStruct((blocks, width, width), BF16),
            jax.ShapeDtypeStruct(vectors.shape, F32),
        ],
        in_specs=[any_space] * 8 + [vmem],
        out_specs=[any_space, vmem],
        scratch_shapes=[low(*factor.shape) for factor in factors]
        + [
            low(duos, 2, width, width), low(sets, width // SETS, width),
            low(sets, 2, 2 * piece, width), low(sets, 2, piece, width),
            low(sets, 2, piece, width), low(sets, piece, width),
            pltpu.VMEM((5,) + vectors.shape, F32), pltpu.VMEM((4,) + vectors.shape, F32),
            dma(8), dma(sets), dma(sets), dma(sets, 2), dma(sets, 2), dma(sets, 2), dma(sets, 2),
            dma(sets, 2), dma(sets, 2), dma(sets), dma(sets),
            dma(sets, 2, 4), dma(sets, 2, 3), dma(sets, 2, 2), dma(sets, 2, 2), dma(sets, 2),
            dma(sets, 2), dma(5), dma(4),
        ],
        compiler_params=pltpu.CompilerParams(
            collective_id=1, has_side_effects=True, vmem_limit_bytes=VMEM_BYTES
        ),
        name="gradients",
    )(*factors, vectors)


def widen_kernel(slabs, total, vec, *outs):
    step = pl.program_id(0)
    inward, outward, expand, shrink = outs[:4]
    ends = (1, 4, 4 + slabs, 4 + 2 * slabs)
    for first, end, out in zip((0,) + ends, ends, (outward, inward, expand, shrink)):
        @pl.when(jnp.logical_and(step >= first, step < end))
        def _():
            out[...] = total[0].astype(F32)

    @pl.when(step == 0)
    def _():
        width = vec.shape[1]
        row = 0
        for out in outs[4:]:
            for i in range(out.shape[1] // width):
                out[:, i * width : (i + 1) * width] = vec[row : row + 1, :]
                row += 1


def widen(total, vec, hidden):
    blocks, width, _ = total.shape
    slabs = hidden // width
    tall = width // 2
    clipped = lambda i, first, count: jnp.clip(i - first, 0, count - 1)

    def spec(first, count, place):
        def index(i, r):
            at = jnp.where(i < first, 0, jnp.where(i >= first + count, 1, r))
            return place(clipped(i, first, count), at)

        return pl.BlockSpec((tall, width), index)

    specs = [
        spec(1, 3, lambda b, r: (r, b)),
        spec(0, 1, lambda b, r: (r, 0)),
        spec(4, slabs, lambda b, r: (r, b)),
        spec(4 + slabs, slabs, lambda b, r: (2 * b + r, 0)),
    ]
    shapes = [(width, 3 * width), (width, width), (width, hidden), (hidden, width)]
    lengths = [3 * width, width, width, width, hidden, width, width, width]
    specs += [pl.BlockSpec((1, n), lambda i, r: (0, 0)) for n in lengths]
    shapes += [(1, n) for n in lengths]
    return pl.pallas_call(
        partial(widen_kernel, slabs),
        out_shape=[jax.ShapeDtypeStruct(shape, F32) for shape in shapes],
        grid=(blocks, 2),
        in_specs=[
            pl.BlockSpec((1, tall, width), lambda i, r: (i, r, 0)),
            pl.BlockSpec(vec.shape, lambda i, r: (0, 0)),
        ],
        out_specs=specs,
        compiler_params=pltpu.CompilerParams(vmem_limit_bytes=VMEM_BYTES),
        name="widen",
    )(total, vec)


def shards(
    boundary, inward, inbias, outward, outbias, normgain, normshift, expand, expbias,
    shrink, shrbias, lastgain, lastshift,
):
    width = outward.shape[-1]
    hidden = expand.shape[-1]
    slabs = hidden // width
    outs = run_layer(
        boundary[0],
        (inward[0], outward[0], expand[0], shrink[0]),
        (inbias, outbias, normgain, normshift, expbias, shrbias, lastgain, lastshift),
    )
    results, factors, vectors = outs[0], outs[1:9], outs[9]
    if lax.axis_size("dp") == 4 * LANES_Z:
        total, vec = reduce_gradients(factors, vectors)
        matrices_vectors = widen(total, vec, hidden)
        matrices, pieces = matrices_vectors[:4], matrices_vectors[4:]
    else:
        f_x, f_a, f_h, f_g, f_p, f_o, f_u, f_f = factors

        def summed(left, right):
            grad = dot_tn(left, right).astype(BF16)
            mine = lax.psum_scatter(grad, "dp", scatter_dimension=0, tiled=True)
            return lax.all_gather(mine, "dp", axis=0, tiled=True).astype(F32)

        matrices = [summed(f_x, f_p), summed(f_a, f_o), summed(f_h, f_u), summed(f_g, f_f)]
        vec = lax.psum(vectors, "dp")
        pieces, row = [], 0
        for count in (3, 1, 1, 1, slabs, 1, 1, 1):
            pieces.append(vec[row : row + count].reshape(1, count * width))
            row += count

    inward_grad, outward_grad, expand_grad, shrink_grad = (m[None] for m in matrices)
    return (
        results[None],
        inward_grad, pieces[0], outward_grad, pieces[1], pieces[2], pieces[3],
        expand_grad, pieces[4], shrink_grad, pieces[5], pieces[6], pieces[7],
    )


def solution(mesh):
    matrix, vector = P("section", None, None), P("section", None)
    params = (
        matrix, vector, matrix, vector, vector, vector, matrix, vector, matrix, vector,
        vector, vector,
    )
    specs = (P("section", "dp", None),) + params
    return jax.shard_map(shards, mesh=mesh, in_specs=specs, out_specs=specs, check_vma=False)
```

```python
from functools import partial
import math

import jax
import jax.numpy as jnp
import numpy as np
from jax import lax
from jax.experimental import pallas as pl
from jax.experimental.pallas import tpu as pltpu
from jax.sharding import PartitionSpec as P

HEAD = 64
SEQ = 512
CHUNK = 256
PAIR = 2 * HEAD
EPSILON = 1e-05
MESH = pl.DeviceIdType.MESH
F32 = jnp.float32
BF16 = jnp.bfloat16
VMEM_BYTES = 63 * 2**20


def dot(a, b):
    return jnp.dot(a, b, preferred_element_type=F32)


def dot_nt(a, b):
    return lax.dot_general(a, b, (((1,), (1,)), ((), ())), preferred_element_type=F32)


def dot_tn(a, b):
    return lax.dot_general(a, b, (((0,), (0,)), ((), ())), preferred_element_type=F32)


def softplus(p):
    return jnp.maximum(p, 0.0) + jnp.log1p(jnp.exp(-jnp.abs(p)))


def sigmoid_of_softplus(q):
    series = q * (1.0 - q * (0.5 - q * (1.0 / 6.0 - q * (1.0 / 24.0))))
    return jnp.where(q < 0.03, series, 1.0 - jnp.exp(-q))


def cosine_tables():
    step = math.pi / (2.0 * SEQ)
    i = np.arange(CHUNK)[:, None]
    j = np.arange(CHUNK)[None, :]
    near = np.where(i >= j, np.cos((i - j) * step), 0.0).astype(np.float32)
    far = np.cos((i - j + CHUNK) * step).astype(np.float32)
    return near, far


def lane_masks():
    lanes = np.arange(PAIR)
    return np.stack([lanes < HEAD, lanes >= HEAD])[:, None, :].astype(np.float32)


def layer_kernel(
    boundary, inward, outward, expand, shrink,
    inbias, outbias, normgain, normshift, expbias, shrbias, lastgain, lastshift,
    near, far, masks,
    results, f_x, f_a, f_h, f_g, f_p, f_o, f_u, f_f, vector_rows,
    win, wout, wexp, wshr,
    xs, qkv, att, low, zin, hbs, gs, gps, n1s, n2s, s1s, s2s, dys, ybuf, xbuf,
    acc, keep, das, carry, vectors,
    load_sems, out_sems, res_sems, fwd_send, fwd_recv, bwd_send, bwd_recv,
):
    rows_all, width = xs.shape
    hidden = wexp.shape[1]
    chunks = rows_all // CHUNK
    pairs = width // PAIR
    slabs = hidden // width
    section = lax.axis_index("section")
    first = section == 0
    peer = {"section": 1 - section}

    loads = [
        pltpu.make_async_copy(src, dst, load_sems.at[i])
        for i, (src, dst) in enumerate(
            [(inward, win), (outward, wout), (expand, wexp), (shrink, wshr)]
        )
    ]
    load_x = pltpu.make_async_copy(boundary, xs, load_sems.at[4])
    load_y = pltpu.make_async_copy(boundary, dys, load_sems.at[4])

    loads[0].start()

    @pl.when(first)
    def _():
        load_x.start()

    @pl.when(jnp.logical_not(first))
    def _():
        load_y.start()

    barrier = pltpu.get_barrier_semaphore()
    pl.semaphore_signal(barrier, inc=1, device_id=peer, device_id_type=MESH)
    vectors[...] = jnp.zeros_like(vectors)
    pl.semaphore_wait(barrier, 1)

    def rows_of(c):
        return pl.ds(pl.multiple_of(c * CHUNK, CHUNK), CHUNK)

    def send_forward(c):
        return pltpu.make_async_remote_copy(
            src_ref=ybuf.at[rows_of(c)], dst_ref=xs.at[rows_of(c)],
            send_sem=fwd_send.at[c], recv_sem=fwd_recv.at[c],
            device_id=peer, device_id_type=MESH,
        )

    def send_backward(c):
        return pltpu.make_async_remote_copy(
            src_ref=xbuf.at[rows_of(c)], dst_ref=dys.at[rows_of(c)],
            send_sem=bwd_send.at[c], recv_sem=bwd_recv.at[c],
            device_id=peer, device_id_type=MESH,
        )

    def result_copy(buf, c):
        return pltpu.make_async_copy(buf.at[rows_of(c)], results.at[rows_of(c)], res_sems.at[c])

    early = [(xs, f_x), (att, f_a), (hbs, f_h), (gs, f_g)]
    late = [(qkv, f_p), (n1s, f_o), (gps, f_u), (n2s, f_f)]

    def factor_copies(c, which, base):
        return [
            pltpu.make_async_copy(src.at[rows_of(c)], dst.at[rows_of(c)], out_sems.at[c, base + i])
            for i, (src, dst) in enumerate(which)
        ]

    def column_sum(at, value):
        vectors[at] += jnp.sum(value, axis=0, keepdims=True)

    def norm_forward(e):
        mean = jnp.mean(e, axis=-1, keepdims=True)
        center = e - mean
        s = lax.rsqrt(jnp.mean(center * center, axis=-1, keepdims=True) + EPSILON)
        return center * s, s

    def norm_backward(dn, n, s):
        m1 = jnp.mean(dn, axis=-1, keepdims=True)
        m2 = jnp.mean(dn * n, axis=-1, keepdims=True)
        return s * (dn - m1 - n * m2)

    def pair_columns(hp):
        return [pl.ds(pl.multiple_of(i * width + hp * PAIR, PAIR), PAIR) for i in range(3)]

    def attend(c, wide):
        rows = rows_of(c)
        tiles = [(rows, near)] + ([(rows_of(c - 1), far)] if wide else [])
        m = [masks[a].astype(BF16) for a in range(2)]

        def one_pair(hp, _):
            cq, ck, cv = pair_columns(hp)
            q = qkv[rows, cq]
            nz = None
            for key_rows, weights in tiles:
                k, v = qkv[key_rows, ck], qkv[key_rows, cv]
                for a in range(2):
                    s = (dot_nt(q * m[a], k) * weights[...]).astype(BF16)
                    right = jnp.concatenate(
                        [v * m[a], jnp.broadcast_to(m[a], v.shape)], axis=1
                    )
                    part = dot(s, right)
                    nz = part if nz is None else nz + part
            inverse = 1.0 / nz[:, PAIR:]
            a_full = nz[:, :PAIR] * inverse
            a_high = a_full.astype(BF16)
            att[rows, cq] = a_high
            low[rows, cq] = (a_full - a_high.astype(F32)).astype(BF16)
            zin[rows, cq] = inverse.astype(BF16)
            return 0

        lax.fori_loop(0, pairs, one_pair, 0, unroll=True)

    def attend_backward(c, wide):
        rows = rows_of(c)
        m = [masks[a].astype(BF16) for a in range(2)]
        left = lax.broadcasted_iota(jnp.int32, (CHUNK, PAIR), 1) < HEAD

        def one_pair(hp, _):
            cq, ck, cv = pair_columns(hp)
            q, k, v = qkv[rows, cq], qkv[rows, ck], qkv[rows, cv]
            dn = (das[:, cq].astype(F32) * zin[rows, cq].astype(F32)).astype(BF16)
            prod = dn.astype(F32) * (att[rows, cq].astype(F32) + low[rows, cq].astype(F32))
            dz = jnp.concatenate(
                [-jnp.sum(prod * masks[a], axis=-1, keepdims=True) for a in range(2)], axis=0
            )
            both_q = jnp.concatenate([q * m[a] for a in range(2)], axis=0)
            both_dn = jnp.concatenate([dn * m[a] for a in range(2)], axis=0)

            def tile(kt, vt, weights):
                w = jnp.concatenate([weights[...]] * 2, axis=0)
                s = (dot_nt(both_q, kt) * w).astype(BF16)
                ds = ((dot_nt(both_dn, vt) + dz) * w).astype(BF16)
                dq2 = dot(ds, kt)
                dq = jnp.where(left, dq2[:CHUNK], dq2[CHUNK:])
                return dq, dot_tn(ds, both_q), dot_tn(s, both_dn)

            dq, dk, dv = tile(k, v, near)
            wide_cols = [pl.ds(pl.multiple_of(i * width + hp * PAIR, PAIR), PAIR) for i in range(2)]
            if wide:
                kp, vp = qkv[rows_of(c - 1), ck], qkv[rows_of(c - 1), cv]
                dqp, dkp, dvp = tile(kp, vp, far)
                dq = dq + dqp
                carry[:, wide_cols[0]] = dkp
                carry[:, wide_cols[1]] = dvp
            else:
                dk = dk + carry[:, wide_cols[0]]
                dv = dv + carry[:, wide_cols[1]]
            qkv[rows, cq] = (dq * sigmoid_of_softplus(q.astype(F32))).astype(BF16)
            qkv[rows, ck] = (dk * sigmoid_of_softplus(k.astype(F32))).astype(BF16)
            qkv[rows, cv] = dv.astype(BF16)
            return 0

        lax.fori_loop(0, pairs, one_pair, 0, unroll=True)

    def forward(c, begins):
        rows = rows_of(c)

        @pl.when(begins)
        def _():
            loads[0].wait()

            @pl.when(first)
            def _():
                load_x.wait()

            for load in loads[1:]:
                load.start()

        @pl.when(jnp.logical_not(first))
        def _():
            send_forward(c).wait_recv()

        for i in range(3):
            cols = slice(i * width, (i + 1) * width)
            p = dot(xs[rows, :], win[:, cols]) + inbias[:, cols]
            qkv[rows, cols] = (softplus(p) if i < 2 else p).astype(BF16)

        @pl.when(c % 2 == 0)
        def _():
            attend(c, False)

        @pl.when(c % 2 == 1)
        def _():
            attend(c, True)

        @pl.when(begins)
        def _():
            for load in loads[1:]:
                load.wait()

        e = xs[rows, :].astype(F32) + (dot(att[rows, :], wout[...]) + outbias[...])
        n1, s1 = norm_forward(e)
        n1s[rows, :] = n1.astype(BF16)
        s1s[rows, :] = s1
        h = n1 * normgain[...] + normshift[...]
        hbs[rows, :] = h.astype(BF16)
        acc[...] = h + shrbias[...]
        for i in range(slabs):
            cols = slice(i * width, (i + 1) * width)
            u = dot(hbs[rows, :], wexp[:, cols]) + expbias[:, cols]
            phi = 0.5 * (1.0 + lax.erf(u * math.sqrt(0.5)))
            g = (u * phi).astype(BF16)
            gs[rows, cols] = g
            gps[rows, cols] = (
                phi + u * (jnp.exp(u * u * -0.5) * (1.0 / math.sqrt(2.0 * math.pi)))
            ).astype(BF16)
            acc[...] += dot(g, wshr[cols, :])
        n2, s2 = norm_forward(acc[...])
        n2s[rows, :] = n2.astype(BF16)
        s2s[rows, :] = s2
        ybuf[rows, :] = (n2 * lastgain[...] + lastshift[...]).astype(BF16)

        @pl.when(first)
        def _():
            send_forward(c).start()

        @pl.when(jnp.logical_not(first))
        def _():
            result_copy(ybuf, c).start()

        for copy in factor_copies(c, early, 0):
            copy.start()

    def backward(c):
        rows = rows_of(c)

        @pl.when(first)
        def _():
            send_backward(c).wait_recv()

        @pl.when(jnp.logical_and(jnp.logical_not(first), c == 1))
        def _():
            load_y.wait()

        dy = dys[rows, :].astype(F32)
        n2 = n2s[rows, :].astype(F32)
        column_sum(7 + slabs, dy * n2)
        column_sum(8 + slabs, dy)
        dr = norm_backward(dy * lastgain[...], n2, s2s[rows, :])
        df = dr.astype(BF16)
        n2s[rows, :] = df
        column_sum(6 + slabs, df.astype(F32))
        acc[...] = dr
        for i in range(slabs):
            cols = slice(i * width, (i + 1) * width)
            dg = dot_nt(n2s[rows, :], wshr[cols, :])
            du = (dg * gps[rows, cols].astype(F32)).astype(BF16)
            gps[rows, cols] = du
            column_sum(6 + i, du.astype(F32))
            acc[...] += dot_nt(du, wexp[:, cols])
        dh = acc[...]
        n1 = n1s[rows, :].astype(F32)
        column_sum(4, dh * n1)
        column_sum(5, dh)
        de = norm_backward(dh * normgain[...], n1, s1s[rows, :])
        keep[...] = de
        do = de.astype(BF16)
        n1s[rows, :] = do
        column_sum(3, do.astype(F32))
        das[...] = dot_nt(do, wout[...]).astype(BF16)

        @pl.when(c % 2 == 0)
        def _():
            attend_backward(c, False)

        @pl.when(c % 2 == 1)
        def _():
            attend_backward(c, True)

        for i in range(3):
            column_sum(i, qkv[rows, i * width : (i + 1) * width].astype(F32))
        dx = keep[...] + dot_nt(qkv[rows, :], win[...])
        xbuf[rows, :] = dx.astype(BF16)

        @pl.when(first)
        def _():
            result_copy(xbuf, c).start()

        @pl.when(jnp.logical_not(first))
        def _():
            send_backward(c).start()

        for copy in factor_copies(c, late, 4):
            copy.start()

    def step(t, _):
        group, place = t // 4, t % 4
        ahead = jnp.where(first, t < chunks, place < 2)
        c_forward = jnp.where(first, t, 2 * group + place)
        back = t - chunks
        c_backward = jnp.where(first, 2 * (back // 2) + 1 - back % 2, 2 * group + 3 - place)

        @pl.when(ahead)
        def _():
            forward(c_forward, t == 0)

        @pl.when(jnp.logical_not(ahead))
        def _():
            backward(c_backward)

        return 0

    lax.fori_loop(0, 2 * chunks, step, 0)
    for i in range(vectors.shape[0]):
        vector_rows[i : i + 1, :] = vectors[i]

    def finish(c, _):
        @pl.when(first)
        def _():
            send_forward(c).wait_send()
            result_copy(xbuf, c).wait()

        @pl.when(jnp.logical_not(first))
        def _():
            send_backward(c).wait_send()
            result_copy(ybuf, c).wait()

        for copy in factor_copies(c, early, 0) + factor_copies(c, late, 4):
            copy.wait()
        return 0

    lax.fori_loop(0, chunks, finish, 0)


def run_layer(boundary, weights, biases):
    rows, width = boundary.shape
    hidden = weights[2].shape[1]
    chunks = rows // CHUNK
    near, far = cosine_tables()
    masks = lane_masks()
    slabs = hidden // width
    any_space = pl.BlockSpec(memory_space=pl.ANY)
    vmem = pl.BlockSpec(memory_space=pltpu.VMEM)
    out_widths = [width] * 4 + [hidden, 3 * width, width, hidden, width]
    out_shape = [jax.ShapeDtypeStruct((rows, w), BF16) for w in out_widths]
    vector_count = -(-(9 + slabs) // 8) * 8
    out_shape.append(jax.ShapeDtypeStruct((vector_count, width), F32))
    low = lambda *shape: pltpu.VMEM(shape, BF16)
    wide = lambda *shape: pltpu.VMEM(shape, F32)
    dma = pltpu.SemaphoreType.DMA
    return pl.pallas_call(
        layer_kernel,
        out_shape=out_shape,
        in_specs=[any_space] * 5 + [vmem] * 11,
        out_specs=[any_space] * 9 + [vmem],
        scratch_shapes=[
            low(width, 3 * width), low(width, width), low(width, hidden), low(hidden, width),
            low(rows, width), low(rows, 3 * width), low(rows, width), low(rows, width),
            low(rows, width), low(rows, width), low(rows, hidden), low(rows, hidden),
            low(rows, width), low(rows, width), wide(rows, 1), wide(rows, 1),
            low(rows, width), low(rows, width), low(rows, width),
            wide(CHUNK, width), wide(CHUNK, width), low(CHUNK, width), wide(CHUNK, 2 * width),
            wide(vector_count, 1, width),
            dma((5,)), dma((chunks, 8)), dma((chunks,)), dma((chunks,)), dma((chunks,)),
            dma((chunks,)), dma((chunks,)),
        ],
        compiler_params=pltpu.CompilerParams(
            collective_id=0, has_side_effects=True, vmem_limit_bytes=VMEM_BYTES
        ),
        name="layer",
    )(boundary, *weights, *biases, jnp.asarray(near), jnp.asarray(far), jnp.asarray(masks))


SETS = 2
LANES_Z = 4

ARRIVE_Y = 2
PAIR_AT = (0, 2, 3, 13)
ONE_AT = (0, 3, 4, 17)
LAST_ONE, LAST_PAIR, LAST_CROSS = 21, 20, 21
BACK_AT = (0, 20, 21, 24)
OUT_AT = (22, 22, 22, 25)


def gradient_kernel(
    f_x, f_a, f_h, f_g, f_p, f_o, f_u, f_f, vec_in,
    total, vec_out,
    x, a, h, g, p, o, u, f,
    part, core_in, chain_pair, chain_one, y_in, end_in, vec, vec_got,
    load_sems, core_s, core_r, y_s, y_r, pair_s, pair_r, one_s, one_r, end_s, end_r,
    got, z_s, yy_s, kept, out_s, out_r, vec_s, vec_r,
):
    width = x.shape[1]
    slabs = g.shape[1] // width
    me = lax.axis_index("dp")
    core, y, z = me % 2, (me // 2) % 2, me // 4
    last = LANES_Z - 1
    core_peer, y_peer = {"dp": me + 1 - 2 * core}, {"dp": me + 2 - 4 * y}
    hop = [last - z, z]
    ahead = [{"dp": me - 4}, {"dp": me + 4}]
    behind = [ahead[1], ahead[0]]

    blocks = (
        [(a, 0, o, 0)]
        + [(x, 0, p, i) for i in range(3)]
        + [(h, 0, u, i) for i in range(slabs)]
        + [(g, i, f, 0) for i in range(slabs)]
    )
    duos = len(blocks) // 2
    sets = duos * SETS
    set_rows = width // SETS
    half = set_rows // 2
    piece = half // 4

    sources = [(f_a, a), (f_o, o), (f_x, x), (f_p, p), (f_h, h), (f_u, u), (f_f, f), (f_g, g)]
    loads = [
        pltpu.make_async_copy(src, dst, load_sems.at[i]) for i, (src, dst) in enumerate(sources)
    ]
    load_at = {0: (0, 1, 2, 3), 2 * SETS: (4, 5), (2 + slabs // 2) * SETS: (6, 7)}
    for load in loads[:4]:
        load.start()

    barrier = pltpu.get_barrier_semaphore()
    for peer in (core_peer, y_peer):
        pl.semaphore_signal(barrier, inc=1, device_id=peer, device_id_type=MESH)
    for d in range(2):
        @pl.when(hop[d] < last)
        def _():
            pl.semaphore_signal(barrier, inc=1, device_id=ahead[d], device_id_type=MESH)
    pl.semaphore_wait(barrier, jnp.where(jnp.logical_and(z > 0, z < last), 4, 3))

    def remote(src, dst, send, recv, peer):
        return pltpu.make_async_remote_copy(
            src_ref=src, dst_ref=dst, send_sem=send, recv_sem=recv,
            device_id=peer, device_id_type=MESH,
        )

    def span(k, d, first, count):
        start = (k % SETS) * set_rows + d * half + first * piece
        return pl.ds(pl.multiple_of(start, 16), count * piece)

    def mine(k, d, first, count=1):
        return part.at[k // SETS, core, span(k, d, first, count)]

    def final(k, d, first, count=1):
        return total.at[2 * (k // SETS) + core, span(k, d, first, count)]

    def add(dst, src):
        dst[...] = (dst[...].astype(F32) + src[...].astype(F32)).astype(BF16)

    def core_copy(k):
        rows = pl.ds(pl.multiple_of((k % SETS) * set_rows, set_rows), set_rows)
        return remote(
            part.at[k // SETS, 1 - core, rows], core_in.at[k], core_s.at[k], core_r.at[k], core_peer
        )

    def y_copy(k, d):
        return remote(mine(k, d, 1 - y), y_in.at[k, d], y_s.at[k, d], y_r.at[k, d], y_peer)

    def pair_copy(k, d):
        return remote(
            mine(k, d, 2, 2), chain_pair.at[k, d], pair_s.at[k, d], pair_r.at[k, d], ahead[d]
        )

    def one_copy(k, d):
        return remote(mine(k, d, y), chain_one.at[k, d], one_s.at[k, d], one_r.at[k, d], ahead[d])

    def end_copy(k, d):
        return remote(mine(k, d, 3 - y), end_in.at[k], end_s.at[k], end_r.at[k], y_peer)

    def spread_z(k, d, b, i, src):
        return remote(src, final(k, d, b), z_s.at[k, d, i], got.at[k, d, b], behind[d])

    def spread_y(k, d, b, i, src):
        return remote(src, final(k, d, b), yy_s.at[k, d, i], got.at[k, d, b], y_peer)

    def keep_copy(k, d, b, i):
        return pltpu.make_async_copy(mine(k, d, b), final(k, d, b), kept.at[k, d, i])

    def out_copy(k, d):
        return remote(
            final(k, d, 0, 4), final(k, d, 0, 4), out_s.at[k, d], out_r.at[k, d], core_peer
        )

    def arrived(k, d, b):
        spread_z(k, d, b, 0, final(k, d, b)).wait_recv()

    outer = jnp.logical_or(z == 0, z == last)
    z_pair = {"dp": me + 4 - 8 * (z % 2)}
    z_mid = {"dp": jnp.where(z == 1, me + 4, me - 4)}
    z_out = {"dp": jnp.where(z == 1, me - 4, me + 4)}

    def vec_copy(i, peer):
        return remote(vec.at[i], vec_got.at[min(i, 3)], vec_s.at[i], vec_r.at[min(i, 3)], peer)

    def compute(k):
        for i in load_at.get(k, ()):
            loads[i].wait()
        m, at = k // SETS, (k % SETS) * set_rows
        for side in range(2):
            left, i, right, j = blocks[2 * m + side]
            cols = slice(i * width + at, i * width + at + set_rows)
            part[m, side, at : at + set_rows, :] = dot_tn(
                left[:, cols], right[:, j * width : (j + 1) * width]
            ).astype(BF16)
        core_copy(k).start()

    vec[0] = vec_in[...]
    vec_copy(0, core_peer).start()
    compute(0)
    for load in loads[4:]:
        load.start()

    def feed(t):
        for k in range(1, sets):
            @pl.when(t == k - 1)
            def _():
                compute(k)

        for i, peer in ((1, y_peer), (2, z_pair)):
            @pl.when(t == i)
            def _():
                vec_copy(i - 1, peer).wait_recv()
                vec[i] = vec[i - 1] + vec_got[i - 1]
                vec_copy(i, peer).start()

        @pl.when(t == 3)
        def _():
            vec_copy(2, z_pair).wait_recv()
            vec[3] = vec[2] + vec_got[2]

            @pl.when(jnp.logical_not(outer))
            def _():
                vec_copy(3, z_mid).start()

        @pl.when(jnp.logical_and(t == 4, jnp.logical_not(outer)))
        def _():
            vec_copy(3, z_mid).wait_recv()
            vec[4] = vec[3] + vec_got[3]
            vec_copy(4, z_out).start()
            vec_out[...] = vec[4]

        @pl.when(jnp.logical_and(t == 5, outer))
        def _():
            vec_copy(3, z_mid).wait_recv()
            vec_out[...] = vec_got[3]

        @pl.when(t < sets)
        def _():
            core_copy(t).wait_recv()
            for d in range(2):
                add(mine(t, d, 0, 4), core_in.at[t, pl.ds(d * half, half)])
                y_copy(t, d).start()

                @pl.when(hop[d] == 0)
                def _():
                    pair_copy(t, d).start()

    def during(k, more=True):
        return jnp.logical_and(jnp.logical_and(k >= 0, k < sets), more)

    def by_place(place, offsets):
        out = jnp.int32(offsets[0])
        for i, offset in enumerate(offsets[1:], 1):
            out = jnp.where(place == i, offset, out)
        return out

    def arrive_y(t):
        k = t - ARRIVE_Y

        @pl.when(during(k))
        def _():
            for d in range(2):
                y_copy(k, d).wait_recv()
                add(mine(k, d, y), y_in.at[k, d])

                @pl.when(hop[d] == 0)
                def _():
                    one_copy(k, d).start()

    def hop_pair(t):
        for d in range(2):
            k = t - by_place(hop[d], PAIR_AT)

            @pl.when(during(k, hop[d] > 0))
            def _():
                pair_copy(k, d).wait_recv()
                add(mine(k, d, 2, 2), chain_pair.at[k, d])

                @pl.when(hop[d] < last)
                def _():
                    pair_copy(k, d).start()

                @pl.when(hop[d] == last)
                def _():
                    end_copy(k, d).start()

    def hop_one(t):
        for d in range(2):
            k = t - by_place(hop[d], ONE_AT)

            @pl.when(during(k, hop[d] > 0))
            def _():
                one_copy(k, d).wait_recv()
                add(mine(k, d, y), chain_one.at[k, d])

                @pl.when(hop[d] < last)
                def _():
                    one_copy(k, d).start()

    def last_one(t):
        k = t - LAST_ONE
        for d in range(2):
            @pl.when(during(k, hop[d] == last))
            def _():
                spread_z(k, d, y, 0, mine(k, d, y)).start()
                spread_y(k, d, y, 0, mine(k, d, y)).start()
                keep_copy(k, d, y, 0).start()

    def last_pair(t):
        k = t - LAST_PAIR
        for d in range(2):
            @pl.when(during(k, hop[d] == last))
            def _():
                end_copy(k, d).wait_recv()
                add(mine(k, d, 2 + y), end_in.at[k])
                spread_y(k, d, 2 + y, 1, mine(k, d, 2 + y)).start()
                spread_z(k, d, 2 + y, 1 + y, mine(k, d, 2 + y)).start()
                keep_copy(k, d, 2 + y, 1).start()

    def last_cross(t):
        k = t - LAST_CROSS
        for d in range(2):
            @pl.when(during(k, hop[d] == last))
            def _():
                arrived(k, d, 3 - y)
                spread_z(k, d, 3 - y, 2 - y, final(k, d, 3 - y)).start()

    def way_back(t):
        for d in range(2):
            k = t - by_place(last - hop[d], BACK_AT)

            @pl.when(during(k, hop[d] < last))
            def _():
                for i, b in ((0, y), (1, 2), (2, 3)):
                    arrived(k, d, b)

                    @pl.when(hop[d] > 0)
                    def _():
                        spread_z(k, d, b, i, final(k, d, b)).start()

                    if i == 0:
                        spread_y(k, d, b, 0, final(k, d, b)).start()

    def to_core(t):
        for d in range(2):
            k = t - by_place(last - hop[d], OUT_AT)

            @pl.when(during(k))
            def _():
                arrived(k, d, 1 - y)

                @pl.when(hop[d] == last)
                def _():
                    keep_copy(k, d, y, 0).wait()
                    keep_copy(k, d, 2 + y, 1).wait()

                out_copy(k, d).start()

    def tick(t, _):
        for stage in (
            last_one, hop_one, arrive_y, hop_pair, to_core, last_cross, feed, last_pair, way_back
        ):
            stage(t)
        return 0

    lax.fori_loop(0, sets + max(OUT_AT), tick, 0)

    def settle(k, _):
        core_copy(k).wait_send()
        for d in range(2):
            y_copy(k, d).wait_send()
            out_copy(k, d).wait()
            spread_y(k, d, y, 0, final(k, d, y)).wait_send()

            @pl.when(hop[d] < last)
            def _():
                pair_copy(k, d).wait_send()
                one_copy(k, d).wait_send()

            @pl.when(hop[d] == last)
            def _():
                end_copy(k, d).wait_send()
                spread_y(k, d, 2 + y, 1, final(k, d, 2 + y)).wait_send()

            @pl.when(hop[d] > 0)
            def _():
                for i, b in ((0, y), (1, 2), (2, 3)):
                    spread_z(k, d, b, i, final(k, d, b)).wait_send()

        return 0

    lax.fori_loop(0, sets, settle, 0)

    for i in range(3):
        vec_copy(i, core_peer).wait_send()

    @pl.when(jnp.logical_not(outer))
    def _():
        vec_copy(3, z_mid).wait_send()
        vec_copy(4, z_out).wait_send()


def reduce_gradients(factors, vectors):
    rows, width = factors[0].shape
    hidden = factors[3].shape[1]
    blocks = 4 + 2 * (hidden // width)
    duos = blocks // 2
    sets = duos * SETS
    piece = width // SETS // 8
    any_space = pl.BlockSpec(memory_space=pl.ANY)
    vmem = pl.BlockSpec(memory_space=pltpu.VMEM)
    low = lambda *shape: pltpu.VMEM(shape, BF16)
    dma = lambda *shape: pltpu.SemaphoreType.DMA(shape)
    return pl.pallas_call(
        gradient_kernel,
        out_shape=[
            jax.ShapeDtypeStruct((blocks, width, width), BF16),
            jax.ShapeDtypeStruct(vectors.shape, F32),
        ],
        in_specs=[any_space] * 8 + [vmem],
        out_specs=[any_space, vmem],
        scratch_shapes=[low(*factor.shape) for factor in factors]
        + [
            low(duos, 2, width, width), low(sets, width // SETS, width),
            low(sets, 2, 2 * piece, width), low(sets, 2, piece, width),
            low(sets, 2, piece, width), low(sets, piece, width),
            pltpu.VMEM((5,) + vectors.shape, F32), pltpu.VMEM((4,) + vectors.shape, F32),
            dma(8), dma(sets), dma(sets), dma(sets, 2), dma(sets, 2), dma(sets, 2), dma(sets, 2),
            dma(sets, 2), dma(sets, 2), dma(sets), dma(sets),
            dma(sets, 2, 4), dma(sets, 2, 3), dma(sets, 2, 2), dma(sets, 2, 2), dma(sets, 2),
            dma(sets, 2), dma(5), dma(4),
        ],
        compiler_params=pltpu.CompilerParams(
            collective_id=1, has_side_effects=True, vmem_limit_bytes=VMEM_BYTES
        ),
        name="gradients",
    )(*factors, vectors)


def widen_kernel(slabs, total, vec, low_results, *refs):
    outs, results = refs[:12], refs[12]
    low, high, held, in_sems, out_sems, side_sems = refs[13:]
    blocks, width, _ = total.shape
    inward, outward, expand, shrink = outs[:4]

    def reads(i):
        return pltpu.make_async_copy(total.at[i], low.at[i], in_sems.at[i])

    def place(i):
        if i < 1:
            return outward
        if i < 4:
            return inward.at[:, pl.ds((i - 1) * width, width)]
        if i < 4 + slabs:
            return expand.at[:, pl.ds((i - 4) * width, width)]
        return shrink.at[pl.ds((i - 4 - slabs) * width, width)]

    def writes(i):
        return pltpu.make_async_copy(high.at[i], place(i), out_sems.at[i])

    side_in = pltpu.make_async_copy(low_results, held, side_sems.at[0])
    side_out = pltpu.make_async_copy(held, results, side_sems.at[1])
    for i in range(blocks):
        reads(i).start()
    side_in.start()
    row = 0
    for out in outs[4:]:
        for i in range(out.shape[1] // width):
            out[:, i * width : (i + 1) * width] = vec[row : row + 1, :]
            row += 1
    for i in range(blocks):
        reads(i).wait()

        def part(r, _):
            rows = pl.ds(pl.multiple_of(r * 64, 64), 64)
            high[i, rows] = low[i, rows].astype(F32)
            return 0

        lax.fori_loop(0, width // 64, part, 0)
        writes(i).start()
    side_in.wait()
    side_out.start()
    for i in range(blocks):
        writes(i).wait()
    side_out.wait()


def widen(total, vec, low_results, hidden):
    blocks, width, _ = total.shape
    slabs = hidden // width
    shapes = [(width, 3 * width), (width, width), (width, hidden), (hidden, width)]
    lengths = [3 * width, width, width, width, hidden, width, width, width]
    any_space = pl.BlockSpec(memory_space=pl.ANY)
    vmem = pl.BlockSpec(memory_space=pltpu.VMEM)
    dma = lambda *shape: pltpu.SemaphoreType.DMA(shape)
    return pl.pallas_call(
        partial(widen_kernel, slabs),
        out_shape=[jax.ShapeDtypeStruct(shape, F32) for shape in shapes]
        + [jax.ShapeDtypeStruct((1, n), F32) for n in lengths]
        + [jax.ShapeDtypeStruct(low_results.shape, BF16)],
        in_specs=[any_space, vmem, any_space],
        out_specs=[any_space] * 4 + [vmem] * 8 + [any_space],
        scratch_shapes=[
            pltpu.VMEM((blocks, width, width), BF16), pltpu.VMEM((blocks, width, width), F32),
            pltpu.VMEM(low_results.shape, BF16), dma(blocks), dma(blocks), dma(2),
        ],
        compiler_params=pltpu.CompilerParams(vmem_limit_bytes=VMEM_BYTES),
        name="widen",
    )(total, vec, low_results)


def shards(
    boundary, inward, inbias, outward, outbias, normgain, normshift, expand, expbias,
    shrink, shrbias, lastgain, lastshift,
):
    width = outward.shape[-1]
    hidden = expand.shape[-1]
    slabs = hidden // width
    outs = run_layer(
        boundary[0],
        (inward[0], outward[0], expand[0], shrink[0]),
        (inbias, outbias, normgain, normshift, expbias, shrbias, lastgain, lastshift),
    )
    results, factors, vectors = outs[0], outs[1:9], outs[9]
    if lax.axis_size("dp") == 4 * LANES_Z:
        total, vec = reduce_gradients(factors, vectors)
        widened = widen(total, vec, results, hidden)
        matrices, pieces, results = widened[:4], widened[4:12], widened[12]
    else:
        f_x, f_a, f_h, f_g, f_p, f_o, f_u, f_f = factors

        def summed(left, right):
            grad = dot_tn(left, right).astype(BF16)
            mine = lax.psum_scatter(grad, "dp", scatter_dimension=0, tiled=True)
            return lax.all_gather(mine, "dp", axis=0, tiled=True).astype(F32)

        matrices = [summed(f_x, f_p), summed(f_a, f_o), summed(f_h, f_u), summed(f_g, f_f)]
        vec = lax.psum(vectors, "dp")
        pieces, row = [], 0
        for count in (3, 1, 1, 1, slabs, 1, 1, 1):
            pieces.append(vec[row : row + count].reshape(1, count * width))
            row += count

    inward_grad, outward_grad, expand_grad, shrink_grad = (m[None] for m in matrices)
    return (
        results[None],
        inward_grad, pieces[0], outward_grad, pieces[1], pieces[2], pieces[3],
        expand_grad, pieces[4], shrink_grad, pieces[5], pieces[6], pieces[7],
    )


def solution(mesh):
    matrix, vector = P("section", None, None), P("section", None)
    params = (
        matrix, vector, matrix, vector, vector, vector, matrix, vector, matrix, vector,
        vector, vector,
    )
    specs = (P("section", "dp", None),) + params
    return jax.shard_map(shards, mesh=mesh, in_specs=specs, out_specs=specs, check_vma=False)
```

```python
from collections.abc import Callable
from functools import partial
import math
from typing import NamedTuple

import jax
import jax.numpy as jnp
import numpy as np
from jax import lax
from jax.experimental import pallas as pl
from jax.experimental.pallas import tpu as pltpu
from jax.sharding import PartitionSpec as P

HEAD = 64
SEQ = 512
CHUNK = 256
PAIR = 2 * HEAD
EPSILON = 1e-05
MESH = pl.DeviceIdType.MESH
F32 = jnp.float32
BF16 = jnp.bfloat16
VMEM_BYTES = 63 * 2**20


def dot(a, b):
    return jnp.dot(a, b, preferred_element_type=F32)


def dot_nt(a, b):
    return lax.dot_general(a, b, (((1,), (1,)), ((), ())), preferred_element_type=F32)


def dot_tn(a, b):
    return lax.dot_general(a, b, (((0,), (0,)), ((), ())), preferred_element_type=F32)


def softplus(p):
    return jnp.maximum(p, 0.0) + jnp.log1p(jnp.exp(-jnp.abs(p)))


def sigmoid_of_softplus(q):
    series = q * (1.0 - q * (0.5 - q * (1.0 / 6.0 - q * (1.0 / 24.0))))
    return jnp.where(q < 0.03, series, 1.0 - jnp.exp(-q))


def cosine_tables():
    step = math.pi / (2.0 * SEQ)
    i = np.arange(CHUNK)[:, None]
    j = np.arange(CHUNK)[None, :]
    near = np.where(i >= j, np.cos((i - j) * step), 0.0).astype(np.float32)
    far = np.cos((i - j + CHUNK) * step).astype(np.float32)
    return near, far


def lane_masks():
    lanes = np.arange(PAIR)
    return np.stack([lanes < HEAD, lanes >= HEAD])[:, None, :].astype(np.float32)


SETS = 2
LANES_Z = 4
STAGES = 3
BEGUN = 2

ARRIVE_Y = 2
PAIR_AT = (0, 2, 3, 13)
ONE_AT = (0, 3, 4, 17)
LAST_ONE, LAST_PAIR, LAST_CROSS = 21, 20, 21
BACK_AT = (0, 20, 21, 24)
OUT_AT = (22, 22, 22, 25)


class Steps(NamedTuple):
    greet: Callable
    free: Callable
    begin: Callable
    run: Callable


def reduction_steps(factors, held, slabs, vectors, outputs, scratch):
    x, a, h, g, p, o, u, f = factors
    total, vec_out = outputs
    (
        stage, chain_pair, chain_one, y_in, end_in, vec, vec_got,
        core_s, core_r, y_s, y_r, pair_s, pair_r, one_s, one_r, end_s, end_r,
        got, z_s, yy_s, kept, out_s, out_r, vec_s, vec_r, freed,
    ) = scratch
    width = x.shape[1]
    me = lax.axis_index("dp")
    core, y, z = me % 2, (me // 2) % 2, me // 4
    last = LANES_Z - 1
    core_peer, y_peer = {"dp": me + 1 - 2 * core}, {"dp": me + 2 - 4 * y}
    hop = [last - z, z]
    ahead = [{"dp": me - 4}, {"dp": me + 4}]
    behind = [ahead[1], ahead[0]]

    blocks = (
        [(g, i, f, 0) for i in range(slabs)]
        + [(h, 0, u, i) for i in range(slabs)]
        + [(a, 0, o, 0)]
        + [(x, 0, p, i) for i in range(3)]
    )
    sets = len(blocks) // 2 * SETS
    set_rows = width // SETS
    half = set_rows // 2
    piece = half // 4

    def greet(barrier):
        for peer in (core_peer, y_peer):
            pl.semaphore_signal(barrier, inc=1, device_id=peer, device_id_type=MESH)
        for d in range(2):
            @pl.when(hop[d] < last)
            def _():
                pl.semaphore_signal(barrier, inc=1, device_id=ahead[d], device_id_type=MESH)
        return jnp.where(jnp.logical_and(z > 0, z < last), 4, 3)

    def free(i):
        pl.semaphore_signal(freed.at[i], inc=1, device_id=core_peer, device_id_type=MESH)

    def remote(src, dst, send, recv, peer):
        return pltpu.make_async_remote_copy(
            src_ref=src, dst_ref=dst, send_sem=send, recv_sem=recv,
            device_id=peer, device_id_type=MESH,
        )

    def span(k, d, first, count):
        start = (k % SETS) * set_rows + d * half + first * piece
        return pl.ds(pl.multiple_of(start, 16), count * piece)

    def place(m, feed_forward, attention):
        return jnp.where(m < slabs, feed_forward + m, attention + m - slabs)

    def mine(k, d, first, count=1):
        return held.at[place(k // SETS, 4 + slabs, 0), span(k, d, first, count)]

    def from_core(k, start, count):
        rows = pl.ds(pl.multiple_of((k % SETS) * set_rows + start, 16), count)
        return held.at[place(k // SETS, 4, 2), rows]

    def final(k, d, first, count=1):
        return total.at[2 * (k // SETS) + core, span(k, d, first, count)]

    def add(dst, src):
        dst[...] = (dst[...].astype(F32) + src[...].astype(F32)).astype(BF16)

    def core_copy(k):
        return remote(
            stage.at[k % STAGES, 1 - core], from_core(k, 0, set_rows), core_s.at[k], core_r.at[k],
            core_peer,
        )

    def y_copy(k, d):
        return remote(mine(k, d, 1 - y), y_in.at[k, d], y_s.at[k, d], y_r.at[k, d], y_peer)

    def pair_copy(k, d):
        return remote(
            mine(k, d, 2, 2), chain_pair.at[k, d], pair_s.at[k, d], pair_r.at[k, d], ahead[d]
        )

    def one_copy(k, d):
        return remote(mine(k, d, y), chain_one.at[k, d], one_s.at[k, d], one_r.at[k, d], ahead[d])

    def end_copy(k, d):
        return remote(mine(k, d, 3 - y), end_in.at[k], end_s.at[k], end_r.at[k], y_peer)

    def spread_z(k, d, b, i, src):
        return remote(src, final(k, d, b), z_s.at[k, d, i], got.at[k, d, b], behind[d])

    def spread_y(k, d, b, i, src):
        return remote(src, final(k, d, b), yy_s.at[k, d, i], got.at[k, d, b], y_peer)

    def keep_copy(k, d, b, i):
        return pltpu.make_async_copy(mine(k, d, b), final(k, d, b), kept.at[k, d, i])

    def out_copy(k, d):
        return remote(
            final(k, d, 0, 4), final(k, d, 0, 4), out_s.at[k, d], out_r.at[k, d], core_peer
        )

    def arrived(k, d, b):
        spread_z(k, d, b, 0, final(k, d, b)).wait_recv()

    outer = jnp.logical_or(z == 0, z == last)
    z_pair = {"dp": me + 4 - 8 * (z % 2)}
    z_mid = {"dp": jnp.where(z == 1, me + 4, me - 4)}
    z_out = {"dp": jnp.where(z == 1, me - 4, me + 4)}

    def vec_copy(i, peer):
        return remote(vec.at[i], vec_got.at[min(i, 3)], vec_s.at[i], vec_r.at[min(i, 3)], peer)

    def compute(k):
        if k >= STAGES:
            core_copy(k - STAGES).wait_send()
        m, at = k // SETS, (k % SETS) * set_rows
        for side in range(2):
            left, i, right, j = blocks[2 * m + side]
            cols = slice(i * width + at, i * width + at + set_rows)
            stage[k % STAGES, side] = dot_tn(
                left[:, cols], right[:, j * width : (j + 1) * width]
            ).astype(BF16)
        if k == slabs * SETS:
            pl.semaphore_wait(freed.at[1], 1)
        core_copy(k).start()

    def feed(k):
        core_copy(k).wait_recv()
        for d in range(2):
            own = stage[k % STAGES, core, d * half : (d + 1) * half].astype(F32)
            other = from_core(k, d * half, half)[...].astype(F32)
            mine(k, d, 0, 4)[...] = (own + other).astype(BF16)
            y_copy(k, d).start()

            @pl.when(hop[d] == 0)
            def _():
                pair_copy(k, d).start()

    def begin():
        pl.semaphore_wait(freed.at[0], 1)
        compute(0)
        compute(1)
        feed(0)
        compute(2)
        feed(1)

    def sum_vectors(t):
        for i, peer in ((1, y_peer), (2, z_pair)):
            @pl.when(t == i + BEGUN)
            def _():
                vec_copy(i - 1, peer).wait_recv()
                vec[i] = vec[i - 1] + vec_got[i - 1]
                vec_copy(i, peer).start()

        @pl.when(t == 3 + BEGUN)
        def _():
            vec_copy(2, z_pair).wait_recv()
            vec[3] = vec[2] + vec_got[2]

            @pl.when(jnp.logical_not(outer))
            def _():
                vec_copy(3, z_mid).start()

        @pl.when(jnp.logical_and(t == 4 + BEGUN, jnp.logical_not(outer)))
        def _():
            vec_copy(3, z_mid).wait_recv()
            vec[4] = vec[3] + vec_got[3]
            vec_copy(4, z_out).start()
            vec_out[...] = vec[4]

        @pl.when(jnp.logical_and(t == 5 + BEGUN, outer))
        def _():
            vec_copy(3, z_mid).wait_recv()
            vec_out[...] = vec_got[3]

    def feed_at(t):
        for k in range(BEGUN + 1, sets):
            @pl.when(t == k - 1)
            def _():
                compute(k)

        sum_vectors(t)

        @pl.when(t < sets)
        def _():
            feed(t)

    def during(k, more=True):
        return jnp.logical_and(jnp.logical_and(k >= 0, k < sets), more)

    def by_place(place, offsets):
        out = jnp.int32(offsets[0])
        for i, offset in enumerate(offsets[1:], 1):
            out = jnp.where(place == i, offset, out)
        return out

    def arrive_y(t):
        k = t - ARRIVE_Y

        @pl.when(during(k))
        def _():
            for d in range(2):
                y_copy(k, d).wait_recv()
                add(mine(k, d, y), y_in.at[k, d])

                @pl.when(hop[d] == 0)
                def _():
                    one_copy(k, d).start()

    def hop_pair(t):
        for d in range(2):
            k = t - by_place(hop[d], PAIR_AT)

            @pl.when(during(k, hop[d] > 0))
            def _():
                pair_copy(k, d).wait_recv()
                add(mine(k, d, 2, 2), chain_pair.at[k, d])

                @pl.when(hop[d] < last)
                def _():
                    pair_copy(k, d).start()

                @pl.when(hop[d] == last)
                def _():
                    end_copy(k, d).start()

    def hop_one(t):
        for d in range(2):
            k = t - by_place(hop[d], ONE_AT)

            @pl.when(during(k, hop[d] > 0))
            def _():
                one_copy(k, d).wait_recv()
                add(mine(k, d, y), chain_one.at[k, d])

                @pl.when(hop[d] < last)
                def _():
                    one_copy(k, d).start()

    def last_one(t):
        k = t - LAST_ONE
        for d in range(2):
            @pl.when(during(k, hop[d] == last))
            def _():
                spread_z(k, d, y, 0, mine(k, d, y)).start()
                spread_y(k, d, y, 0, mine(k, d, y)).start()
                keep_copy(k, d, y, 0).start()

    def last_pair(t):
        k = t - LAST_PAIR
        for d in range(2):
            @pl.when(during(k, hop[d] == last))
            def _():
                end_copy(k, d).wait_recv()
                add(mine(k, d, 2 + y), end_in.at[k])
                spread_y(k, d, 2 + y, 1, mine(k, d, 2 + y)).start()
                spread_z(k, d, 2 + y, 1 + y, mine(k, d, 2 + y)).start()
                keep_copy(k, d, 2 + y, 1).start()

    def last_cross(t):
        k = t - LAST_CROSS
        for d in range(2):
            @pl.when(during(k, hop[d] == last))
            def _():
                arrived(k, d, 3 - y)
                spread_z(k, d, 3 - y, 2 - y, final(k, d, 3 - y)).start()

    def way_back(t):
        for d in range(2):
            k = t - by_place(last - hop[d], BACK_AT)

            @pl.when(during(k, hop[d] < last))
            def _():
                for i, b in ((0, y), (1, 2), (2, 3)):
                    arrived(k, d, b)

                    @pl.when(hop[d] > 0)
                    def _():
                        spread_z(k, d, b, i, final(k, d, b)).start()

                    if i == 0:
                        spread_y(k, d, b, 0, final(k, d, b)).start()

    def to_core(t):
        for d in range(2):
            k = t - by_place(last - hop[d], OUT_AT)

            @pl.when(during(k))
            def _():
                arrived(k, d, 1 - y)

                @pl.when(hop[d] == last)
                def _():
                    keep_copy(k, d, y, 0).wait()
                    keep_copy(k, d, 2 + y, 1).wait()

                out_copy(k, d).start()

    def tick(t, _):
        for stage in (
            last_one, hop_one, arrive_y, hop_pair, to_core, last_cross, feed_at, last_pair, way_back
        ):
            stage(t)
        return 0

    def run():
        for i in range(vectors.shape[0]):
            vec[0, i : i + 1, :] = vectors[i]
        vec_copy(0, core_peer).start()
        lax.fori_loop(BEGUN, sets + max(OUT_AT), tick, 0)

        def settle(k, _):
            for d in range(2):
                y_copy(k, d).wait_send()
                out_copy(k, d).wait()
                spread_y(k, d, y, 0, final(k, d, y)).wait_send()

                @pl.when(hop[d] < last)
                def _():
                    pair_copy(k, d).wait_send()
                    one_copy(k, d).wait_send()

                @pl.when(hop[d] == last)
                def _():
                    end_copy(k, d).wait_send()
                    spread_y(k, d, 2 + y, 1, final(k, d, 2 + y)).wait_send()

                @pl.when(hop[d] > 0)
                def _():
                    for i, b in ((0, y), (1, 2), (2, 3)):
                        spread_z(k, d, b, i, final(k, d, b)).wait_send()

            return 0

        lax.fori_loop(0, sets, settle, 0)
        for k in range(sets - STAGES, sets):
            core_copy(k).wait_send()

        for i in range(3):
            vec_copy(i, core_peer).wait_send()

        @pl.when(jnp.logical_not(outer))
        def _():
            vec_copy(3, z_mid).wait_send()
            vec_copy(4, z_out).wait_send()

    return Steps(greet, free, begin, run)


def layer_kernel(merged, *refs):
    refs = list(refs)

    def take(count):
        out = refs[:count]
        del refs[:count]
        return out

    boundary, inward, outward, expand, shrink = take(5)
    small_in = take(11)
    (results,) = take(1)
    outputs = take(2 if merged else 9)
    small = take(11)
    (
        inbias, outbias, normgain, normshift, expbias, shrbias, lastgain, lastshift,
        near, far, masks,
    ) = small
    (
        held, xs, qkv, att, low, zin, hbs, gs, gps, n1s, n2s, s1s, s2s, dys, ybuf,
        acc, keep, das, carry, vectors,
        load_sems, small_sems, res_sems, fwd_send, fwd_recv, bwd_send, bwd_recv,
    ) = take(27)
    rows_all, width = xs.shape
    hidden = gs.shape[1]
    chunks = rows_all // CHUNK
    pairs = width // PAIR
    slabs = hidden // width
    section = lax.axis_index("section")
    first = section == 0
    peer = {"section": 1 - section}

    def slab(i):
        return pl.ds(i * width, width)

    w_in, w_out, w_up, w_down = 0, 3, 4, 4 + slabs
    pieces = (
        [inward.at[:, slab(i)] for i in range(3)] + [outward]
        + [expand.at[:, slab(i)] for i in range(slabs)]
        + [shrink.at[slab(i)] for i in range(slabs)]
    )
    loads = [
        pltpu.make_async_copy(src, held.at[i], load_sems.at[i]) for i, src in enumerate(pieces)
    ]
    load_x = pltpu.make_async_copy(boundary, xs, load_sems.at[len(pieces)])
    load_y = pltpu.make_async_copy(boundary, dys, load_sems.at[len(pieces)])
    small_loads = [
        pltpu.make_async_copy(src, dst, small_sems.at[i])
        for i, (src, dst) in enumerate(zip(small_in, small))
    ]

    @pl.when(first)
    def _():
        load_x.start()

    for load in loads[:3] + small_loads:
        load.start()

    @pl.when(jnp.logical_not(first))
    def _():
        load_y.start()

    barrier = pltpu.get_barrier_semaphore()
    pl.semaphore_signal(barrier, inc=1, device_id=peer, device_id_type=MESH)
    if merged:
        reduction = reduction_steps(
            (xs, att, hbs, gs, qkv, n1s, gps, n2s), held, slabs, vectors, outputs, take(26)
        )
        expected = 1 + reduction.greet(barrier)
    else:
        expected = 1
    vectors[...] = jnp.zeros_like(vectors)
    pl.semaphore_wait(barrier, expected)
    for load in small_loads:
        load.wait()

    def rows_of(c):
        return pl.ds(pl.multiple_of(c * CHUNK, CHUNK), CHUNK)

    def send_forward(c):
        return pltpu.make_async_remote_copy(
            src_ref=ybuf.at[rows_of(c)], dst_ref=xs.at[rows_of(c)],
            send_sem=fwd_send.at[c], recv_sem=fwd_recv.at[c],
            device_id=peer, device_id_type=MESH,
        )

    def send_backward(c):
        return pltpu.make_async_remote_copy(
            src_ref=ybuf.at[rows_of(c)], dst_ref=dys.at[rows_of(c)],
            send_sem=bwd_send.at[c], recv_sem=bwd_recv.at[c],
            device_id=peer, device_id_type=MESH,
        )

    def result_copy(c):
        return pltpu.make_async_copy(ybuf.at[rows_of(c)], results.at[rows_of(c)], res_sems.at[c])

    def column_sum(at, value):
        vectors[at] += jnp.sum(value, axis=0, keepdims=True)

    def norm_forward(e):
        mean = jnp.mean(e, axis=-1, keepdims=True)
        center = e - mean
        s = lax.rsqrt(jnp.mean(center * center, axis=-1, keepdims=True) + EPSILON)
        return center * s, s

    def norm_backward(dn, n, s):
        m1 = jnp.mean(dn, axis=-1, keepdims=True)
        m2 = jnp.mean(dn * n, axis=-1, keepdims=True)
        return s * (dn - m1 - n * m2)

    def pair_columns(hp):
        return [pl.ds(pl.multiple_of(i * width + hp * PAIR, PAIR), PAIR) for i in range(3)]

    def attend(c, wide):
        rows = rows_of(c)
        tiles = [(rows, near)] + ([(rows_of(c - 1), far)] if wide else [])
        m = [masks[a].astype(BF16) for a in range(2)]

        def one_pair(hp, _):
            cq, ck, cv = pair_columns(hp)
            q = qkv[rows, cq]
            nz = None
            for key_rows, weights in tiles:
                k, v = qkv[key_rows, ck], qkv[key_rows, cv]
                for a in range(2):
                    s = (dot_nt(q * m[a], k) * weights[...]).astype(BF16)
                    right = jnp.concatenate(
                        [v * m[a], jnp.broadcast_to(m[a], v.shape)], axis=1
                    )
                    part = dot(s, right)
                    nz = part if nz is None else nz + part
            inverse = 1.0 / nz[:, PAIR:]
            a_full = nz[:, :PAIR] * inverse
            a_high = a_full.astype(BF16)
            att[rows, cq] = a_high
            low[rows, cq] = (a_full - a_high.astype(F32)).astype(BF16)
            zin[rows, cq] = inverse.astype(BF16)
            return 0

        lax.fori_loop(0, pairs, one_pair, 0, unroll=True)

    def attend_backward(c, wide):
        rows = rows_of(c)
        m = [masks[a].astype(BF16) for a in range(2)]
        left = lax.broadcasted_iota(jnp.int32, (CHUNK, PAIR), 1) < HEAD

        def one_pair(hp, _):
            cq, ck, cv = pair_columns(hp)
            q, k, v = qkv[rows, cq], qkv[rows, ck], qkv[rows, cv]
            dn = (das[:, cq].astype(F32) * zin[rows, cq].astype(F32)).astype(BF16)
            prod = dn.astype(F32) * (att[rows, cq].astype(F32) + low[rows, cq].astype(F32))
            dz = jnp.concatenate(
                [-jnp.sum(prod * masks[a], axis=-1, keepdims=True) for a in range(2)], axis=0
            )
            both_q = jnp.concatenate([q * m[a] for a in range(2)], axis=0)
            both_dn = jnp.concatenate([dn * m[a] for a in range(2)], axis=0)

            def tile(kt, vt, weights):
                w = jnp.concatenate([weights[...]] * 2, axis=0)
                s = (dot_nt(both_q, kt) * w).astype(BF16)
                ds = ((dot_nt(both_dn, vt) + dz) * w).astype(BF16)
                dq2 = dot(ds, kt)
                dq = jnp.where(left, dq2[:CHUNK], dq2[CHUNK:])
                return dq, dot_tn(ds, both_q), dot_tn(s, both_dn)

            dq, dk, dv = tile(k, v, near)
            wide_cols = [pl.ds(pl.multiple_of(i * width + hp * PAIR, PAIR), PAIR) for i in range(2)]
            if wide:
                kp, vp = qkv[rows_of(c - 1), ck], qkv[rows_of(c - 1), cv]
                dqp, dkp, dvp = tile(kp, vp, far)
                dq = dq + dqp
                carry[:, wide_cols[0]] = dkp
                carry[:, wide_cols[1]] = dvp
            else:
                dk = dk + carry[:, wide_cols[0]]
                dv = dv + carry[:, wide_cols[1]]
            qkv[rows, cq] = (dq * sigmoid_of_softplus(q.astype(F32))).astype(BF16)
            qkv[rows, ck] = (dk * sigmoid_of_softplus(k.astype(F32))).astype(BF16)
            qkv[rows, cv] = dv.astype(BF16)
            return 0

        lax.fori_loop(0, pairs, one_pair, 0, unroll=True)

    def forward(c, begins):
        rows = rows_of(c)

        @pl.when(begins)
        def _():
            @pl.when(first)
            def _():
                load_x.wait()

            for load in loads[:3]:
                load.wait()
            for load in loads[3:]:
                load.start()

        @pl.when(jnp.logical_not(first))
        def _():
            send_forward(c).wait_recv()

        for i in range(3):
            cols = slice(i * width, (i + 1) * width)
            p = dot(xs[rows, :], held[w_in + i]) + inbias[:, cols]
            qkv[rows, cols] = (softplus(p) if i < 2 else p).astype(BF16)

        @pl.when(c % 2 == 0)
        def _():
            attend(c, False)

        @pl.when(c % 2 == 1)
        def _():
            attend(c, True)

        @pl.when(begins)
        def _():
            for load in loads[3:]:
                load.wait()

        e = xs[rows, :].astype(F32) + (dot(att[rows, :], held[w_out]) + outbias[...])
        n1, s1 = norm_forward(e)
        n1s[rows, :] = n1.astype(BF16)
        s1s[rows, :] = s1
        h = n1 * normgain[...] + normshift[...]
        hbs[rows, :] = h.astype(BF16)
        acc[...] = h + shrbias[...]
        for i in range(slabs):
            cols = slice(i * width, (i + 1) * width)
            u = dot(hbs[rows, :], held[w_up + i]) + expbias[:, cols]
            phi = 0.5 * (1.0 + lax.erf(u * math.sqrt(0.5)))
            g = (u * phi).astype(BF16)
            gs[rows, cols] = g
            gps[rows, cols] = (
                phi + u * (jnp.exp(u * u * -0.5) * (1.0 / math.sqrt(2.0 * math.pi)))
            ).astype(BF16)
            acc[...] += dot(g, held[w_down + i])
        n2, s2 = norm_forward(acc[...])
        n2s[rows, :] = n2.astype(BF16)
        s2s[rows, :] = s2
        ybuf[rows, :] = (n2 * lastgain[...] + lastshift[...]).astype(BF16)

        @pl.when(first)
        def _():
            send_forward(c).start()

        @pl.when(jnp.logical_not(first))
        def _():
            result_copy(c).start()

    def backward(c, ends):
        rows = rows_of(c)

        @pl.when(first)
        def _():
            send_backward(c).wait_recv()

        @pl.when(jnp.logical_and(jnp.logical_not(first), c == 1))
        def _():
            load_y.wait()

        dy = dys[rows, :].astype(F32)
        n2 = n2s[rows, :].astype(F32)
        column_sum(7 + slabs, dy * n2)
        column_sum(8 + slabs, dy)
        dr = norm_backward(dy * lastgain[...], n2, s2s[rows, :])
        df = dr.astype(BF16)
        n2s[rows, :] = df
        column_sum(6 + slabs, df.astype(F32))
        acc[...] = dr
        for i in range(slabs):
            cols = slice(i * width, (i + 1) * width)
            dg = dot_nt(n2s[rows, :], held[w_down + i])
            du = (dg * gps[rows, cols].astype(F32)).astype(BF16)
            gps[rows, cols] = du
            column_sum(6 + i, du.astype(F32))
            acc[...] += dot_nt(du, held[w_up + i])
        if merged:
            @pl.when(ends)
            def _():
                reduction.free(0)

                @pl.when(first)
                def _():
                    reduction.begin()

        dh = acc[...]
        n1 = n1s[rows, :].astype(F32)
        column_sum(4, dh * n1)
        column_sum(5, dh)
        de = norm_backward(dh * normgain[...], n1, s1s[rows, :])
        keep[...] = de
        do = de.astype(BF16)
        n1s[rows, :] = do
        column_sum(3, do.astype(F32))
        das[...] = dot_nt(do, held[w_out]).astype(BF16)

        @pl.when(c % 2 == 0)
        def _():
            attend_backward(c, False)

        @pl.when(c % 2 == 1)
        def _():
            attend_backward(c, True)

        for i in range(3):
            column_sum(i, qkv[rows, i * width : (i + 1) * width].astype(F32))
        dx = keep[...]
        for i in range(3):
            dx += dot_nt(qkv[rows, i * width : (i + 1) * width], held[w_in + i])

        @pl.when(first)
        def _():
            send_forward(c).wait_send()

        @pl.when(jnp.logical_not(first))
        def _():
            result_copy(c).wait()

        ybuf[rows, :] = dx.astype(BF16)

        @pl.when(first)
        def _():
            result_copy(c).start()

        @pl.when(jnp.logical_not(first))
        def _():
            send_backward(c).start()

    def step(t, _):
        group, place = t // 4, t % 4
        ahead = jnp.where(first, t < chunks, place < 2)
        c_forward = jnp.where(first, t, 2 * group + place)
        back = t - chunks
        c_backward = jnp.where(first, 2 * (back // 2) + 1 - back % 2, 2 * group + 3 - place)

        @pl.when(ahead)
        def _():
            forward(c_forward, t == 0)

        @pl.when(jnp.logical_not(ahead))
        def _():
            backward(c_backward, t == 2 * chunks - 1)

        return 0

    lax.fori_loop(0, 2 * chunks, step, 0)
    if merged:
        reduction.free(1)

        @pl.when(jnp.logical_not(first))
        def _():
            reduction.begin()

        reduction.run()
    else:
        f_x, f_a, f_h, f_g, f_p, f_o, f_u, f_f, vector_rows = outputs
        (out_sems,) = take(1)
        for i in range(vectors.shape[0]):
            vector_rows[i : i + 1, :] = vectors[i]
        pairs_out = [
            (xs, f_x), (att, f_a), (hbs, f_h), (gs, f_g), (qkv, f_p), (n1s, f_o), (gps, f_u),
            (n2s, f_f),
        ]
        copies = [
            pltpu.make_async_copy(src, dst, out_sems.at[i])
            for i, (src, dst) in enumerate(pairs_out)
        ]
        for copy in copies:
            copy.start()
        for copy in copies:
            copy.wait()

    def finish(c, _):
        @pl.when(first)
        def _():
            result_copy(c).wait()

        @pl.when(jnp.logical_not(first))
        def _():
            send_backward(c).wait_send()

        return 0

    lax.fori_loop(0, chunks, finish, 0)


def run_layer(merged, boundary, weights, biases):
    rows, width = boundary.shape
    hidden = weights[2].shape[1]
    chunks = rows // CHUNK
    near, far = cosine_tables()
    slabs = hidden // width
    blocks = 4 + 2 * slabs
    sets = blocks // 2 * SETS
    piece = width // SETS // 8
    any_space = pl.BlockSpec(memory_space=pl.ANY)
    vmem = pl.BlockSpec(memory_space=pltpu.VMEM)
    vector_count = -(-(9 + slabs) // 8) * 8
    low = lambda *shape: pltpu.VMEM(shape, BF16)
    wide = lambda *shape: pltpu.VMEM(shape, F32)
    dma = lambda *shape: pltpu.SemaphoreType.DMA(shape)
    small = list(biases) + [jnp.asarray(near), jnp.asarray(far), jnp.asarray(lane_masks())]
    scratch = [pltpu.VMEM(value.shape, F32) for value in small] + [
        low(blocks, width, width),
        low(rows, width), low(rows, 3 * width), low(rows, width), low(rows, width),
        low(rows, width), low(rows, width), low(rows, hidden), low(rows, hidden),
        low(rows, width), low(rows, width), wide(rows, 1), wide(rows, 1),
        low(rows, width), low(rows, width),
        wide(CHUNK, width), wide(CHUNK, width), low(CHUNK, width), wide(CHUNK, 2 * width),
        wide(vector_count, 1, width),
        dma(blocks + 1), dma(len(small)), dma(chunks), dma(chunks), dma(chunks), dma(chunks),
        dma(chunks),
    ]
    vector_shape = jax.ShapeDtypeStruct((vector_count, width), F32)
    if merged:
        rest = [jax.ShapeDtypeStruct((blocks, width, width), BF16), vector_shape]
        rest_specs = [any_space, vmem]
        scratch += [
            low(STAGES, 2, width // SETS, width),
            low(sets, 2, 2 * piece, width), low(sets, 2, piece, width),
            low(sets, 2, piece, width), low(sets, piece, width),
            wide(5, vector_count, width), wide(4, vector_count, width),
            dma(sets), dma(sets), dma(sets, 2), dma(sets, 2), dma(sets, 2), dma(sets, 2),
            dma(sets, 2), dma(sets, 2), dma(sets), dma(sets),
            dma(sets, 2, 4), dma(sets, 2, 3), dma(sets, 2, 2), dma(sets, 2, 2), dma(sets, 2),
            dma(sets, 2), dma(5), dma(4), pltpu.SemaphoreType.REGULAR((2,)),
        ]
    else:
        widths = [width] * 3 + [hidden, 3 * width, width, hidden, width]
        rest = [jax.ShapeDtypeStruct((rows, w), BF16) for w in widths] + [vector_shape]
        rest_specs = [any_space] * 8 + [vmem]
        scratch += [dma(8)]
    return pl.pallas_call(
        partial(layer_kernel, merged),
        out_shape=[jax.ShapeDtypeStruct((rows, width), BF16)] + rest,
        in_specs=[any_space] * (5 + len(small)),
        out_specs=[any_space] + rest_specs,
        scratch_shapes=scratch,
        compiler_params=pltpu.CompilerParams(
            collective_id=0, has_side_effects=True, vmem_limit_bytes=VMEM_BYTES
        ),
        name="layer",
    )(boundary, *weights, *small)


def widen_kernel(slabs, total, vec, low_results, *refs):
    outs, results = refs[:12], refs[12]
    low, high, held, in_sems, out_sems, side_sems = refs[13:]
    blocks, width, _ = total.shape
    inward, outward, expand, shrink = outs[:4]

    def reads(i):
        return pltpu.make_async_copy(total.at[i], low.at[i], in_sems.at[i])

    def place(i):
        if i < slabs:
            return shrink.at[pl.ds(i * width, width)]
        if i < 2 * slabs:
            return expand.at[:, pl.ds((i - slabs) * width, width)]
        if i == 2 * slabs:
            return outward
        return inward.at[:, pl.ds((i - 2 * slabs - 1) * width, width)]

    def writes(i):
        return pltpu.make_async_copy(high.at[i], place(i), out_sems.at[i])

    side_in = pltpu.make_async_copy(low_results, held, side_sems.at[0])
    side_out = pltpu.make_async_copy(held, results, side_sems.at[1])
    for i in range(blocks):
        reads(i).start()
    side_in.start()
    row = 0
    for out in outs[4:]:
        for i in range(out.shape[1] // width):
            out[:, i * width : (i + 1) * width] = vec[row : row + 1, :]
            row += 1
    for i in range(blocks):
        reads(i).wait()

        def part(r, _):
            rows = pl.ds(pl.multiple_of(r * 64, 64), 64)
            high[i, rows] = low[i, rows].astype(F32)
            return 0

        lax.fori_loop(0, width // 64, part, 0)
        writes(i).start()
    side_in.wait()
    side_out.start()
    for i in range(blocks):
        writes(i).wait()
    side_out.wait()


def widen(total, vec, low_results, hidden):
    blocks, width, _ = total.shape
    slabs = hidden // width
    shapes = [(width, 3 * width), (width, width), (width, hidden), (hidden, width)]
    lengths = [3 * width, width, width, width, hidden, width, width, width]
    any_space = pl.BlockSpec(memory_space=pl.ANY)
    vmem = pl.BlockSpec(memory_space=pltpu.VMEM)
    dma = lambda *shape: pltpu.SemaphoreType.DMA(shape)
    return pl.pallas_call(
        partial(widen_kernel, slabs),
        out_shape=[jax.ShapeDtypeStruct(shape, F32) for shape in shapes]
        + [jax.ShapeDtypeStruct((1, n), F32) for n in lengths]
        + [jax.ShapeDtypeStruct(low_results.shape, BF16)],
        in_specs=[any_space, vmem, any_space],
        out_specs=[any_space] * 4 + [vmem] * 8 + [any_space],
        scratch_shapes=[
            pltpu.VMEM((blocks, width, width), BF16), pltpu.VMEM((blocks, width, width), F32),
            pltpu.VMEM(low_results.shape, BF16), dma(blocks), dma(blocks), dma(2),
        ],
        compiler_params=pltpu.CompilerParams(vmem_limit_bytes=VMEM_BYTES),
        name="widen",
    )(total, vec, low_results)


def shards(
    boundary, inward, inbias, outward, outbias, normgain, normshift, expand, expbias,
    shrink, shrbias, lastgain, lastshift,
):
    width = outward.shape[-1]
    hidden = expand.shape[-1]
    slabs = hidden // width
    merged = lax.axis_size("dp") == 4 * LANES_Z
    results, *rest = run_layer(
        merged,
        boundary[0],
        (inward[0], outward[0], expand[0], shrink[0]),
        (inbias, outbias, normgain, normshift, expbias, shrbias, lastgain, lastshift),
    )
    if merged:
        total, vec = rest
        widened = widen(total, vec, results, hidden)
        matrices, pieces, results = widened[:4], widened[4:12], widened[12]
    else:
        f_x, f_a, f_h, f_g, f_p, f_o, f_u, f_f, vectors = rest

        def summed(left, right):
            grad = dot_tn(left, right).astype(BF16)
            mine = lax.psum_scatter(grad, "dp", scatter_dimension=0, tiled=True)
            return lax.all_gather(mine, "dp", axis=0, tiled=True).astype(F32)

        matrices = [summed(f_x, f_p), summed(f_a, f_o), summed(f_h, f_u), summed(f_g, f_f)]
        vec = lax.psum(vectors, "dp")
        pieces, row = [], 0
        for count in (3, 1, 1, 1, slabs, 1, 1, 1):
            pieces.append(vec[row : row + count].reshape(1, count * width))
            row += count

    inward_grad, outward_grad, expand_grad, shrink_grad = (m[None] for m in matrices)
    return (
        results[None],
        inward_grad, pieces[0], outward_grad, pieces[1], pieces[2], pieces[3],
        expand_grad, pieces[4], shrink_grad, pieces[5], pieces[6], pieces[7],
    )


def solution(mesh):
    matrix, vector = P("section", None, None), P("section", None)
    params = (
        matrix, vector, matrix, vector, vector, vector, matrix, vector, matrix, vector,
        vector, vector,
    )
    specs = (P("section", "dp", None),) + params
    return jax.shard_map(shards, mesh=mesh, in_specs=specs, out_specs=specs, check_vma=False)
```

```python
from functools import partial
import math

import jax
import jax.numpy as jnp
import numpy as np
from jax import lax
from jax.experimental import pallas as pl
from jax.experimental.pallas import tpu as pltpu
from jax.sharding import PartitionSpec as P

HEAD = 64
SEQ = 512
CHUNK = 256
PAIR = 2 * HEAD
EPSILON = 1e-05
MESH = pl.DeviceIdType.MESH
F32 = jnp.float32
BF16 = jnp.bfloat16
VMEM_BYTES = 63 * 2**20
LAYER_VMEM = 63 * 2**20
GRADIENT_VMEM = 46 * 2**20
WIDEN_VMEM = 34 * 2**20


def dot(a, b):
    return jnp.dot(a, b, preferred_element_type=F32)


def dot_nt(a, b):
    return lax.dot_general(a, b, (((1,), (1,)), ((), ())), preferred_element_type=F32)


def dot_tn(a, b):
    return lax.dot_general(a, b, (((0,), (0,)), ((), ())), preferred_element_type=F32)


def softplus(p):
    return jnp.maximum(p, 0.0) + jnp.log1p(jnp.exp(-jnp.abs(p)))


def sigmoid_of_softplus(q):
    series = q * (1.0 - q * (0.5 - q * (1.0 / 6.0 - q * (1.0 / 24.0))))
    return jnp.where(q < 0.03, series, 1.0 - jnp.exp(-q))


def cosine_tables():
    step = math.pi / (2.0 * SEQ)
    i = np.arange(CHUNK)[:, None]
    j = np.arange(CHUNK)[None, :]
    near = np.where(i >= j, np.cos((i - j) * step), 0.0).astype(np.float32)
    far = np.cos((i - j + CHUNK) * step).astype(np.float32)
    return near, far


def lane_masks():
    lanes = np.arange(PAIR)
    return np.stack([lanes < HEAD, lanes >= HEAD])[:, None, :].astype(np.float32)


def layer_kernel(
    boundary, inward, outward, expand, shrink,
    inbias, outbias, normgain, normshift, expbias, shrbias, lastgain, lastshift,
    near, far, masks,
    results, f_x, f_a, f_h, f_g, f_p, f_o, f_u, f_f, vector_rows,
    win, wout, wexp, wshr,
    xs, qkv, att, low, zin, hbs, gs, gps, n1s, n2s, scales, dys, ybuf,
    acc, keep, das, carry, vectors,
    load_sems, out_sems, res_sems, fwd_send, fwd_recv, bwd_send, bwd_recv,
):
    rows_all, width = xs.shape
    hidden = wexp.shape[1]
    chunks = rows_all // CHUNK
    pairs = width // PAIR
    slabs = hidden // width
    section = lax.axis_index("section")
    first = section == 0
    peer = {"section": 1 - section}

    loads = [
        pltpu.make_async_copy(src, dst, load_sems.at[i])
        for i, (src, dst) in enumerate(
            [(inward, win), (outward, wout), (expand, wexp), (shrink, wshr)]
        )
    ]
    load_x = pltpu.make_async_copy(boundary, xs, load_sems.at[4])
    load_y = pltpu.make_async_copy(boundary, dys, load_sems.at[4])

    loads[0].start()

    @pl.when(first)
    def _():
        load_x.start()

    @pl.when(jnp.logical_not(first))
    def _():
        load_y.start()

    barrier = pltpu.get_barrier_semaphore()
    pl.semaphore_signal(barrier, inc=1, device_id=peer, device_id_type=MESH)
    vectors[...] = jnp.zeros_like(vectors)
    pl.semaphore_wait(barrier, 1)

    def rows_of(c):
        return pl.ds(pl.multiple_of(c * CHUNK, CHUNK), CHUNK)

    def send_forward(c):
        return pltpu.make_async_remote_copy(
            src_ref=ybuf.at[rows_of(c)], dst_ref=xs.at[rows_of(c)],
            send_sem=fwd_send.at[c], recv_sem=fwd_recv.at[c],
            device_id=peer, device_id_type=MESH,
        )

    def send_backward(c):
        return pltpu.make_async_remote_copy(
            src_ref=ybuf.at[rows_of(c)], dst_ref=dys.at[rows_of(c)],
            send_sem=bwd_send.at[c], recv_sem=bwd_recv.at[c],
            device_id=peer, device_id_type=MESH,
        )

    def result_copy(c):
        return pltpu.make_async_copy(ybuf.at[rows_of(c)], results.at[rows_of(c)], res_sems.at[c])

    early = [(xs, f_x), (att, f_a), (hbs, f_h)]
    late = [(qkv, f_p), (n1s, f_o), (gps, f_u), (n2s, f_f)]

    def factor_copies(c, which, base):
        return [
            pltpu.make_async_copy(src.at[rows_of(c)], dst.at[rows_of(c)], out_sems.at[c, base + i])
            for i, (src, dst) in enumerate(which)
        ]

    def active_copy(c):
        return pltpu.make_async_copy(gs.at[c % 2], f_g.at[rows_of(c)], out_sems.at[c, 3])

    def column_sum(at, value):
        vectors[at] += jnp.sum(value, axis=0, keepdims=True)

    def norm_forward(e):
        mean = jnp.mean(e, axis=-1, keepdims=True)
        center = e - mean
        s = lax.rsqrt(jnp.mean(center * center, axis=-1, keepdims=True) + EPSILON)
        return center * s, s

    def norm_backward(dn, n, s):
        m1 = jnp.mean(dn, axis=-1, keepdims=True)
        m2 = jnp.mean(dn * n, axis=-1, keepdims=True)
        return s * (dn - m1 - n * m2)

    def pair_columns(hp):
        return [pl.ds(pl.multiple_of(i * width + hp * PAIR, PAIR), PAIR) for i in range(3)]

    def attend(c, wide):
        rows = rows_of(c)
        tiles = [(rows, near)] + ([(rows_of(c - 1), far)] if wide else [])
        m = [masks[a].astype(BF16) for a in range(2)]

        def one_pair(hp, _):
            cq, ck, cv = pair_columns(hp)
            q = qkv[rows, cq]
            nz = None
            for key_rows, weights in tiles:
                k, v = qkv[key_rows, ck], qkv[key_rows, cv]
                for a in range(2):
                    s = (dot_nt(q * m[a], k) * weights[...]).astype(BF16)
                    right = jnp.concatenate(
                        [v * m[a], jnp.broadcast_to(m[a], v.shape)], axis=1
                    )
                    part = dot(s, right)
                    nz = part if nz is None else nz + part
            inverse = 1.0 / nz[:, PAIR:]
            a_full = nz[:, :PAIR] * inverse
            a_high = a_full.astype(BF16)
            att[rows, cq] = a_high
            low[rows, cq] = (a_full - a_high.astype(F32)).astype(BF16)
            zin[rows, cq] = inverse.astype(BF16)
            return 0

        lax.fori_loop(0, pairs, one_pair, 0, unroll=True)

    def attend_backward(c, wide):
        rows = rows_of(c)
        m = [masks[a].astype(BF16) for a in range(2)]
        left = lax.broadcasted_iota(jnp.int32, (CHUNK, PAIR), 1) < HEAD

        def one_pair(hp, _):
            cq, ck, cv = pair_columns(hp)
            q, k, v = qkv[rows, cq], qkv[rows, ck], qkv[rows, cv]
            dn = (das[:, cq].astype(F32) * zin[rows, cq].astype(F32)).astype(BF16)
            prod = dn.astype(F32) * (att[rows, cq].astype(F32) + low[rows, cq].astype(F32))
            dz = jnp.concatenate(
                [-jnp.sum(prod * masks[a], axis=-1, keepdims=True) for a in range(2)], axis=0
            )
            both_q = jnp.concatenate([q * m[a] for a in range(2)], axis=0)
            both_dn = jnp.concatenate([dn * m[a] for a in range(2)], axis=0)

            def tile(kt, vt, weights):
                w = jnp.concatenate([weights[...]] * 2, axis=0)
                s = (dot_nt(both_q, kt) * w).astype(BF16)
                ds = ((dot_nt(both_dn, vt) + dz) * w).astype(BF16)
                dq2 = dot(ds, kt)
                dq = jnp.where(left, dq2[:CHUNK], dq2[CHUNK:])
                return dq, dot_tn(ds, both_q), dot_tn(s, both_dn)

            dq, dk, dv = tile(k, v, near)
            wide_cols = [pl.ds(pl.multiple_of(i * width + hp * PAIR, PAIR), PAIR) for i in range(2)]
            if wide:
                kp, vp = qkv[rows_of(c - 1), ck], qkv[rows_of(c - 1), cv]
                dqp, dkp, dvp = tile(kp, vp, far)
                dq = dq + dqp
                carry[:, wide_cols[0]] = dkp
                carry[:, wide_cols[1]] = dvp
            else:
                dk = dk + carry[:, wide_cols[0]]
                dv = dv + carry[:, wide_cols[1]]
            qkv[rows, cq] = (dq * sigmoid_of_softplus(q.astype(F32))).astype(BF16)
            qkv[rows, ck] = (dk * sigmoid_of_softplus(k.astype(F32))).astype(BF16)
            qkv[rows, cv] = dv.astype(BF16)
            return 0

        lax.fori_loop(0, pairs, one_pair, 0, unroll=True)

    def forward(c, begins):
        rows = rows_of(c)

        @pl.when(begins)
        def _():
            loads[0].wait()

            @pl.when(first)
            def _():
                load_x.wait()

            for load in loads[1:]:
                load.start()

        @pl.when(jnp.logical_not(first))
        def _():
            send_forward(c).wait_recv()

        for i in range(3):
            cols = slice(i * width, (i + 1) * width)
            p = dot(xs[rows, :], win[:, cols]) + inbias[:, cols]
            qkv[rows, cols] = (softplus(p) if i < 2 else p).astype(BF16)

        @pl.when(c % 2 == 0)
        def _():
            attend(c, False)

        @pl.when(c % 2 == 1)
        def _():
            attend(c, True)

        @pl.when(begins)
        def _():
            for load in loads[1:]:
                load.wait()

        e = xs[rows, :].astype(F32) + (dot(att[rows, :], wout[...]) + outbias[...])
        n1, s1 = norm_forward(e)
        n1s[rows, :] = n1.astype(BF16)
        scales[rows, 0:1] = s1
        h = n1 * normgain[...] + normshift[...]
        hbs[rows, :] = h.astype(BF16)

        @pl.when(c >= 2)
        def _():
            active_copy(c - 2).wait()

        acc[...] = h + shrbias[...]
        for i in range(slabs):
            cols = slice(i * width, (i + 1) * width)
            u = dot(hbs[rows, :], wexp[:, cols]) + expbias[:, cols]
            phi = 0.5 * (1.0 + lax.erf(u * math.sqrt(0.5)))
            g = (u * phi).astype(BF16)
            gs[c % 2, :, cols] = g
            gps[rows, cols] = (
                phi + u * (jnp.exp(u * u * -0.5) * (1.0 / math.sqrt(2.0 * math.pi)))
            ).astype(BF16)
            acc[...] += dot(g, wshr[cols, :])
        n2, s2 = norm_forward(acc[...])
        n2s[rows, :] = n2.astype(BF16)
        scales[rows, 1:2] = s2
        ybuf[rows, :] = (n2 * lastgain[...] + lastshift[...]).astype(BF16)

        @pl.when(first)
        def _():
            send_forward(c).start()

        @pl.when(jnp.logical_not(first))
        def _():
            result_copy(c).start()

        for copy in factor_copies(c, early, 0) + [active_copy(c)]:
            copy.start()

    def backward(c):
        rows = rows_of(c)

        @pl.when(first)
        def _():
            send_backward(c).wait_recv()

        @pl.when(jnp.logical_and(jnp.logical_not(first), c == 1))
        def _():
            load_y.wait()

        dy = dys[rows, :].astype(F32)
        n2 = n2s[rows, :].astype(F32)
        column_sum(7 + slabs, dy * n2)
        column_sum(8 + slabs, dy)
        dr = norm_backward(dy * lastgain[...], n2, scales[rows, 1:2])
        df = dr.astype(BF16)
        n2s[rows, :] = df
        column_sum(6 + slabs, df.astype(F32))
        acc[...] = dr
        for i in range(slabs):
            cols = slice(i * width, (i + 1) * width)
            dg = dot_nt(n2s[rows, :], wshr[cols, :])
            du = (dg * gps[rows, cols].astype(F32)).astype(BF16)
            gps[rows, cols] = du
            column_sum(6 + i, du.astype(F32))
            acc[...] += dot_nt(du, wexp[:, cols])
        dh = acc[...]
        n1 = n1s[rows, :].astype(F32)
        column_sum(4, dh * n1)
        column_sum(5, dh)
        de = norm_backward(dh * normgain[...], n1, scales[rows, 0:1])
        keep[...] = de
        do = de.astype(BF16)
        n1s[rows, :] = do
        column_sum(3, do.astype(F32))
        das[...] = dot_nt(do, wout[...]).astype(BF16)

        @pl.when(c % 2 == 0)
        def _():
            attend_backward(c, False)

        @pl.when(c % 2 == 1)
        def _():
            attend_backward(c, True)

        for i in range(3):
            column_sum(i, qkv[rows, i * width : (i + 1) * width].astype(F32))
        dx = keep[...] + dot_nt(qkv[rows, :], win[...])

        @pl.when(first)
        def _():
            send_forward(c).wait_send()

        @pl.when(jnp.logical_not(first))
        def _():
            result_copy(c).wait()

        ybuf[rows, :] = dx.astype(BF16)

        @pl.when(first)
        def _():
            result_copy(c).start()

        @pl.when(jnp.logical_not(first))
        def _():
            send_backward(c).start()

        for copy in factor_copies(c, late, 4):
            copy.start()

    def step(t, _):
        group, place = t // 4, t % 4
        ahead = jnp.where(first, t < chunks, place < 2)
        c_forward = jnp.where(first, t, 2 * group + place)
        back = t - chunks
        c_backward = jnp.where(first, 2 * (back // 2) + 1 - back % 2, 2 * group + 3 - place)

        @pl.when(ahead)
        def _():
            forward(c_forward, t == 0)

        @pl.when(jnp.logical_not(ahead))
        def _():
            backward(c_backward)

        return 0

    lax.fori_loop(0, 2 * chunks, step, 0)
    for i in range(vectors.shape[0]):
        vector_rows[i : i + 1, :] = vectors[i]

    def finish(c, _):
        @pl.when(first)
        def _():
            result_copy(c).wait()

        @pl.when(jnp.logical_not(first))
        def _():
            send_backward(c).wait_send()

        for copy in factor_copies(c, early, 0) + factor_copies(c, late, 4):
            copy.wait()

        @pl.when(c >= chunks - 2)
        def _():
            active_copy(c).wait()

        return 0

    lax.fori_loop(0, chunks, finish, 0)


def run_layer(boundary, weights, biases):
    rows, width = boundary.shape
    hidden = weights[2].shape[1]
    chunks = rows // CHUNK
    near, far = cosine_tables()
    masks = lane_masks()
    slabs = hidden // width
    any_space = pl.BlockSpec(memory_space=pl.ANY)
    vmem = pl.BlockSpec(memory_space=pltpu.VMEM)
    out_widths = [width] * 4 + [hidden, 3 * width, width, hidden, width]
    out_shape = [jax.ShapeDtypeStruct((rows, w), BF16) for w in out_widths]
    vector_count = -(-(9 + slabs) // 8) * 8
    out_shape.append(jax.ShapeDtypeStruct((vector_count, width), F32))
    low = lambda *shape: pltpu.VMEM(shape, BF16)
    wide = lambda *shape: pltpu.VMEM(shape, F32)
    dma = pltpu.SemaphoreType.DMA
    return pl.pallas_call(
        layer_kernel,
        out_shape=out_shape,
        in_specs=[any_space] * 5 + [vmem] * 11,
        out_specs=[any_space] * 9 + [vmem],
        scratch_shapes=[
            low(width, 3 * width), low(width, width), low(width, hidden), low(hidden, width),
            low(rows, width), low(rows, 3 * width), low(rows, width), low(rows, width),
            low(rows, width), low(rows, width), low(2, CHUNK, hidden), low(rows, hidden),
            low(rows, width), low(rows, width), wide(rows, 2),
            low(rows, width), low(rows, width),
            wide(CHUNK, width), wide(CHUNK, width), low(CHUNK, width), wide(CHUNK, 2 * width),
            wide(vector_count, 1, width),
            dma((5,)), dma((chunks, 8)), dma((chunks,)), dma((chunks,)), dma((chunks,)),
            dma((chunks,)), dma((chunks,)),
        ],
        compiler_params=pltpu.CompilerParams(
            collective_id=0, has_side_effects=True, vmem_limit_bytes=LAYER_VMEM
        ),
        name="layer",
    )(boundary, *weights, *biases, jnp.asarray(near), jnp.asarray(far), jnp.asarray(masks))


SETS = 2
LANES_Z = 4
STAGES = 3

ARRIVE_Y = 2
PAIR_AT = (0, 2, 3, 13)
ONE_AT = (0, 3, 4, 17)
LAST_ONE, LAST_PAIR, LAST_CROSS = 21, 20, 21
BACK_AT = (0, 20, 21, 24)
OUT_AT = (22, 22, 22, 25)


def gradient_kernel(
    f_x, f_a, f_h, f_g, f_p, f_o, f_u, f_f, vec_in,
    total, vec_out,
    x, a, h, g, p, o, u, f,
    own, stage, core_in, chain_pair, chain_one, y_in, end_in, vec, vec_got,
    load_sems, core_s, core_r, y_s, y_r, pair_s, pair_r, one_s, one_r, end_s, end_r,
    got, z_s, yy_s, kept, out_s, out_r, vec_s, vec_r, credit,
):
    width = x.shape[1]
    slabs = g.shape[1] // width
    me = lax.axis_index("dp")
    core, y, z = me % 2, (me // 2) % 2, me // 4
    last = LANES_Z - 1
    core_peer, y_peer = {"dp": me + 1 - 2 * core}, {"dp": me + 2 - 4 * y}
    hop = [last - z, z]
    ahead = [{"dp": me - 4}, {"dp": me + 4}]
    behind = [ahead[1], ahead[0]]

    blocks = (
        [(a, 0, o, 0)]
        + [(x, 0, p, i) for i in range(3)]
        + [(h, 0, u, i) for i in range(slabs)]
        + [(g, i, f, 0) for i in range(slabs)]
    )
    duos = len(blocks) // 2
    sets = duos * SETS
    set_rows = width // SETS
    half = set_rows // 2
    piece = half // 4

    sources = [(f_a, a), (f_o, o), (f_x, x), (f_p, p), (f_h, h), (f_u, u), (f_f, f), (f_g, g)]
    loads = [
        pltpu.make_async_copy(src, dst, load_sems.at[i]) for i, (src, dst) in enumerate(sources)
    ]
    load_at = {0: (0, 1, 2, 3), 2 * SETS: (4, 5), (2 + slabs // 2) * SETS: (6, 7)}
    for load in loads[:4]:
        load.start()

    barrier = pltpu.get_barrier_semaphore()
    for peer in (core_peer, y_peer):
        pl.semaphore_signal(barrier, inc=1, device_id=peer, device_id_type=MESH)
    for d in range(2):
        @pl.when(hop[d] < last)
        def _():
            pl.semaphore_signal(barrier, inc=1, device_id=ahead[d], device_id_type=MESH)
    pl.semaphore_wait(barrier, jnp.where(jnp.logical_and(z > 0, z < last), 4, 3))

    def remote(src, dst, send, recv, peer):
        return pltpu.make_async_remote_copy(
            src_ref=src, dst_ref=dst, send_sem=send, recv_sem=recv,
            device_id=peer, device_id_type=MESH,
        )

    def span(k, d, first, count):
        start = (k % SETS) * set_rows + d * half + first * piece
        return pl.ds(pl.multiple_of(start, 16), count * piece)

    def mine(k, d, first, count=1):
        return own.at[k // SETS, span(k, d, first, count)]


    def final(k, d, first, count=1):
        return total.at[2 * (k // SETS) + core, span(k, d, first, count)]

    def add(dst, src):
        dst[...] = (dst[...].astype(F32) + src[...].astype(F32)).astype(BF16)

    def core_copy(k):
        return remote(
            stage.at[k % STAGES, 1 - core], core_in.at[k % STAGES], core_s.at[k], core_r.at[k],
            core_peer,
        )

    def y_copy(k, d):
        return remote(mine(k, d, 1 - y), y_in.at[k, d], y_s.at[k, d], y_r.at[k, d], y_peer)

    def pair_copy(k, d):
        return remote(
            mine(k, d, 2, 2), chain_pair.at[k, d], pair_s.at[k, d], pair_r.at[k, d], ahead[d]
        )

    def one_copy(k, d):
        return remote(mine(k, d, y), chain_one.at[k, d], one_s.at[k, d], one_r.at[k, d], ahead[d])

    def end_copy(k, d):
        return remote(mine(k, d, 3 - y), end_in.at[k], end_s.at[k], end_r.at[k], y_peer)

    def spread_z(k, d, b, i, src):
        return remote(src, final(k, d, b), z_s.at[k, d, i], got.at[k, d, b], behind[d])

    def spread_y(k, d, b, i, src):
        return remote(src, final(k, d, b), yy_s.at[k, d, i], got.at[k, d, b], y_peer)

    def keep_copy(k, d, b, i):
        return pltpu.make_async_copy(mine(k, d, b), final(k, d, b), kept.at[k, d, i])

    def out_copy(k, d):
        return remote(
            final(k, d, 0, 4), final(k, d, 0, 4), out_s.at[k, d], out_r.at[k, d], core_peer
        )

    def arrived(k, d, b):
        spread_z(k, d, b, 0, final(k, d, b)).wait_recv()

    outer = jnp.logical_or(z == 0, z == last)
    z_pair = {"dp": me + 4 - 8 * (z % 2)}
    z_mid = {"dp": jnp.where(z == 1, me + 4, me - 4)}
    z_out = {"dp": jnp.where(z == 1, me - 4, me + 4)}

    def vec_copy(i, peer):
        return remote(vec.at[i], vec_got.at[min(i, 3)], vec_s.at[i], vec_r.at[min(i, 3)], peer)

    def compute(k):
        for i in load_at.get(k, ()):
            loads[i].wait()
        if k >= STAGES:
            core_copy(k - STAGES).wait_send()
            pl.semaphore_wait(credit, 1)
        m, at = k // SETS, (k % SETS) * set_rows
        for side in range(2):
            left, i, right, j = blocks[2 * m + side]
            cols = slice(i * width + at, i * width + at + set_rows)
            stage[k % STAGES, side] = dot_tn(
                left[:, cols], right[:, j * width : (j + 1) * width]
            ).astype(BF16)
        core_copy(k).start()

    vec[0] = vec_in[...]
    vec_copy(0, core_peer).start()
    compute(0)
    for load in loads[4:]:
        load.start()

    def feed(t):
        for k in range(1, sets):
            @pl.when(t == k - 1)
            def _():
                compute(k)

        for i, peer in ((1, y_peer), (2, z_pair)):
            @pl.when(t == i)
            def _():
                vec_copy(i - 1, peer).wait_recv()
                vec[i] = vec[i - 1] + vec_got[i - 1]
                vec_copy(i, peer).start()

        @pl.when(t == 3)
        def _():
            vec_copy(2, z_pair).wait_recv()
            vec[3] = vec[2] + vec_got[2]

            @pl.when(jnp.logical_not(outer))
            def _():
                vec_copy(3, z_mid).start()

        @pl.when(jnp.logical_and(t == 4, jnp.logical_not(outer)))
        def _():
            vec_copy(3, z_mid).wait_recv()
            vec[4] = vec[3] + vec_got[3]
            vec_copy(4, z_out).start()
            vec_out[...] = vec[4]

        @pl.when(jnp.logical_and(t == 5, outer))
        def _():
            vec_copy(3, z_mid).wait_recv()
            vec_out[...] = vec_got[3]

        @pl.when(t < sets)
        def _():
            core_copy(t).wait_recv()
            for d in range(2):
                here = stage[t % STAGES, core, d * half : (d + 1) * half].astype(F32)
                there = core_in[t % STAGES, d * half : (d + 1) * half].astype(F32)
                mine(t, d, 0, 4)[...] = (here + there).astype(BF16)
                y_copy(t, d).start()

                @pl.when(hop[d] == 0)
                def _():
                    pair_copy(t, d).start()

            @pl.when(t < sets - STAGES)
            def _():
                pl.semaphore_signal(credit, inc=1, device_id=core_peer, device_id_type=MESH)

    def during(k, more=True):
        return jnp.logical_and(jnp.logical_and(k >= 0, k < sets), more)

    def by_place(place, offsets):
        out = jnp.int32(offsets[0])
        for i, offset in enumerate(offsets[1:], 1):
            out = jnp.where(place == i, offset, out)
        return out

    def arrive_y(t):
        k = t - ARRIVE_Y

        @pl.when(during(k))
        def _():
            for d in range(2):
                y_copy(k, d).wait_recv()
                add(mine(k, d, y), y_in.at[k, d])

                @pl.when(hop[d] == 0)
                def _():
                    one_copy(k, d).start()

    def hop_pair(t):
        for d in range(2):
            k = t - by_place(hop[d], PAIR_AT)

            @pl.when(during(k, hop[d] > 0))
            def _():
                pair_copy(k, d).wait_recv()
                add(mine(k, d, 2, 2), chain_pair.at[k, d])

                @pl.when(hop[d] < last)
                def _():
                    pair_copy(k, d).start()

                @pl.when(hop[d] == last)
                def _():
                    end_copy(k, d).start()

    def hop_one(t):
        for d in range(2):
            k = t - by_place(hop[d], ONE_AT)

            @pl.when(during(k, hop[d] > 0))
            def _():
                one_copy(k, d).wait_recv()
                add(mine(k, d, y), chain_one.at[k, d])

                @pl.when(hop[d] < last)
                def _():
                    one_copy(k, d).start()

    def last_one(t):
        k = t - LAST_ONE
        for d in range(2):
            @pl.when(during(k, hop[d] == last))
            def _():
                spread_z(k, d, y, 0, mine(k, d, y)).start()
                spread_y(k, d, y, 0, mine(k, d, y)).start()
                keep_copy(k, d, y, 0).start()

    def last_pair(t):
        k = t - LAST_PAIR
        for d in range(2):
            @pl.when(during(k, hop[d] == last))
            def _():
                end_copy(k, d).wait_recv()
                add(mine(k, d, 2 + y), end_in.at[k])
                spread_y(k, d, 2 + y, 1, mine(k, d, 2 + y)).start()
                spread_z(k, d, 2 + y, 1 + y, mine(k, d, 2 + y)).start()
                keep_copy(k, d, 2 + y, 1).start()

    def last_cross(t):
        k = t - LAST_CROSS
        for d in range(2):
            @pl.when(during(k, hop[d] == last))
            def _():
                arrived(k, d, 3 - y)
                spread_z(k, d, 3 - y, 2 - y, final(k, d, 3 - y)).start()

    def way_back(t):
        for d in range(2):
            k = t - by_place(last - hop[d], BACK_AT)

            @pl.when(during(k, hop[d] < last))
            def _():
                for i, b in ((0, y), (1, 2), (2, 3)):
                    arrived(k, d, b)

                    @pl.when(hop[d] > 0)
                    def _():
                        spread_z(k, d, b, i, final(k, d, b)).start()

                    if i == 0:
                        spread_y(k, d, b, 0, final(k, d, b)).start()

    def to_core(t):
        for d in range(2):
            k = t - by_place(last - hop[d], OUT_AT)

            @pl.when(during(k))
            def _():
                arrived(k, d, 1 - y)

                @pl.when(hop[d] == last)
                def _():
                    keep_copy(k, d, y, 0).wait()
                    keep_copy(k, d, 2 + y, 1).wait()

                out_copy(k, d).start()

    def tick(t, _):
        for stage in (
            last_one, hop_one, arrive_y, hop_pair, to_core, last_cross, feed, last_pair, way_back
        ):
            stage(t)
        return 0

    lax.fori_loop(0, sets + max(OUT_AT), tick, 0)

    def settle(k, _):
        for d in range(2):
            y_copy(k, d).wait_send()
            out_copy(k, d).wait()
            spread_y(k, d, y, 0, final(k, d, y)).wait_send()

            @pl.when(hop[d] < last)
            def _():
                pair_copy(k, d).wait_send()
                one_copy(k, d).wait_send()

            @pl.when(hop[d] == last)
            def _():
                end_copy(k, d).wait_send()
                spread_y(k, d, 2 + y, 1, final(k, d, 2 + y)).wait_send()

            @pl.when(hop[d] > 0)
            def _():
                for i, b in ((0, y), (1, 2), (2, 3)):
                    spread_z(k, d, b, i, final(k, d, b)).wait_send()

        return 0

    lax.fori_loop(0, sets, settle, 0)
    for k in range(sets - STAGES, sets):
        core_copy(k).wait_send()

    for i in range(3):
        vec_copy(i, core_peer).wait_send()

    @pl.when(jnp.logical_not(outer))
    def _():
        vec_copy(3, z_mid).wait_send()
        vec_copy(4, z_out).wait_send()


def reduce_gradients(factors, vectors):
    rows, width = factors[0].shape
    hidden = factors[3].shape[1]
    blocks = 4 + 2 * (hidden // width)
    duos = blocks // 2
    sets = duos * SETS
    piece = width // SETS // 8
    vmem = pl.BlockSpec(memory_space=pltpu.VMEM)
    low = lambda *shape: pltpu.VMEM(shape, BF16)
    dma = lambda *shape: pltpu.SemaphoreType.DMA(shape)
    any_space = pl.BlockSpec(memory_space=pl.ANY)
    return pl.pallas_call(
        gradient_kernel,
        out_shape=[low(blocks, width, width), jax.ShapeDtypeStruct(vectors.shape, F32)],
        in_specs=[any_space] * 8 + [vmem],
        out_specs=[vmem, vmem],
        scratch_shapes=[low(*factor.shape) for factor in factors]
        + [
            low(duos, width, width), low(STAGES, 2, width // SETS, width),
            low(STAGES, width // SETS, width),
            low(sets, 2, 2 * piece, width), low(sets, 2, piece, width),
            low(sets, 2, piece, width), low(sets, piece, width),
            pltpu.VMEM((5,) + vectors.shape, F32), pltpu.VMEM((4,) + vectors.shape, F32),
            dma(8), dma(sets), dma(sets), dma(sets, 2), dma(sets, 2), dma(sets, 2), dma(sets, 2),
            dma(sets, 2), dma(sets, 2), dma(sets), dma(sets),
            dma(sets, 2, 4), dma(sets, 2, 3), dma(sets, 2, 2), dma(sets, 2, 2), dma(sets, 2),
            dma(sets, 2), dma(5), dma(4), pltpu.SemaphoreType.REGULAR,
        ],
        compiler_params=pltpu.CompilerParams(
            collective_id=1, has_side_effects=True, vmem_limit_bytes=GRADIENT_VMEM
        ),
        name="gradients",
    )(*factors, vectors)


def widen_kernel(slabs, total, vec, low_results, *refs):
    outs, results = refs[:12], refs[12]
    high, held, out_sems, side_sems = refs[13:]
    blocks, width, _ = total.shape
    inward, outward, expand, shrink = outs[:4]

    def place(i):
        if i < 1:
            return outward
        if i < 4:
            return inward.at[:, pl.ds((i - 1) * width, width)]
        if i < 4 + slabs:
            return expand.at[:, pl.ds((i - 4) * width, width)]
        return shrink.at[pl.ds((i - 4 - slabs) * width, width)]

    def writes(i):
        return pltpu.make_async_copy(high.at[i], place(i), out_sems.at[i])

    side_in = pltpu.make_async_copy(low_results, held, side_sems.at[0])
    side_out = pltpu.make_async_copy(held, results, side_sems.at[1])
    side_in.start()
    row = 0
    for out in outs[4:]:
        for i in range(out.shape[1] // width):
            out[:, i * width : (i + 1) * width] = vec[row : row + 1, :]
            row += 1
    for i in range(blocks):
        def part(r, _):
            rows = pl.ds(pl.multiple_of(r * 64, 64), 64)
            high[i, rows] = total[i, rows].astype(F32)
            return 0

        lax.fori_loop(0, width // 64, part, 0)
        writes(i).start()
    side_in.wait()
    side_out.start()
    for i in range(blocks):
        writes(i).wait()
    side_out.wait()


def widen(total, vec, low_results, hidden):
    blocks, width, _ = total.shape
    slabs = hidden // width
    shapes = [(width, 3 * width), (width, width), (width, hidden), (hidden, width)]
    lengths = [3 * width, width, width, width, hidden, width, width, width]
    any_space = pl.BlockSpec(memory_space=pl.ANY)
    vmem = pl.BlockSpec(memory_space=pltpu.VMEM)
    dma = lambda *shape: pltpu.SemaphoreType.DMA(shape)
    return pl.pallas_call(
        partial(widen_kernel, slabs),
        out_shape=[jax.ShapeDtypeStruct(shape, F32) for shape in shapes]
        + [jax.ShapeDtypeStruct((1, n), F32) for n in lengths]
        + [jax.ShapeDtypeStruct(low_results.shape, BF16)],
        in_specs=[vmem, vmem, any_space],
        out_specs=[any_space] * 4 + [vmem] * 8 + [any_space],
        scratch_shapes=[
            pltpu.VMEM((blocks, width, width), F32), pltpu.VMEM(low_results.shape, BF16),
            dma(blocks), dma(2),
        ],
        compiler_params=pltpu.CompilerParams(vmem_limit_bytes=WIDEN_VMEM),
        name="widen",
    )(pltpu.with_memory_space_constraint(total, pltpu.VMEM), vec, low_results)


def shards(
    boundary, inward, inbias, outward, outbias, normgain, normshift, expand, expbias,
    shrink, shrbias, lastgain, lastshift,
):
    width = outward.shape[-1]
    hidden = expand.shape[-1]
    slabs = hidden // width
    outs = run_layer(
        boundary[0],
        (inward[0], outward[0], expand[0], shrink[0]),
        (inbias, outbias, normgain, normshift, expbias, shrbias, lastgain, lastshift),
    )
    results, factors, vectors = outs[0], outs[1:9], outs[9]
    if lax.axis_size("dp") == 4 * LANES_Z:
        total, vec = reduce_gradients(factors, vectors)
        widened = widen(total, vec, results, hidden)
        matrices, pieces, results = widened[:4], widened[4:12], widened[12]
    else:
        f_x, f_a, f_h, f_g, f_p, f_o, f_u, f_f = factors

        def summed(left, right):
            grad = dot_tn(left, right).astype(BF16)
            mine = lax.psum_scatter(grad, "dp", scatter_dimension=0, tiled=True)
            return lax.all_gather(mine, "dp", axis=0, tiled=True).astype(F32)

        matrices = [summed(f_x, f_p), summed(f_a, f_o), summed(f_h, f_u), summed(f_g, f_f)]
        vec = lax.psum(vectors, "dp")
        pieces, row = [], 0
        for count in (3, 1, 1, 1, slabs, 1, 1, 1):
            pieces.append(vec[row : row + count].reshape(1, count * width))
            row += count

    inward_grad, outward_grad, expand_grad, shrink_grad = (m[None] for m in matrices)
    return (
        results[None],
        inward_grad, pieces[0], outward_grad, pieces[1], pieces[2], pieces[3],
        expand_grad, pieces[4], shrink_grad, pieces[5], pieces[6], pieces[7],
    )


def solution(mesh):
    matrix, vector = P("section", None, None), P("section", None)
    params = (
        matrix, vector, matrix, vector, vector, vector, matrix, vector, matrix, vector,
        vector, vector,
    )
    specs = (P("section", "dp", None),) + params
    return jax.shard_map(shards, mesh=mesh, in_specs=specs, out_specs=specs, check_vma=False)
```

```python
from functools import partial
import math

import jax
import jax.numpy as jnp
import numpy as np
from jax import lax
from jax.experimental import pallas as pl
from jax.experimental.pallas import tpu as pltpu
from jax.sharding import PartitionSpec as P

HEAD = 64
SEQ = 512
CHUNK = 256
PAIR = 2 * HEAD
EPSILON = 1e-05
MESH = pl.DeviceIdType.MESH
F32 = jnp.float32
BF16 = jnp.bfloat16
VMEM_BYTES = 63 * 2**20
LAYER_VMEM = 63 * 2**20
GRADIENT_VMEM = 46 * 2**20
WIDEN_VMEM = 34 * 2**20


def dot(a, b):
    return jnp.dot(a, b, preferred_element_type=F32)


def dot_nt(a, b):
    return lax.dot_general(a, b, (((1,), (1,)), ((), ())), preferred_element_type=F32)


def dot_tn(a, b):
    return lax.dot_general(a, b, (((0,), (0,)), ((), ())), preferred_element_type=F32)


def softplus(p):
    return jnp.maximum(p, 0.0) + jnp.log1p(jnp.exp(-jnp.abs(p)))


def sigmoid_of_softplus(q):
    series = q * (1.0 - q * (0.5 - q * (1.0 / 6.0 - q * (1.0 / 24.0))))
    return jnp.where(q < 0.03, series, 1.0 - jnp.exp(-q))


def cosine_tables():
    step = math.pi / (2.0 * SEQ)
    i = np.arange(CHUNK)[:, None]
    j = np.arange(CHUNK)[None, :]
    near = np.where(i >= j, np.cos((i - j) * step), 0.0).astype(np.float32)
    far = np.cos((i - j + CHUNK) * step).astype(np.float32)
    return near, far


def lane_masks():
    lanes = np.arange(PAIR)
    return np.stack([lanes < HEAD, lanes >= HEAD])[:, None, :].astype(np.float32)


def layer_kernel(
    boundary, inward, outward, expand, shrink,
    inbias, outbias, normgain, normshift, expbias, shrbias, lastgain, lastshift,
    near, far, masks,
    results, f_x, f_a, f_h, f_g, f_p, f_o, f_u, f_f, vector_rows,
    win, wout, wexp, wshr,
    xs, qkv, att, low, zin, hbs, gs, gps, n1s, n2s, scales, dys, ybuf,
    acc, keep, das, carry, vectors,
    load_sems, out_sems, res_sems, fwd_send, fwd_recv, bwd_send, bwd_recv,
):
    rows_all, width = xs.shape
    hidden = wexp.shape[1]
    chunks = rows_all // CHUNK
    pairs = width // PAIR
    slabs = hidden // width
    section = lax.axis_index("section")
    first = section == 0
    peer = {"section": 1 - section}

    loads = [
        pltpu.make_async_copy(src, dst, load_sems.at[i])
        for i, (src, dst) in enumerate(
            [(inward, win), (outward, wout), (expand, wexp), (shrink, wshr)]
        )
    ]
    head, rest = pl.ds(0, CHUNK), pl.ds(CHUNK, rows_all - CHUNK)
    load_x = pltpu.make_async_copy(boundary.at[head], xs.at[head], load_sems.at[4])
    load_rest = pltpu.make_async_copy(boundary.at[rest], xs.at[rest], load_sems.at[5])
    load_y = pltpu.make_async_copy(boundary, dys, load_sems.at[4])

    @pl.when(first)
    def _():
        load_x.start()

    loads[0].start()

    @pl.when(jnp.logical_not(first))
    def _():
        load_y.start()

    barrier = pltpu.get_barrier_semaphore()
    pl.semaphore_signal(barrier, inc=1, device_id=peer, device_id_type=MESH)
    vectors[...] = jnp.zeros_like(vectors)
    pl.semaphore_wait(barrier, 1)

    def rows_of(c):
        return pl.ds(pl.multiple_of(c * CHUNK, CHUNK), CHUNK)

    def send_forward(c):
        return pltpu.make_async_remote_copy(
            src_ref=ybuf.at[rows_of(c)], dst_ref=xs.at[rows_of(c)],
            send_sem=fwd_send.at[c], recv_sem=fwd_recv.at[c],
            device_id=peer, device_id_type=MESH,
        )

    def send_backward(c):
        return pltpu.make_async_remote_copy(
            src_ref=ybuf.at[rows_of(c)], dst_ref=dys.at[rows_of(c)],
            send_sem=bwd_send.at[c], recv_sem=bwd_recv.at[c],
            device_id=peer, device_id_type=MESH,
        )

    def result_copy(c):
        return pltpu.make_async_copy(ybuf.at[rows_of(c)], results.at[rows_of(c)], res_sems.at[c])

    early = [(xs, f_x), (att, f_a), (hbs, f_h)]
    late = [(qkv, f_p), (n1s, f_o), (gps, f_u), (n2s, f_f)]

    def factor_copies(c, which, base):
        return [
            pltpu.make_async_copy(src.at[rows_of(c)], dst.at[rows_of(c)], out_sems.at[c, base + i])
            for i, (src, dst) in enumerate(which)
        ]

    def active_copy(c):
        return pltpu.make_async_copy(gs.at[c % 2], f_g.at[rows_of(c)], out_sems.at[c, 3])

    def column_sum(at, value):
        vectors[at] += jnp.sum(value, axis=0, keepdims=True)

    def norm_forward(e):
        mean = jnp.mean(e, axis=-1, keepdims=True)
        center = e - mean
        s = lax.rsqrt(jnp.mean(center * center, axis=-1, keepdims=True) + EPSILON)
        return center * s, s

    def norm_backward(dn, n, s):
        m1 = jnp.mean(dn, axis=-1, keepdims=True)
        m2 = jnp.mean(dn * n, axis=-1, keepdims=True)
        return s * (dn - m1 - n * m2)

    def pair_columns(hp):
        return [pl.ds(pl.multiple_of(i * width + hp * PAIR, PAIR), PAIR) for i in range(3)]

    def attend(c, wide):
        rows = rows_of(c)
        tiles = [(rows, near)] + ([(rows_of(c - 1), far)] if wide else [])
        m = [masks[a].astype(BF16) for a in range(2)]

        def one_pair(hp, _):
            cq, ck, cv = pair_columns(hp)
            q = qkv[rows, cq]
            nz = None
            for key_rows, weights in tiles:
                k, v = qkv[key_rows, ck], qkv[key_rows, cv]
                for a in range(2):
                    s = (dot_nt(q * m[a], k) * weights[...]).astype(BF16)
                    right = jnp.concatenate(
                        [v * m[a], jnp.broadcast_to(m[a], v.shape)], axis=1
                    )
                    part = dot(s, right)
                    nz = part if nz is None else nz + part
            inverse = 1.0 / nz[:, PAIR:]
            a_full = nz[:, :PAIR] * inverse
            a_high = a_full.astype(BF16)
            att[rows, cq] = a_high
            low[rows, cq] = (a_full - a_high.astype(F32)).astype(BF16)
            zin[rows, cq] = inverse.astype(BF16)
            return 0

        lax.fori_loop(0, pairs, one_pair, 0, unroll=True)

    def attend_backward(c, wide):
        rows = rows_of(c)
        m = [masks[a].astype(BF16) for a in range(2)]
        left = lax.broadcasted_iota(jnp.int32, (CHUNK, PAIR), 1) < HEAD

        def one_pair(hp, _):
            cq, ck, cv = pair_columns(hp)
            q, k, v = qkv[rows, cq], qkv[rows, ck], qkv[rows, cv]
            dn = (das[:, cq].astype(F32) * zin[rows, cq].astype(F32)).astype(BF16)
            prod = dn.astype(F32) * (att[rows, cq].astype(F32) + low[rows, cq].astype(F32))
            dz = jnp.concatenate(
                [-jnp.sum(prod * masks[a], axis=-1, keepdims=True) for a in range(2)], axis=0
            )
            both_q = jnp.concatenate([q * m[a] for a in range(2)], axis=0)
            both_dn = jnp.concatenate([dn * m[a] for a in range(2)], axis=0)

            def tile(kt, vt, weights):
                w = jnp.concatenate([weights[...]] * 2, axis=0)
                s = (dot_nt(both_q, kt) * w).astype(BF16)
                ds = ((dot_nt(both_dn, vt) + dz) * w).astype(BF16)
                dq2 = dot(ds, kt)
                dq = jnp.where(left, dq2[:CHUNK], dq2[CHUNK:])
                return dq, dot_tn(ds, both_q), dot_tn(s, both_dn)

            dq, dk, dv = tile(k, v, near)
            wide_cols = [pl.ds(pl.multiple_of(i * width + hp * PAIR, PAIR), PAIR) for i in range(2)]
            if wide:
                kp, vp = qkv[rows_of(c - 1), ck], qkv[rows_of(c - 1), cv]
                dqp, dkp, dvp = tile(kp, vp, far)
                dq = dq + dqp
                carry[:, wide_cols[0]] = dkp
                carry[:, wide_cols[1]] = dvp
            else:
                dk = dk + carry[:, wide_cols[0]]
                dv = dv + carry[:, wide_cols[1]]
            qkv[rows, cq] = (dq * sigmoid_of_softplus(q.astype(F32))).astype(BF16)
            qkv[rows, ck] = (dk * sigmoid_of_softplus(k.astype(F32))).astype(BF16)
            qkv[rows, cv] = dv.astype(BF16)
            return 0

        lax.fori_loop(0, pairs, one_pair, 0, unroll=True)

    def forward(c, begins):
        rows = rows_of(c)

        @pl.when(begins)
        def _():
            loads[0].wait()

            @pl.when(first)
            def _():
                load_x.wait()

            for load in loads[1:]:
                load.start()

            @pl.when(first)
            def _():
                load_rest.start()

        @pl.when(jnp.logical_not(first))
        def _():
            send_forward(c).wait_recv()

        for i in range(3):
            cols = slice(i * width, (i + 1) * width)
            p = dot(xs[rows, :], win[:, cols]) + inbias[:, cols]
            qkv[rows, cols] = (softplus(p) if i < 2 else p).astype(BF16)

        @pl.when(c % 2 == 0)
        def _():
            attend(c, False)

        @pl.when(c % 2 == 1)
        def _():
            attend(c, True)

        @pl.when(begins)
        def _():
            for load in loads[1:]:
                load.wait()

            @pl.when(first)
            def _():
                load_rest.wait()

        e = xs[rows, :].astype(F32) + (dot(att[rows, :], wout[...]) + outbias[...])
        n1, s1 = norm_forward(e)
        n1s[rows, :] = n1.astype(BF16)
        scales[rows, 0:1] = s1
        h = n1 * normgain[...] + normshift[...]
        hbs[rows, :] = h.astype(BF16)

        @pl.when(c >= 2)
        def _():
            active_copy(c - 2).wait()

        acc[...] = h + shrbias[...]
        for i in range(slabs):
            cols = slice(i * width, (i + 1) * width)
            u = dot(hbs[rows, :], wexp[:, cols]) + expbias[:, cols]
            phi = 0.5 * (1.0 + lax.erf(u * math.sqrt(0.5)))
            g = (u * phi).astype(BF16)
            gs[c % 2, :, cols] = g
            gps[rows, cols] = (
                phi + u * (jnp.exp(u * u * -0.5) * (1.0 / math.sqrt(2.0 * math.pi)))
            ).astype(BF16)
            acc[...] += dot(g, wshr[cols, :])
        n2, s2 = norm_forward(acc[...])
        n2s[rows, :] = n2.astype(BF16)
        scales[rows, 1:2] = s2
        ybuf[rows, :] = (n2 * lastgain[...] + lastshift[...]).astype(BF16)

        @pl.when(first)
        def _():
            send_forward(c).start()

        @pl.when(jnp.logical_not(first))
        def _():
            result_copy(c).start()

        for copy in factor_copies(c, early, 0) + [active_copy(c)]:
            copy.start()

    def backward(c):
        rows = rows_of(c)

        @pl.when(first)
        def _():
            send_backward(c).wait_recv()

        @pl.when(jnp.logical_and(jnp.logical_not(first), c == 1))
        def _():
            load_y.wait()

        dy = dys[rows, :].astype(F32)
        n2 = n2s[rows, :].astype(F32)
        column_sum(7 + slabs, dy * n2)
        column_sum(8 + slabs, dy)
        dr = norm_backward(dy * lastgain[...], n2, scales[rows, 1:2])
        df = dr.astype(BF16)
        n2s[rows, :] = df
        column_sum(6 + slabs, df.astype(F32))
        acc[...] = dr
        for i in range(slabs):
            cols = slice(i * width, (i + 1) * width)
            dg = dot_nt(n2s[rows, :], wshr[cols, :])
            du = (dg * gps[rows, cols].astype(F32)).astype(BF16)
            gps[rows, cols] = du
            column_sum(6 + i, du.astype(F32))
            acc[...] += dot_nt(du, wexp[:, cols])
        dh = acc[...]
        n1 = n1s[rows, :].astype(F32)
        column_sum(4, dh * n1)
        column_sum(5, dh)
        de = norm_backward(dh * normgain[...], n1, scales[rows, 0:1])
        keep[...] = de
        do = de.astype(BF16)
        n1s[rows, :] = do
        column_sum(3, do.astype(F32))
        das[...] = dot_nt(do, wout[...]).astype(BF16)

        @pl.when(c % 2 == 0)
        def _():
            attend_backward(c, False)

        @pl.when(c % 2 == 1)
        def _():
            attend_backward(c, True)

        for i in range(3):
            column_sum(i, qkv[rows, i * width : (i + 1) * width].astype(F32))
        dx = keep[...] + dot_nt(qkv[rows, :], win[...])

        @pl.when(first)
        def _():
            send_forward(c).wait_send()

        @pl.when(jnp.logical_not(first))
        def _():
            result_copy(c).wait()

        ybuf[rows, :] = dx.astype(BF16)

        @pl.when(first)
        def _():
            result_copy(c).start()

        @pl.when(jnp.logical_not(first))
        def _():
            send_backward(c).start()

        for copy in factor_copies(c, late, 4):
            copy.start()

    def step(t, _):
        group, place = t // 4, t % 4
        ahead = jnp.where(first, t < chunks, place < 2)
        c_forward = jnp.where(first, t, 2 * group + place)
        back = t - chunks
        c_backward = jnp.where(first, 2 * (back // 2) + 1 - back % 2, 2 * group + 3 - place)

        @pl.when(ahead)
        def _():
            forward(c_forward, t == 0)

        @pl.when(jnp.logical_not(ahead))
        def _():
            backward(c_backward)

        return 0

    lax.fori_loop(0, 2 * chunks, step, 0)
    for i in range(vectors.shape[0]):
        vector_rows[i : i + 1, :] = vectors[i]

    def finish(c, _):
        @pl.when(first)
        def _():
            result_copy(c).wait()

        @pl.when(jnp.logical_not(first))
        def _():
            send_backward(c).wait_send()

        for copy in factor_copies(c, early, 0) + factor_copies(c, late, 4):
            copy.wait()

        @pl.when(c >= chunks - 2)
        def _():
            active_copy(c).wait()

        return 0

    lax.fori_loop(0, chunks, finish, 0)


def run_layer(boundary, weights, biases):
    rows, width = boundary.shape
    hidden = weights[2].shape[1]
    chunks = rows // CHUNK
    near, far = cosine_tables()
    masks = lane_masks()
    slabs = hidden // width
    any_space = pl.BlockSpec(memory_space=pl.ANY)
    vmem = pl.BlockSpec(memory_space=pltpu.VMEM)
    out_widths = [width] * 4 + [hidden, 3 * width, width, hidden, width]
    out_shape = [jax.ShapeDtypeStruct((rows, w), BF16) for w in out_widths]
    vector_count = -(-(9 + slabs) // 8) * 8
    out_shape.append(jax.ShapeDtypeStruct((vector_count, width), F32))
    low = lambda *shape: pltpu.VMEM(shape, BF16)
    wide = lambda *shape: pltpu.VMEM(shape, F32)
    dma = pltpu.SemaphoreType.DMA
    return pl.pallas_call(
        layer_kernel,
        out_shape=out_shape,
        in_specs=[any_space] * 5 + [vmem] * 11,
        out_specs=[any_space] * 9 + [vmem],
        scratch_shapes=[
            low(width, 3 * width), low(width, width), low(width, hidden), low(hidden, width),
            low(rows, width), low(rows, 3 * width), low(rows, width), low(rows, width),
            low(rows, width), low(rows, width), low(2, CHUNK, hidden), low(rows, hidden),
            low(rows, width), low(rows, width), wide(rows, 2),
            low(rows, width), low(rows, width),
            wide(CHUNK, width), wide(CHUNK, width), low(CHUNK, width), wide(CHUNK, 2 * width),
            wide(vector_count, 1, width),
            dma((6,)), dma((chunks, 8)), dma((chunks,)), dma((chunks,)), dma((chunks,)),
            dma((chunks,)), dma((chunks,)),
        ],
        compiler_params=pltpu.CompilerParams(
            collective_id=0, has_side_effects=True, vmem_limit_bytes=LAYER_VMEM
        ),
        name="layer",
    )(boundary, *weights, *biases, jnp.asarray(near), jnp.asarray(far), jnp.asarray(masks))


SETS = 2
LANES_Z = 4
STAGES = 3

ARRIVE_Y = 2
PAIR_AT = (0, 2, 3, 13)
ONE_AT = (0, 3, 4, 17)
LAST_ONE, LAST_PAIR, LAST_CROSS = 21, 20, 21
BACK_AT = (0, 20, 21, 24)
OUT_AT = (22, 22, 22, 25)


def gradient_kernel(
    f_x, f_a, f_h, f_g, f_p, f_o, f_u, f_f, vec_in,
    total, vec_out,
    x, a, h, g, p, o, u, f,
    own, stage, core_in, chain_pair, chain_one, y_in, end_in, vec, vec_got,
    load_sems, core_s, core_r, y_s, y_r, pair_s, pair_r, one_s, one_r, end_s, end_r,
    got, z_s, yy_s, kept, out_s, out_r, vec_s, vec_r, credit,
):
    width = x.shape[1]
    slabs = g.shape[1] // width
    me = lax.axis_index("dp")
    core, y, z = me % 2, (me // 2) % 2, me // 4
    last = LANES_Z - 1
    core_peer, y_peer = {"dp": me + 1 - 2 * core}, {"dp": me + 2 - 4 * y}
    hop = [last - z, z]
    ahead = [{"dp": me - 4}, {"dp": me + 4}]
    behind = [ahead[1], ahead[0]]

    blocks = (
        [(a, 0, o, 0)]
        + [(x, 0, p, i) for i in range(3)]
        + [(h, 0, u, i) for i in range(slabs)]
        + [(g, i, f, 0) for i in range(slabs)]
    )
    duos = len(blocks) // 2
    sets = duos * SETS
    set_rows = width // SETS
    half = set_rows // 2
    piece = half // 4

    slabs_p = [pl.ds(i * width, width) for i in range(3)]
    sources = [(f_a, a), (f_o, o), (f_x, x)]
    sources += [(f_p.at[:, cols], p.at[:, cols]) for cols in slabs_p]
    sources += [(f_h, h), (f_u, u), (f_f, f), (f_g, g)]
    loads = [
        pltpu.make_async_copy(src, dst, load_sems.at[i]) for i, (src, dst) in enumerate(sources)
    ]
    load_at = {0: (0, 1, 2, 3), SETS: (4, 5), 2 * SETS: (6, 7), (2 + slabs // 2) * SETS: (8, 9)}
    for load in loads[:4]:
        load.start()

    barrier = pltpu.get_barrier_semaphore()
    for peer in (core_peer, y_peer):
        pl.semaphore_signal(barrier, inc=1, device_id=peer, device_id_type=MESH)
    for d in range(2):
        @pl.when(hop[d] < last)
        def _():
            pl.semaphore_signal(barrier, inc=1, device_id=ahead[d], device_id_type=MESH)
    pl.semaphore_wait(barrier, jnp.where(jnp.logical_and(z > 0, z < last), 4, 3))

    def remote(src, dst, send, recv, peer):
        return pltpu.make_async_remote_copy(
            src_ref=src, dst_ref=dst, send_sem=send, recv_sem=recv,
            device_id=peer, device_id_type=MESH,
        )

    def span(k, d, first, count):
        start = (k % SETS) * set_rows + d * half + first * piece
        return pl.ds(pl.multiple_of(start, 16), count * piece)

    def mine(k, d, first, count=1):
        return own.at[k // SETS, span(k, d, first, count)]


    def final(k, d, first, count=1):
        return total.at[2 * (k // SETS) + core, span(k, d, first, count)]

    def add(dst, src):
        dst[...] = (dst[...].astype(F32) + src[...].astype(F32)).astype(BF16)

    def core_copy(k):
        return remote(
            stage.at[k % STAGES, 1 - core], core_in.at[k % STAGES], core_s.at[k], core_r.at[k],
            core_peer,
        )

    def y_copy(k, d):
        return remote(mine(k, d, 1 - y), y_in.at[k, d], y_s.at[k, d], y_r.at[k, d], y_peer)

    def pair_copy(k, d):
        return remote(
            mine(k, d, 2, 2), chain_pair.at[k, d], pair_s.at[k, d], pair_r.at[k, d], ahead[d]
        )

    def one_copy(k, d):
        return remote(mine(k, d, y), chain_one.at[k, d], one_s.at[k, d], one_r.at[k, d], ahead[d])

    def end_copy(k, d):
        return remote(mine(k, d, 3 - y), end_in.at[k], end_s.at[k], end_r.at[k], y_peer)

    def spread_z(k, d, b, i, src):
        return remote(src, final(k, d, b), z_s.at[k, d, i], got.at[k, d, b], behind[d])

    def spread_y(k, d, b, i, src):
        return remote(src, final(k, d, b), yy_s.at[k, d, i], got.at[k, d, b], y_peer)

    def keep_copy(k, d, b, i):
        return pltpu.make_async_copy(mine(k, d, b), final(k, d, b), kept.at[k, d, i])

    def out_copy(k, d):
        return remote(
            final(k, d, 0, 4), final(k, d, 0, 4), out_s.at[k, d], out_r.at[k, d], core_peer
        )

    def arrived(k, d, b):
        spread_z(k, d, b, 0, final(k, d, b)).wait_recv()

    outer = jnp.logical_or(z == 0, z == last)
    z_pair = {"dp": me + 4 - 8 * (z % 2)}
    z_mid = {"dp": jnp.where(z == 1, me + 4, me - 4)}
    z_out = {"dp": jnp.where(z == 1, me - 4, me + 4)}

    def vec_copy(i, peer):
        return remote(vec.at[i], vec_got.at[min(i, 3)], vec_s.at[i], vec_r.at[min(i, 3)], peer)

    def compute(k):
        for i in load_at.get(k, ()):
            loads[i].wait()
        if k >= STAGES:
            core_copy(k - STAGES).wait_send()
            pl.semaphore_wait(credit, 1)
        m, at = k // SETS, (k % SETS) * set_rows
        for side in range(2):
            left, i, right, j = blocks[2 * m + side]
            cols = slice(i * width + at, i * width + at + set_rows)
            stage[k % STAGES, side] = dot_tn(
                left[:, cols], right[:, j * width : (j + 1) * width]
            ).astype(BF16)
        core_copy(k).start()

    vec[0] = vec_in[...]
    vec_copy(0, core_peer).start()
    compute(0)
    for load in loads[4:]:
        load.start()

    def feed(t):
        for k in range(1, sets):
            @pl.when(t == k - 1)
            def _():
                compute(k)

        for i, peer in ((1, y_peer), (2, z_pair)):
            @pl.when(t == i)
            def _():
                vec_copy(i - 1, peer).wait_recv()
                vec[i] = vec[i - 1] + vec_got[i - 1]
                vec_copy(i, peer).start()

        @pl.when(t == 3)
        def _():
            vec_copy(2, z_pair).wait_recv()
            vec[3] = vec[2] + vec_got[2]

            @pl.when(jnp.logical_not(outer))
            def _():
                vec_copy(3, z_mid).start()

        @pl.when(jnp.logical_and(t == 4, jnp.logical_not(outer)))
        def _():
            vec_copy(3, z_mid).wait_recv()
            vec[4] = vec[3] + vec_got[3]
            vec_copy(4, z_out).start()
            vec_out[...] = vec[4]

        @pl.when(jnp.logical_and(t == 5, outer))
        def _():
            vec_copy(3, z_mid).wait_recv()
            vec_out[...] = vec_got[3]

        @pl.when(t < sets)
        def _():
            core_copy(t).wait_recv()
            for d in range(2):
                here = stage[t % STAGES, core, d * half : (d + 1) * half].astype(F32)
                there = core_in[t % STAGES, d * half : (d + 1) * half].astype(F32)
                mine(t, d, 0, 4)[...] = (here + there).astype(BF16)
                y_copy(t, d).start()

                @pl.when(hop[d] == 0)
                def _():
                    pair_copy(t, d).start()

            @pl.when(t < sets - STAGES)
            def _():
                pl.semaphore_signal(credit, inc=1, device_id=core_peer, device_id_type=MESH)

    def during(k, more=True):
        return jnp.logical_and(jnp.logical_and(k >= 0, k < sets), more)

    def by_place(place, offsets):
        out = jnp.int32(offsets[0])
        for i, offset in enumerate(offsets[1:], 1):
            out = jnp.where(place == i, offset, out)
        return out

    def arrive_y(t):
        k = t - ARRIVE_Y

        @pl.when(during(k))
        def _():
            for d in range(2):
                y_copy(k, d).wait_recv()
                add(mine(k, d, y), y_in.at[k, d])

                @pl.when(hop[d] == 0)
                def _():
                    one_copy(k, d).start()

    def hop_pair(t):
        for d in range(2):
            k = t - by_place(hop[d], PAIR_AT)

            @pl.when(during(k, hop[d] > 0))
            def _():
                pair_copy(k, d).wait_recv()
                add(mine(k, d, 2, 2), chain_pair.at[k, d])

                @pl.when(hop[d] < last)
                def _():
                    pair_copy(k, d).start()

                @pl.when(hop[d] == last)
                def _():
                    end_copy(k, d).start()

    def hop_one(t):
        for d in range(2):
            k = t - by_place(hop[d], ONE_AT)

            @pl.when(during(k, hop[d] > 0))
            def _():
                one_copy(k, d).wait_recv()
                add(mine(k, d, y), chain_one.at[k, d])

                @pl.when(hop[d] < last)
                def _():
                    one_copy(k, d).start()

    def last_one(t):
        k = t - LAST_ONE
        for d in range(2):
            @pl.when(during(k, hop[d] == last))
            def _():
                spread_z(k, d, y, 0, mine(k, d, y)).start()
                spread_y(k, d, y, 0, mine(k, d, y)).start()
                keep_copy(k, d, y, 0).start()

    def last_pair(t):
        k = t - LAST_PAIR
        for d in range(2):
            @pl.when(during(k, hop[d] == last))
            def _():
                end_copy(k, d).wait_recv()
                add(mine(k, d, 2 + y), end_in.at[k])
                spread_y(k, d, 2 + y, 1, mine(k, d, 2 + y)).start()
                spread_z(k, d, 2 + y, 1 + y, mine(k, d, 2 + y)).start()
                keep_copy(k, d, 2 + y, 1).start()

    def last_cross(t):
        k = t - LAST_CROSS
        for d in range(2):
            @pl.when(during(k, hop[d] == last))
            def _():
                arrived(k, d, 3 - y)
                spread_z(k, d, 3 - y, 2 - y, final(k, d, 3 - y)).start()

    def way_back(t):
        for d in range(2):
            k = t - by_place(last - hop[d], BACK_AT)

            @pl.when(during(k, hop[d] < last))
            def _():
                for i, b in ((0, y), (1, 2), (2, 3)):
                    arrived(k, d, b)

                    @pl.when(hop[d] > 0)
                    def _():
                        spread_z(k, d, b, i, final(k, d, b)).start()

                    if i == 0:
                        spread_y(k, d, b, 0, final(k, d, b)).start()

    def to_core(t):
        for d in range(2):
            k = t - by_place(last - hop[d], OUT_AT)

            @pl.when(during(k))
            def _():
                arrived(k, d, 1 - y)

                @pl.when(hop[d] == last)
                def _():
                    keep_copy(k, d, y, 0).wait()
                    keep_copy(k, d, 2 + y, 1).wait()

                out_copy(k, d).start()

    def tick(t, _):
        for stage in (
            last_one, hop_one, arrive_y, hop_pair, to_core, last_cross, feed, last_pair, way_back
        ):
            stage(t)
        return 0

    lax.fori_loop(0, sets + max(OUT_AT), tick, 0)

    def settle(k, _):
        for d in range(2):
            y_copy(k, d).wait_send()
            out_copy(k, d).wait()
            spread_y(k, d, y, 0, final(k, d, y)).wait_send()

            @pl.when(hop[d] < last)
            def _():
                pair_copy(k, d).wait_send()
                one_copy(k, d).wait_send()

            @pl.when(hop[d] == last)
            def _():
                end_copy(k, d).wait_send()
                spread_y(k, d, 2 + y, 1, final(k, d, 2 + y)).wait_send()

            @pl.when(hop[d] > 0)
            def _():
                for i, b in ((0, y), (1, 2), (2, 3)):
                    spread_z(k, d, b, i, final(k, d, b)).wait_send()

        return 0

    lax.fori_loop(0, sets, settle, 0)
    for k in range(sets - STAGES, sets):
        core_copy(k).wait_send()

    for i in range(3):
        vec_copy(i, core_peer).wait_send()

    @pl.when(jnp.logical_not(outer))
    def _():
        vec_copy(3, z_mid).wait_send()
        vec_copy(4, z_out).wait_send()


def reduce_gradients(factors, vectors):
    rows, width = factors[0].shape
    hidden = factors[3].shape[1]
    blocks = 4 + 2 * (hidden // width)
    duos = blocks // 2
    sets = duos * SETS
    piece = width // SETS // 8
    vmem = pl.BlockSpec(memory_space=pltpu.VMEM)
    low = lambda *shape: pltpu.VMEM(shape, BF16)
    dma = lambda *shape: pltpu.SemaphoreType.DMA(shape)
    any_space = pl.BlockSpec(memory_space=pl.ANY)
    return pl.pallas_call(
        gradient_kernel,
        out_shape=[low(blocks, width, width), jax.ShapeDtypeStruct(vectors.shape, F32)],
        in_specs=[any_space] * 8 + [vmem],
        out_specs=[vmem, vmem],
        scratch_shapes=[low(*factor.shape) for factor in factors]
        + [
            low(duos, width, width), low(STAGES, 2, width // SETS, width),
            low(STAGES, width // SETS, width),
            low(sets, 2, 2 * piece, width), low(sets, 2, piece, width),
            low(sets, 2, piece, width), low(sets, piece, width),
            pltpu.VMEM((5,) + vectors.shape, F32), pltpu.VMEM((4,) + vectors.shape, F32),
            dma(10), dma(sets), dma(sets), dma(sets, 2), dma(sets, 2), dma(sets, 2), dma(sets, 2),
            dma(sets, 2), dma(sets, 2), dma(sets), dma(sets),
            dma(sets, 2, 4), dma(sets, 2, 3), dma(sets, 2, 2), dma(sets, 2, 2), dma(sets, 2),
            dma(sets, 2), dma(5), dma(4), pltpu.SemaphoreType.REGULAR,
        ],
        compiler_params=pltpu.CompilerParams(
            collective_id=1, has_side_effects=True, vmem_limit_bytes=GRADIENT_VMEM
        ),
        name="gradients",
    )(*factors, vectors)


def widen_kernel(slabs, total, vec, low_results, *refs):
    outs, results = refs[:12], refs[12]
    high, held, out_sems, side_sems = refs[13:]
    blocks, width, _ = total.shape
    inward, outward, expand, shrink = outs[:4]

    def place(i):
        if i < 1:
            return outward
        if i < 4:
            return inward.at[:, pl.ds((i - 1) * width, width)]
        if i < 4 + slabs:
            return expand.at[:, pl.ds((i - 4) * width, width)]
        return shrink.at[pl.ds((i - 4 - slabs) * width, width)]

    def writes(i):
        return pltpu.make_async_copy(high.at[i], place(i), out_sems.at[i])

    side_in = pltpu.make_async_copy(low_results, held, side_sems.at[0])
    side_out = pltpu.make_async_copy(held, results, side_sems.at[1])
    side_in.start()
    row = 0
    for out in outs[4:]:
        for i in range(out.shape[1] // width):
            out[:, i * width : (i + 1) * width] = vec[row : row + 1, :]
            row += 1
    for i in range(blocks):
        def part(r, _):
            rows = pl.ds(pl.multiple_of(r * 64, 64), 64)
            high[i, rows] = total[i, rows].astype(F32)
            return 0

        lax.fori_loop(0, width // 64, part, 0)
        writes(i).start()
    side_in.wait()
    side_out.start()
    for i in range(blocks):
        writes(i).wait()
    side_out.wait()


def widen(total, vec, low_results, hidden):
    blocks, width, _ = total.shape
    slabs = hidden // width
    shapes = [(width, 3 * width), (width, width), (width, hidden), (hidden, width)]
    lengths = [3 * width, width, width, width, hidden, width, width, width]
    any_space = pl.BlockSpec(memory_space=pl.ANY)
    vmem = pl.BlockSpec(memory_space=pltpu.VMEM)
    dma = lambda *shape: pltpu.SemaphoreType.DMA(shape)
    return pl.pallas_call(
        partial(widen_kernel, slabs),
        out_shape=[jax.ShapeDtypeStruct(shape, F32) for shape in shapes]
        + [jax.ShapeDtypeStruct((1, n), F32) for n in lengths]
        + [jax.ShapeDtypeStruct(low_results.shape, BF16)],
        in_specs=[vmem, vmem, any_space],
        out_specs=[any_space] * 4 + [vmem] * 8 + [any_space],
        scratch_shapes=[
            pltpu.VMEM((blocks, width, width), F32), pltpu.VMEM(low_results.shape, BF16),
            dma(blocks), dma(2),
        ],
        compiler_params=pltpu.CompilerParams(vmem_limit_bytes=WIDEN_VMEM),
        name="widen",
    )(pltpu.with_memory_space_constraint(total, pltpu.VMEM), vec, low_results)


def shards(
    boundary, inward, inbias, outward, outbias, normgain, normshift, expand, expbias,
    shrink, shrbias, lastgain, lastshift,
):
    width = outward.shape[-1]
    hidden = expand.shape[-1]
    slabs = hidden // width
    outs = run_layer(
        boundary[0],
        (inward[0], outward[0], expand[0], shrink[0]),
        (inbias, outbias, normgain, normshift, expbias, shrbias, lastgain, lastshift),
    )
    results, factors, vectors = outs[0], outs[1:9], outs[9]
    if lax.axis_size("dp") == 4 * LANES_Z:
        total, vec = reduce_gradients(factors, vectors)
        widened = widen(total, vec, results, hidden)
        matrices, pieces, results = widened[:4], widened[4:12], widened[12]
    else:
        f_x, f_a, f_h, f_g, f_p, f_o, f_u, f_f = factors

        def summed(left, right):
            grad = dot_tn(left, right).astype(BF16)
            mine = lax.psum_scatter(grad, "dp", scatter_dimension=0, tiled=True)
            return lax.all_gather(mine, "dp", axis=0, tiled=True).astype(F32)

        matrices = [summed(f_x, f_p), summed(f_a, f_o), summed(f_h, f_u), summed(f_g, f_f)]
        vec = lax.psum(vectors, "dp")
        pieces, row = [], 0
        for count in (3, 1, 1, 1, slabs, 1, 1, 1):
            pieces.append(vec[row : row + count].reshape(1, count * width))
            row += count

    inward_grad, outward_grad, expand_grad, shrink_grad = (m[None] for m in matrices)
    return (
        results[None],
        inward_grad, pieces[0], outward_grad, pieces[1], pieces[2], pieces[3],
        expand_grad, pieces[4], shrink_grad, pieces[5], pieces[6], pieces[7],
    )


def solution(mesh):
    matrix, vector = P("section", None, None), P("section", None)
    params = (
        matrix, vector, matrix, vector, vector, vector, matrix, vector, matrix, vector,
        vector, vector,
    )
    specs = (P("section", "dp", None),) + params
    return jax.shard_map(shards, mesh=mesh, in_specs=specs, out_specs=specs, check_vma=False)
```
